128 devices in a mesh: seq: 16 (over z, x), exp: 8 (over y, core).
Axes of the slice: x: 4, y: 4, z: 4, core: 2. Of those that a mesh axis runs over, the one named last changes fastest.
Arguments:
- hidden_in: bfloat16 [16384, 2560], P(('seq', 'exp')), may hold values from -6 to 6
- grad_out: bfloat16 [16384, 2560], P(('seq', 'exp')), may hold values from -1.5 to 1.5
- expert_ids: int32 [16384, 6], P(('seq', 'exp')), may hold values from 0 to 127, as said below
- gate_weights: float32 [16384, 6], P(('seq', 'exp')), may hold values from 0.25 to 4
- w_gate: bfloat16 [128, 2560, 768], P(('seq', 'exp')), may hold values from -0.125 to 0.125
- w_up: bfloat16 [128, 2560, 768], P(('seq', 'exp')), may hold values from -0.125 to 0.125
- w_down: bfloat16 [128, 768, 2560], P(('seq', 'exp')), may hold values from -0.21875 to 0.21875
Outputs:
- grad_in: bfloat16 [16384, 2560], P(('seq', 'exp'))
- grad_gates: bfloat16 [16384, 6], P(('seq', 'exp'))
The draws below stay inside these ranges and needn't reach their ends.
Inputs may be any that keep to these rules, and one draw needn't show every extreme that they name: `expert_ids`: expert e lies in group e // 8. Each row names 6 different experts: entries 2j and 2j + 1 (j = 0, 1, 2) lie in one group, and the three groups of a row differ. Among the 128 rows of one device each group is named by exactly 24 rows, no expert is named more than 9 times, and in every device one expert is named exactly 9 times.
All inputs are finite; a program needn't handle non-finite values.
Results may differ from the reference program's by a relative error of at most 0.0057.
Values may be sent and summed in bfloat16 or wider, within the bound.
No kernel may reach another device: no remote copies, remote signals or barrier semaphores. Data moves between devices by JAX's collectives and lax.ppermute only.
A program may use at most 128 MiB of HBM per device.

```python
import math
import jax
import jax.numpy as jnp
from jax import lax

D = 2560
FFE = 768
TOP = 6
TOK_DEV = 128
EXPERTS = 128
CAP = 9
TOKENS = 16384
N_SEQ = 16
N_EXP = 8
DEVICES = 128


def draw_expert_ids(key, part):
    key = jax.random.fold_in(key, 11)
    unit_index = jnp.arange(3 * TOK_DEV, dtype=jnp.int32)
    group_slot = unit_index % N_SEQ
    visit = unit_index // N_SEQ
    first_drawn = 2 * visit % N_EXP
    second_drawn = (2 * visit + 1) % N_EXP
    others = N_EXP - 1
    later = visit - CAP
    first_hot = jnp.where(visit < CAP, 0, 1 + 2 * later % others)
    second_hot = jnp.where(visit < CAP, 1 + visit % others, 1 + (2 * later + 1) % others)

    def one_block(block_key):
        key_hot, key_group, key_member, key_token = jax.random.split(block_key, 4)
        hot_group = jax.random.randint(key_hot, (), 0, N_SEQ)
        is_hot = group_slot == hot_group
        first_local = jnp.where(is_hot, first_hot, first_drawn)
        second_local = jnp.where(is_hot, second_hot, second_drawn)
        group_order = jax.random.permutation(key_group, N_SEQ).astype(jnp.int32)
        member_order = jax.vmap(lambda member_key: jax.random.permutation(member_key, N_EXP))(jax.random.split(key_member, N_SEQ)).astype(jnp.int32)
        group_label = group_order[group_slot]
        first_id = group_label * N_EXP + member_order[group_slot, first_local]
        second_id = group_label * N_EXP + member_order[group_slot, second_local]
        chosen = jnp.stack([first_id, second_id], axis=1).reshape(TOK_DEV, 6)
        token_order = jax.random.permutation(key_token, TOK_DEV)
        return chosen[token_order]
    blocks = jax.vmap(one_block)(jax.random.split(key, DEVICES))
    return blocks.reshape(TOKENS, 6).astype(jnp.int32)


def block_scale(rng, extent, pieces, low, largest):
    def one(dim, blocks):
        draws = jax.random.uniform(jax.random.fold_in(jax.random.fold_in(rng, 6), dim), (blocks,), jnp.float32, low / len(pieces), largest / len(pieces))
        return jnp.repeat(jnp.exp(draws), extent[dim] // blocks).reshape((-1,) + (1,) * (len(extent) - dim - 1))

    factor_of = one(*pieces[0])
    for cut in pieces[1:]:
        factor_of = factor_of * one(*cut)
    return factor_of


def scatter_about(rng, shape, width, most, shards=(), held_as=jnp.bfloat16):
    result = width * jax.random.normal(rng, shape, jnp.float32)
    if shards:
        result = result * block_scale(rng, shape, shards, -0.22, 0.18)
    return jnp.clip(result, -most, most).astype(held_as)


def setup_inputs(seed: int = 0) -> dict:
    seeds = jax.random.split(jax.random.key(seed), 8)
    hidden_in = scatter_about(seeds[0], (TOKENS, D), 1.0, 6.0, ((0, 128),))
    grad_out = scatter_about(seeds[1], (TOKENS, D), 0.25, 1.5, ((0, 128),))
    expert_ids = draw_expert_ids(jax.random.fold_in(seeds[7], 71), 0)
    gate_weights = jnp.clip(jnp.exp(math.log(4.0) - 2.7725887 * jax.random.uniform(seeds[3], (TOKENS, TOP), jnp.float32) ** block_scale(seeds[3], (TOKENS, TOP), ((0, 128),), -0.2, 0.2)), 0.25, 4.0)
    w_gate = scatter_about(seeds[4], (EXPERTS, D, FFE), D ** -0.5, 0.125, ((0, 128),))
    w_up = scatter_about(seeds[5], (EXPERTS, D, FFE), D ** -0.5, 0.125, ((0, 128),))
    w_down = scatter_about(seeds[6], (EXPERTS, FFE, D), FFE ** -0.5, 0.21875, ((0, 128),))
    return dict(hidden_in=hidden_in, grad_out=grad_out, expert_ids=expert_ids, gate_weights=gate_weights, w_gate=w_gate, w_up=w_up, w_down=w_down)


def slot_numbers(chosen, experts):
    onehot = (chosen[:, None] == jnp.arange(experts, dtype=jnp.int32)[None, :]).astype(jnp.int32)
    earlier = jnp.cumsum(onehot, axis=0) - onehot
    return jnp.sum(earlier * onehot, axis=1).astype(jnp.int32)


def expert_backward(rows_in, rows_grad, gate_mat, up_mat, down_mat):
    pre_gate = jnp.dot(rows_in, gate_mat, preferred_element_type=jnp.float32)
    pre_up = jnp.dot(rows_in, up_mat, preferred_element_type=jnp.float32)
    sigmoid = jax.nn.sigmoid(pre_gate)
    active = pre_gate * sigmoid
    hidden = (active * pre_up).astype(jnp.bfloat16)
    output = jnp.dot(hidden, down_mat, preferred_element_type=jnp.float32)
    gate_dot = jnp.sum(output * rows_grad.astype(jnp.float32), axis=-1).astype(jnp.bfloat16)
    contract = (((1,), (1,)), ((), ()))
    grad_hidden = lax.dot_general(rows_grad, down_mat, contract, preferred_element_type=jnp.float32)
    grad_gate = (grad_hidden * pre_up * sigmoid * (1.0 + pre_gate * (1.0 - sigmoid))).astype(jnp.bfloat16)
    grad_up = (grad_hidden * active).astype(jnp.bfloat16)
    returned = lax.dot_general(grad_gate, gate_mat, contract, preferred_element_type=jnp.float32)
    returned = returned + lax.dot_general(grad_up, up_mat, contract, preferred_element_type=jnp.float32)
    return returned.astype(jnp.bfloat16), gate_dot


def reference(hidden_in, grad_out, expert_ids, gate_weights, w_gate, w_up, w_down):
    blocked = expert_ids.reshape(DEVICES, TOK_DEV * TOP).astype(jnp.int32)
    slots = jax.vmap(lambda row_ids: slot_numbers(row_ids, EXPERTS))(blocked)
    source = jnp.arange(DEVICES, dtype=jnp.int32)[:, None]
    target = (blocked * (DEVICES * CAP) + source * CAP + slots).reshape(-1)
    pair_index = jnp.arange(TOKENS * TOP, dtype=jnp.int32)
    table_tok = jnp.full((EXPERTS * DEVICES * CAP,), TOKENS, jnp.int32).at[target].set(pair_index // TOP)
    table_pair = jnp.full((EXPERTS * DEVICES * CAP,), TOKENS * TOP, jnp.int32).at[target].set(pair_index)
    table_tok = table_tok.reshape(EXPERTS, DEVICES * CAP)
    table_pair = table_pair.reshape(EXPERTS, DEVICES * CAP)
    padded_in = jnp.concatenate([hidden_in, jnp.zeros((1, D), hidden_in.dtype)], axis=0)
    padded_grad = jnp.concatenate([grad_out, jnp.zeros((1, D), grad_out.dtype)], axis=0)
    gates_ext = jnp.concatenate([gate_weights.reshape(-1), jnp.zeros((1,), jnp.float32)], axis=0)

    def scan_step(carry, slab_items):
        grad_sum, gate_grads = carry
        gate_mat, up_mat, down_mat, token_rows, pair_rows = slab_items
        returned, gate_dot = expert_backward(padded_in[token_rows], padded_grad[token_rows], gate_mat, up_mat, down_mat)
        weight = gates_ext[pair_rows]
        grad_sum = grad_sum.at[token_rows].add(weight[:, None] * returned.astype(jnp.float32))
        gate_grads = gate_grads.at[pair_rows].set(gate_dot)
        return (grad_sum, gate_grads), None

    start = (jnp.zeros((TOKENS + 1, D), jnp.float32), jnp.zeros((TOKENS * TOP + 1,), jnp.bfloat16))
    (grad_sum, gate_grads), _ = lax.scan(scan_step, start, (w_gate, w_up, w_down, table_tok, table_pair))
    grad_in = grad_sum[:TOKENS].astype(jnp.bfloat16)
    grad_gates = gate_grads[:TOKENS * TOP].reshape(TOKENS, TOP)
    return grad_in, grad_gates
```

```python
import jax
import jax.numpy as jnp
from jax import lax
from jax.sharding import PartitionSpec as P

BF = jnp.bfloat16
F32 = jnp.float32
LANES = 128


def dot(a, b):
    return jnp.dot(a, b, preferred_element_type=F32)


def dot_t(a, b):
    return lax.dot_general(a, b, (((0,), (0,)), ((), ())), preferred_element_type=F32)


def dot_nt(a, b):
    return lax.dot_general(a, b, (((1,), (1,)), ((), ())), preferred_element_type=F32)


def earlier_counts(names):
    n = names.shape[-2]
    lower = (jnp.arange(n)[:, None] > jnp.arange(n)[None, :]).astype(BF)
    counts = jnp.einsum("ij,...jm->...im", lower, names.astype(BF), preferred_element_type=F32)
    return jnp.where(names, counts, -1.0)


def weight_parts(weights):
    first = lax.reduce_precision(weights, 8, 7)
    rest = weights - first
    second = lax.reduce_precision(rest, 8, 7)
    third = lax.reduce_precision(rest - second, 8, 7)
    return first, second, third


def exchange(blocks, n_exp):
    out = [blocks[0]]
    for k in range(1, n_exp):
        out.append(lax.ppermute(blocks[k], "exp", [(i, i ^ k) for i in range(n_exp)]))
    return out


def per_device(hidden_in, grad_out, expert_ids, gate_weights, w_gate, w_up, w_down):
    n_tok, features = hidden_in.shape
    top = expert_ids.shape[1]
    n_seq, n_exp = lax.axis_size("seq"), lax.axis_size("exp")
    group, member = lax.axis_index("seq"), lax.axis_index("exp")
    experts = n_seq * n_exp
    cap = 3 * top * n_tok // (2 * experts)
    per_group = top // 2 * n_tok // n_seq
    half = features // 2
    gate_mat, up_mat, down_mat = w_gate[0], w_up[0], w_down[0]

    meta = jnp.concatenate(
        (expert_ids.astype(F32),) + weight_parts(gate_weights)
        + (jnp.zeros((n_tok, LANES - 4 * top), F32),), axis=1).astype(BF)

    def read_meta(lanes):
        lanes = lanes.astype(F32)
        ids = lanes[:, :top]
        weights = lanes[:, top:2 * top] + lanes[:, 2 * top:3 * top] + lanes[:, 3 * top:4 * top]
        return ids, weights

    column = lax.all_gather(jnp.concatenate((grad_out, meta), axis=1), "exp", axis=0, tiled=True)

    group_ids = expert_ids // n_exp
    in_group = jnp.any(group_ids[:, :, None] == jnp.arange(n_seq)[None, None, :], axis=1)
    group_rank = earlier_counts(in_group).T
    pick = (group_rank[:, None, :] == jnp.arange(per_group, dtype=F32)[None, :, None])
    pick = pick.astype(BF).reshape(n_seq * per_group, n_tok)
    send = dot(pick, jnp.concatenate((hidden_in, meta), axis=1)).astype(BF)
    hub = lax.all_to_all(send.reshape(n_seq, per_group, features + LANES), "seq", 0, 0, tiled=True)
    hub = hub.reshape(n_seq * per_group, features + LANES)

    hub_ids, hub_weights = read_meta(hub[:, features:])
    local = jnp.arange(n_exp) + group * n_exp
    hits = hub_ids[:, :, None] == local.astype(F32)[None, None, :]
    named = jnp.any(hits, axis=1)
    weight_a = jnp.sum(jnp.where(hits, hub_weights[:, :, None], 0.0), axis=1)
    rank = earlier_counts(named.reshape(n_seq, per_group, n_exp)).reshape(n_seq * per_group, n_exp)
    block = (jnp.arange(n_seq * per_group) // per_group).astype(F32)
    slot_a = jnp.where(named, block[:, None] * cap + rank, -1.0)
    rows_a = n_seq * cap
    place = jnp.arange(rows_a, dtype=F32)
    put_a, wput_a = [], []
    for k in range(n_exp):
        mine = (jnp.arange(n_exp) == (member ^ k))[None, :]
        slot_k = jnp.sum(jnp.where(mine, slot_a, 0.0), axis=1)
        weight_k = jnp.sum(jnp.where(mine, weight_a, 0.0), axis=1)
        hot = slot_k[None, :] == place[:, None]
        put_a.append(hot)
        wput_a.append(jnp.where(hot, weight_k[None, :], 0.0))
    blocks = [dot(hot.astype(BF), hub[:, :features]).astype(BF) for hot in put_a]
    rows_in = jnp.concatenate(exchange(blocks, n_exp), axis=0)

    col_ids, col_weights = read_meta(column[:, features:])
    theirs = (jnp.arange(n_seq) * n_exp + member).astype(F32)
    hits_b = col_ids[:, :, None] == theirs[None, None, :]
    named_b = jnp.any(hits_b, axis=1)
    weight_b = jnp.sum(jnp.where(hits_b, col_weights[:, :, None], 0.0), axis=1)
    rank_b = earlier_counts(named_b.reshape(n_exp, n_tok, n_seq)).reshape(n_exp * n_tok, n_seq)
    order = (jnp.arange(n_exp * n_tok) // n_tok) ^ member
    slot_b = jnp.where(named_b, order[:, None].astype(F32) * cap + rank_b, -1.0)
    rows_b = n_exp * cap
    put_b = slot_b.T[:, None, :] == jnp.arange(rows_b, dtype=F32)[None, :, None]
    send_b = dot(put_b.astype(BF).reshape(n_seq * rows_b, n_exp * n_tok), column[:, :features]).astype(BF)
    recv_b = lax.all_to_all(send_b.reshape(n_seq, rows_b, features), "seq", 0, 0, tiled=True)
    recv_b = recv_b.reshape(n_seq * rows_b, features)

    total = n_seq * n_exp * cap
    row = jnp.arange(total)
    k_of, s_of, c_of = row // rows_a, row % rows_a // cap, row % cap
    order_a = (s_of * rows_b + k_of * cap + c_of)[:, None] == row[None, :]
    order_a = order_a.astype(BF)
    rows_grad = dot(order_a, recv_b).astype(BF)

    pre_gate = dot(rows_in, gate_mat)
    pre_up = dot(rows_in, up_mat)
    sigmoid = jax.nn.sigmoid(pre_gate)
    active = pre_gate * sigmoid
    hidden = (active * pre_up).astype(BF)
    grad_hidden = dot_nt(rows_grad, down_mat)
    gate_dot = jnp.sum(hidden.astype(F32) * grad_hidden, axis=1).astype(BF)
    grad_gate = (grad_hidden * pre_up * sigmoid * (1.0 + pre_gate * (1.0 - sigmoid))).astype(BF)
    grad_up = (grad_hidden * active).astype(BF)
    returned = (dot_nt(grad_gate, gate_mat) + dot_nt(grad_up, up_mat)).astype(BF)
    lane = jnp.arange(LANES) == group * n_exp + member
    gate_lanes = jnp.where(lane[None, :], gate_dot[:, None], jnp.zeros((), BF))

    back_a = jnp.concatenate((returned[:, :half], gate_lanes), axis=1)
    got = exchange([back_a[k * rows_a:(k + 1) * rows_a] for k in range(n_exp)], n_exp)
    got = jnp.concatenate(got, axis=0)
    hot_a = jnp.concatenate(put_a, axis=0).astype(BF)
    weights_a = jnp.concatenate(wput_a, axis=0)
    first, second, _ = weight_parts(weights_a)
    sums = dot_t(first.astype(BF), got[:, :half]) + dot_t(second.astype(BF), got[:, :half])
    gates = dot_t(hot_a, got[:, half:])
    back = jnp.concatenate((sums, gates), axis=1).astype(BF)
    back = lax.all_to_all(back.reshape(n_seq, per_group, half + LANES), "seq", 0, 0, tiled=True)
    final_a = dot_t(pick, back.reshape(n_seq * per_group, half + LANES))

    back_b = dot_t(order_a, returned[:, half:]).astype(BF)
    got_b = lax.all_to_all(back_b.reshape(n_seq, rows_b, half), "seq", 0, 0, tiled=True)
    got_b = got_b.reshape(n_seq * rows_b, half)
    parts = []
    for k in range(n_exp):
        start = (member ^ k) * n_tok
        slot_k = lax.dynamic_slice_in_dim(slot_b, start, n_tok, 0)
        weight_k = lax.dynamic_slice_in_dim(weight_b, start, n_tok, 0)
        hot = slot_k[:, :, None] == jnp.arange(rows_b, dtype=F32)[None, None, :]
        mixed = jnp.where(hot, weight_k[:, :, None], 0.0).reshape(n_tok, n_seq * rows_b)
        first, second, _ = weight_parts(mixed)
        parts.append((dot(first.astype(BF), got_b) + dot(second.astype(BF), got_b)).astype(BF))
    final_b = sum(p.astype(F32) for p in exchange(parts, n_exp))

    grad_in = jnp.concatenate((final_a[:, :half], final_b), axis=1).astype(BF)
    table = final_a[:, half:]
    chosen = expert_ids[:, :, None] == jnp.arange(experts)[None, None, :]
    grad_gates = jnp.sum(jnp.where(chosen, table[:, None, :experts], 0.0), axis=2).astype(BF)
    return grad_in, grad_gates


def solution(mesh):
    rows, mats = P(("seq", "exp"), None), P(("seq", "exp"), None, None)
    return jax.shard_map(
        per_device, mesh=mesh, in_specs=(rows,) * 4 + (mats,) * 3, out_specs=(rows, rows), check_vma=False
    )
```

```python
import jax
import jax.numpy as jnp
from jax import lax
from jax.experimental import pallas as pl
from jax.experimental.pallas import tpu as pltpu
from jax.sharding import PartitionSpec as P

BF = jnp.bfloat16
F32 = jnp.float32
LANES = 128


def dot(a, b):
    return jnp.dot(a, b, preferred_element_type=F32)


def dot_t(a, b):
    return lax.dot_general(a, b, (((0,), (0,)), ((), ())), preferred_element_type=F32)


def dot_nt(a, b):
    return lax.dot_general(a, b, (((1,), (1,)), ((), ())), preferred_element_type=F32)


def earlier_counts(names):
    n = names.shape[-2]
    lower = (jnp.arange(n)[:, None] > jnp.arange(n)[None, :]).astype(BF)
    counts = jnp.einsum("ij,...jm->...im", lower, names.astype(BF), preferred_element_type=F32)
    return jnp.where(names, counts, -1.0)


def barrier(*values):
    return lax.optimization_barrier(values)


def exchange(blocks, n_exp):
    out = [blocks[0]]
    for k in range(1, n_exp):
        out.append(lax.ppermute(blocks[k], "exp", [(i, i ^ k) for i in range(n_exp)]))
    return out


def whole(shape, at=(0, 0)):
    return pl.BlockSpec(shape, lambda *_: at, pipeline_mode=pl.Buffered(1))


def params(mib):
    return pltpu.CompilerParams(vmem_limit_bytes=mib * 2**20)


def cost(flops, nbytes):
    return pl.CostEstimate(flops=flops, bytes_accessed=nbytes, transcendentals=0)


def window_tables(n_seq, n_exp, cap):
    pair = 2 * n_exp * cap
    d = jnp.arange(pair)
    source = d % (n_exp * cap) // cap * 32 + d // (n_exp * cap) * cap + d % cap
    i = jnp.arange(n_seq // 2)
    at = source[None, :] + (2 * cap - 16) * i[:, None]
    wide = jnp.arange(32 * n_exp)
    to_b = (at[:, :, None] == wide[None, None, :]).astype(BF)
    to_a = (at[:, None, :] == wide[None, :, None]).astype(BF)
    return to_b, to_a


def pre_kernel(n_exp, pairs, table, *refs):
    blocks, (gate, up, out_gate, out_up, rows) = refs[:n_exp], refs[n_exp:]
    size = table.shape[1]

    @pl.when(pl.program_id(0) == 0)
    def _():
        for i in range(pairs):
            window = jnp.concatenate([b[16 * i:16 * i + 32, :] for b in blocks], axis=0)
            rows[size * i:size * (i + 1), :] = dot(table[i], window).astype(BF)

    out_gate[...] = dot(rows[...], gate[...])
    out_up[...] = dot(rows[...], up[...])


def pre_products(table, blocks, gate_mat, up_mat):
    n_exp, pairs = len(blocks), table.shape[0]
    rows, features = blocks[0].shape
    total, units = rows * n_exp, gate_mat.shape[1]
    wide = 256 if units % 256 == 0 else units
    column = pl.BlockSpec((features, wide), lambda j: (0, j))
    result = pl.BlockSpec((total, wide), lambda j: (0, j))
    return pl.pallas_call(
        lambda *refs: pre_kernel(n_exp, pairs, *refs),
        grid=(units // wide,),
        in_specs=[whole(table.shape, (0, 0, 0))] + [whole((rows, features))] * n_exp + [column, column],
        out_specs=[result, result],
        out_shape=[jax.ShapeDtypeStruct((total, units), F32)] * 2,
        scratch_shapes=[pltpu.VMEM((total, features), BF)],
        compiler_params=params(44),
        cost_estimate=cost(4 * total * features * units, 2 * total * features + 4 * features * units + 8 * total * units),
        name="pre_products",
    )(table, *blocks, gate_mat, up_mat)


def grad_kernel(lane, grad, down, pre_gate, pre_up, out_gate, out_up, out_dot):
    grad_hidden = dot_nt(grad[...], down[...])
    gate, up = pre_gate[...], pre_up[...]
    sigmoid = jax.nn.sigmoid(gate)
    active = gate * sigmoid
    hidden = (active * up).astype(BF).astype(F32)
    gate_dot = jnp.sum(hidden * grad_hidden, axis=1, keepdims=True)
    out_dot[...] = (gate_dot * lane[0:1, :]).astype(BF)
    out_gate[...] = (grad_hidden * up * sigmoid * (1.0 + gate * (1.0 - sigmoid))).astype(BF)
    out_up[...] = (grad_hidden * active).astype(BF)


def hidden_grads(lane, rows_grad, down_mat, pre_gate, pre_up):
    total, features = rows_grad.shape
    units = down_mat.shape[0]
    tall = total // 4
    row = lambda width: pl.BlockSpec((tall, width), lambda i: (i, 0))
    return pl.pallas_call(
        grad_kernel,
        grid=(4,),
        in_specs=[whole(lane.shape), row(features), whole(down_mat.shape), row(units), row(units)],
        out_specs=[row(units), row(units), row(LANES)],
        out_shape=[jax.ShapeDtypeStruct((total, units), BF)] * 2 + [jax.ShapeDtypeStruct((total, LANES), BF)],
        compiler_params=params(44),
        cost_estimate=cost(2 * total * features * units, 2 * total * features + 2 * features * units + 12 * total * units),
        name="hidden_grads",
    )(lane, rows_grad, down_mat, pre_gate, pre_up)


def back_a_kernel(n_exp, pairs, table, grad_gate, grad_up, gate, up, gate_dot, *outs):
    half = gate.shape[0]
    size = table.shape[2]

    def reorder(values, start, width):
        before = None
        for i in range(pairs):
            moved = dot(table[i], values[size * i:size * (i + 1), :])
            for k in range(n_exp):
                part = moved[32 * k:32 * k + 16, :]
                if before is not None:
                    part = part + before[32 * k + 16:32 * k + 32, :]
                outs[k][16 * i:16 * i + 16, start:start + width] = part.astype(BF)
            before = moved
        for k in range(n_exp):
            part = before[32 * k + 16:32 * k + 32, :]
            outs[k][16 * pairs:16 * pairs + 16, start:start + width] = part.astype(BF)

    wide = 256 if half % 256 == 0 else half
    for start in range(0, half, wide):
        values = dot_nt(grad_gate[...], gate[start:start + wide, :]) + dot_nt(grad_up[...], up[start:start + wide, :])
        reorder(values.astype(BF), start, wide)
    reorder(gate_dot[...], half, LANES)


def returned_a(table, grad_gate, grad_up, gate_mat, up_mat, gate_dot, n_exp):
    total, units = grad_gate.shape
    half = gate_mat.shape[0] // 2
    pairs = table.shape[0]
    mat = whole((half, units))
    block = (total // n_exp, half + LANES)
    return pl.pallas_call(
        lambda *refs: back_a_kernel(n_exp, pairs, *refs),
        grid=(1,),
        in_specs=[whole(table.shape, (0, 0, 0)), whole(grad_gate.shape), whole(grad_up.shape), mat, mat, whole(gate_dot.shape)],
        out_specs=[whole(block)] * n_exp,
        out_shape=[jax.ShapeDtypeStruct(block, BF)] * n_exp,
        compiler_params=params(44),
        cost_estimate=cost(4 * total * half * units, 4 * half * units + 4 * total * units + 2 * total * half),
        name="returned_a",
    )(table, grad_gate, grad_up, gate_mat, up_mat, gate_dot)


def back_b_kernel(grad_gate, grad_up, gate, up, out):
    out[...] = (dot_nt(grad_gate[...], gate[...]) + dot_nt(grad_up[...], up[...])).astype(BF)


def returned_b(grad_gate, grad_up, gate_mat, up_mat):
    total, units = grad_gate.shape
    half = gate_mat.shape[0] // 2
    wide = 256 if half % 256 == 0 else half
    mat = pl.BlockSpec((wide, units), lambda j: (half // wide + j, 0))
    return pl.pallas_call(
        back_b_kernel,
        grid=(half // wide,),
        in_specs=[whole(grad_gate.shape), whole(grad_up.shape), mat, mat],
        out_specs=pl.BlockSpec((total, wide), lambda j: (0, j)),
        out_shape=jax.ShapeDtypeStruct((total, half), BF),
        compiler_params=params(44),
        cost_estimate=cost(4 * total * half * units, 4 * half * units + 4 * total * units + 2 * total * half),
        name="returned_b",
    )(grad_gate, grad_up, gate_mat, up_mat)


def sum_kernel(n_exp, slot, weight, *refs):
    blocks, (out,) = refs[:n_exp], refs[n_exp:]
    half = out.shape[1] - LANES
    rows = blocks[0].shape[0]
    place = lax.broadcasted_iota(jnp.int32, (slot.shape[0], rows), 1).astype(F32)
    sums = jnp.zeros((slot.shape[0], half), F32)
    gates = jnp.zeros((slot.shape[0], LANES), F32)
    for k in range(n_exp):
        hot = slot[:, k:k + 1] == place
        sums += dot(jnp.where(hot, weight[:, k:k + 1], 0.0).astype(BF), blocks[k][:, :half])
        gates += dot(jnp.where(hot, 1.0, 0.0).astype(BF), blocks[k][:, half:])
    out[:, :half] = sums.astype(BF)
    out[:, half:] = gates.astype(BF)


def group_sums(slot, weight, blocks):
    n_exp = len(blocks)
    n_rows, width = slot.shape[0], blocks[0].shape[1]
    return pl.pallas_call(
        lambda *refs: sum_kernel(n_exp, *refs),
        grid=(1,),
        in_specs=[whole(slot.shape), whole(weight.shape)] + [whole(blocks[0].shape)] * n_exp,
        out_specs=whole((n_rows, width)),
        out_shape=jax.ShapeDtypeStruct((n_rows, width), BF),
        compiler_params=params(32),
        cost_estimate=cost(2 * n_rows * blocks[0].shape[0] * n_exp * width, 2 * n_exp * blocks[0].size),
        name="group_sums",
    )(slot, weight, *blocks)


def per_device(hidden_in, grad_out, expert_ids, gate_weights, w_gate, w_up, w_down):
    n_tok, features = hidden_in.shape
    top = expert_ids.shape[1]
    n_seq, n_exp = lax.axis_size("seq"), lax.axis_size("exp")
    group, member = lax.axis_index("seq"), lax.axis_index("exp")
    experts = n_seq * n_exp
    cap = 3 * top * n_tok // (2 * experts)
    per_group = top // 2 * n_tok // n_seq
    half = features // 2
    gate_mat, up_mat, down_mat = w_gate[0], w_up[0], w_down[0]
    partner = member ^ jnp.arange(n_exp)
    to_b, to_a = window_tables(n_seq, n_exp, cap)

    meta = jnp.concatenate(
        (expert_ids.astype(BF), gate_weights.astype(BF), jnp.zeros((n_tok, LANES - 2 * top), BF)), axis=1)

    def read_meta(lanes):
        lanes = lanes.astype(F32)
        return lanes[:, :top], lanes[:, top:2 * top]

    column = lax.all_gather(jnp.concatenate((grad_out, meta), axis=1), "exp", axis=0, tiled=True)

    group_ids = expert_ids // n_exp
    in_group = jnp.any(group_ids[:, :, None] == jnp.arange(n_seq)[None, None, :], axis=1)
    group_rank = earlier_counts(in_group).T
    pick = (group_rank[:, None, :] == jnp.arange(per_group, dtype=F32)[None, :, None])
    pick = pick.astype(BF).reshape(n_seq * per_group, n_tok)
    send = dot(pick, jnp.concatenate((hidden_in, meta), axis=1)).astype(BF)
    hub = lax.all_to_all(send.reshape(n_seq, per_group, features + LANES), "seq", 0, 0, tiled=True)
    hub = hub.reshape(n_seq * per_group, features + LANES)

    col_ids, col_weights = read_meta(column[:, features:])
    theirs = (jnp.arange(n_seq) * n_exp + member).astype(F32)
    hits_b = col_ids[:, :, None] == theirs[None, None, :]
    named_b = jnp.any(hits_b, axis=1)
    weight_b = jnp.sum(jnp.where(hits_b, col_weights[:, :, None], 0.0), axis=1)
    rank_b = earlier_counts(named_b.reshape(n_exp, n_tok, n_seq)).reshape(n_exp * n_tok, n_seq)
    order = (jnp.arange(n_exp * n_tok) // n_tok) ^ member
    slot_b = jnp.where(named_b, order[:, None].astype(F32) * cap + rank_b, -1.0)
    rows_b = n_exp * cap
    put_b = slot_b.T[:, None, :] == jnp.arange(rows_b, dtype=F32)[None, :, None]
    send_b = dot(put_b.astype(BF).reshape(n_seq * rows_b, n_exp * n_tok), column[:, :features]).astype(BF)
    hub, send_b = barrier(hub, send_b)
    recv_b = lax.all_to_all(send_b.reshape(n_seq, rows_b, features), "seq", 0, 0, tiled=True)
    recv_b = recv_b.reshape(n_seq * rows_b, features)

    hub_ids, hub_weights = read_meta(hub[:, features:])
    local = (partner + group * n_exp).astype(F32)
    hits = hub_ids[:, :, None] == local[None, None, :]
    named = jnp.any(hits, axis=1)
    weight_a = jnp.sum(jnp.where(hits, hub_weights[:, :, None], 0.0), axis=1)
    rank = earlier_counts(named.reshape(n_seq, per_group, n_exp)).reshape(n_seq * per_group, n_exp)
    block = (jnp.arange(n_seq * per_group) // per_group).astype(F32)
    slot_a = jnp.where(named, block[:, None] * cap + rank, -1.0)
    rows_a = n_seq * cap
    put_a = slot_a.T[:, None, :] == jnp.arange(rows_a, dtype=F32)[None, :, None]
    blocks = [dot(put_a[k].astype(BF), hub[:, :features]).astype(BF) for k in range(n_exp)]
    rows_in = exchange(blocks, n_exp)

    pre_gate, pre_up = pre_products(to_b, rows_in, gate_mat, up_mat)
    lane = jnp.broadcast_to((jnp.arange(LANES) == group * n_exp + member).astype(F32), (8, LANES))
    grad_gate, grad_up, gate_dot = hidden_grads(lane, recv_b, down_mat, pre_gate, pre_up)

    got_a = exchange(returned_a(to_a, grad_gate, grad_up, gate_mat, up_mat, gate_dot, n_exp), n_exp)
    back_b = returned_b(grad_gate, grad_up, gate_mat, up_mat)
    got_b = lax.all_to_all(back_b.reshape(n_seq, rows_b, half), "seq", 0, 0, tiled=True)
    *got_a, got_b = barrier(*got_a, got_b)

    back = group_sums(slot_a, weight_a, got_a)
    back = lax.all_to_all(back.reshape(n_seq, per_group, half + LANES), "seq", 0, 0, tiled=True)
    final_a = dot_t(pick, back.reshape(n_seq * per_group, half + LANES))

    got_b = got_b.reshape(n_seq * rows_b, half)
    parts = []
    for k in range(n_exp):
        start = (member ^ k) * n_tok
        slot_k = lax.dynamic_slice_in_dim(slot_b, start, n_tok, 0)
        weight_k = lax.dynamic_slice_in_dim(weight_b, start, n_tok, 0)
        hot = slot_k[:, :, None] == jnp.arange(rows_b, dtype=F32)[None, None, :]
        mixed = jnp.where(hot, weight_k[:, :, None], 0.0).reshape(n_tok, n_seq * rows_b)
        parts.append(dot(mixed.astype(BF), got_b).astype(BF))
    final_b = sum(p.astype(F32) for p in exchange(parts, n_exp))

    grad_in = jnp.concatenate((final_a[:, :half], final_b), axis=1).astype(BF)
    table = final_a[:, half:]
    chosen = expert_ids[:, :, None] == jnp.arange(experts)[None, None, :]
    grad_gates = jnp.sum(jnp.where(chosen, table[:, None, :experts], 0.0), axis=2).astype(BF)
    return grad_in, grad_gates


def solution(mesh):
    rows, mats = P(("seq", "exp"), None), P(("seq", "exp"), None, None)
    return jax.shard_map(
        per_device, mesh=mesh, in_specs=(rows,) * 4 + (mats,) * 3, out_specs=(rows, rows), check_vma=False
    )
```

```python
import jax
import jax.numpy as jnp
from jax import lax
from jax.experimental import pallas as pl
from jax.experimental.pallas import tpu as pltpu
from jax.sharding import PartitionSpec as P

BF = jnp.bfloat16
F32 = jnp.float32
LANES = 128


def dot(a, b):
    return jnp.dot(a, b, preferred_element_type=F32)


def dot_t(a, b):
    return lax.dot_general(a, b, (((0,), (0,)), ((), ())), preferred_element_type=F32)


def dot_nt(a, b):
    return lax.dot_general(a, b, (((1,), (1,)), ((), ())), preferred_element_type=F32)


def earlier_counts(names):
    n = names.shape[-2]
    lower = (jnp.arange(n)[:, None] > jnp.arange(n)[None, :]).astype(BF)
    counts = jnp.einsum("ij,...jm->...im", lower, names.astype(BF), preferred_element_type=F32)
    return jnp.where(names, counts, -1.0)


def barrier(*values):
    return lax.optimization_barrier(values)


def exchange(blocks, n_exp):
    out = [blocks[0]]
    for k in range(1, n_exp):
        out.append(lax.ppermute(blocks[k], "exp", [(i, i ^ k) for i in range(n_exp)]))
    return out


def whole(shape, at=(0, 0)):
    return pl.BlockSpec(shape, lambda *_: at, pipeline_mode=pl.Buffered(1))


def params(mib):
    return pltpu.CompilerParams(vmem_limit_bytes=mib * 2**20)


def cost(flops, nbytes):
    return pl.CostEstimate(flops=flops, bytes_accessed=nbytes, transcendentals=0)


def window_tables(n_seq, n_exp, cap):
    pair = 2 * n_exp * cap
    d = jnp.arange(pair)
    source = d % (n_exp * cap) // cap * 32 + d // (n_exp * cap) * cap + d % cap
    i = jnp.arange(n_seq // 2)
    at = source[None, :] + (2 * cap - 16) * i[:, None]
    wide = jnp.arange(32 * n_exp)
    to_b = (at[:, :, None] == wide[None, None, :]).astype(BF)
    to_a = (at[:, None, :] == wide[None, :, None]).astype(BF)
    return to_b, to_a


def pre_kernel(n_exp, pairs, table, *refs):
    blocks, (gate, up, out_gate, out_up, rows) = refs[:n_exp], refs[n_exp:]
    size = table.shape[1]

    @pl.when(pl.program_id(0) == 0)
    def _():
        for i in range(pairs):
            window = jnp.concatenate([b[16 * i:16 * i + 32, :] for b in blocks], axis=0)
            rows[size * i:size * (i + 1), :] = dot(table[i], window).astype(BF)

    out_gate[...] = dot(rows[...], gate[...])
    out_up[...] = dot(rows[...], up[...])


def pre_products(table, blocks, gate_mat, up_mat):
    n_exp, pairs = len(blocks), table.shape[0]
    rows, features = blocks[0].shape
    total, units = rows * n_exp, gate_mat.shape[1]
    wide = 256 if units % 256 == 0 else units
    column = pl.BlockSpec((features, wide), lambda j: (0, j))
    result = pl.BlockSpec((total, wide), lambda j: (0, j))
    return pl.pallas_call(
        lambda *refs: pre_kernel(n_exp, pairs, *refs),
        grid=(units // wide,),
        in_specs=[whole(table.shape, (0, 0, 0))] + [whole((rows, features))] * n_exp + [column, column],
        out_specs=[result, result],
        out_shape=[jax.ShapeDtypeStruct((total, units), F32)] * 2,
        scratch_shapes=[pltpu.VMEM((total, features), BF)],
        compiler_params=params(44),
        cost_estimate=cost(4 * total * features * units, 2 * total * features + 4 * features * units + 8 * total * units),
        name="pre_products",
    )(table, *blocks, gate_mat, up_mat)


def grad_kernel(lane, grad, down, pre_gate, pre_up, out_gate, out_up, out_dot):
    grad_hidden = dot_nt(grad[...], down[...])
    gate, up = pre_gate[...], pre_up[...]
    sigmoid = jax.nn.sigmoid(gate)
    active = gate * sigmoid
    hidden = (active * up).astype(BF).astype(F32)
    gate_dot = jnp.sum(hidden * grad_hidden, axis=1, keepdims=True)
    out_dot[...] = (gate_dot * lane[0:1, :]).astype(BF)
    out_gate[...] = (grad_hidden * up * sigmoid * (1.0 + gate * (1.0 - sigmoid))).astype(BF)
    out_up[...] = (grad_hidden * active).astype(BF)


def hidden_grads(lane, rows_grad, down_mat, pre_gate, pre_up):
    total, features = rows_grad.shape
    units = down_mat.shape[0]
    tall = total // 4
    row = lambda width: pl.BlockSpec((tall, width), lambda i: (i, 0))
    return pl.pallas_call(
        grad_kernel,
        grid=(4,),
        in_specs=[whole(lane.shape), row(features), whole(down_mat.shape), row(units), row(units)],
        out_specs=[row(units), row(units), row(LANES)],
        out_shape=[jax.ShapeDtypeStruct((total, units), BF)] * 2 + [jax.ShapeDtypeStruct((total, LANES), BF)],
        compiler_params=params(44),
        cost_estimate=cost(2 * total * features * units, 2 * total * features + 2 * features * units + 12 * total * units),
        name="hidden_grads",
    )(lane, rows_grad, down_mat, pre_gate, pre_up)


def back_a_kernel(n_exp, pairs, table, grad_gate, grad_up, gate, up, gate_dot, *outs):
    wide = gate.shape[0]
    half = outs[0].shape[1] - LANES
    size = table.shape[2]

    def reorder(values, start, width):
        before = None
        for i in range(pairs):
            moved = dot(table[i], values[size * i:size * (i + 1), :])
            for k in range(n_exp):
                part = moved[32 * k:32 * k + 16, :]
                if before is not None:
                    part = part + before[32 * k + 16:32 * k + 32, :]
                outs[k][16 * i:16 * i + 16, pl.ds(start, width)] = part.astype(BF)
            before = moved
        for k in range(n_exp):
            part = before[32 * k + 16:32 * k + 32, :]
            outs[k][16 * pairs:16 * pairs + 16, pl.ds(start, width)] = part.astype(BF)

    j = pl.program_id(0)
    values = dot_nt(grad_gate[...], gate[...]) + dot_nt(grad_up[...], up[...])
    reorder(values.astype(BF), pl.multiple_of(j * wide, wide), wide)

    @pl.when(j == 0)
    def _():
        reorder(gate_dot[...], half, LANES)


def returned_a(table, grad_gate, grad_up, gate_mat, up_mat, gate_dot, n_exp):
    total, units = grad_gate.shape
    half = gate_mat.shape[0] // 2
    pairs = table.shape[0]
    wide = 256 if half % 256 == 0 else half
    mat = pl.BlockSpec((wide, units), lambda j: (j, 0))
    block = (total // n_exp, half + LANES)
    return pl.pallas_call(
        lambda *refs: back_a_kernel(n_exp, pairs, *refs),
        grid=(half // wide,),
        in_specs=[whole(table.shape, (0, 0, 0)), whole(grad_gate.shape), whole(grad_up.shape), mat, mat, whole(gate_dot.shape)],
        out_specs=[whole(block)] * n_exp,
        out_shape=[jax.ShapeDtypeStruct(block, BF)] * n_exp,
        compiler_params=params(44),
        cost_estimate=cost(4 * total * half * units, 4 * half * units + 4 * total * units + 2 * total * half),
        name="returned_a",
    )(table, grad_gate, grad_up, gate_mat, up_mat, gate_dot)


def back_b_kernel(grad_gate, grad_up, gate, up, out):
    out[...] = (dot_nt(grad_gate[...], gate[...]) + dot_nt(grad_up[...], up[...])).astype(BF)


def returned_b(grad_gate, grad_up, gate_mat, up_mat):
    total, units = grad_gate.shape
    half = gate_mat.shape[0] // 2
    wide = 256 if half % 256 == 0 else half
    mat = pl.BlockSpec((wide, units), lambda j: (half // wide + j, 0))
    return pl.pallas_call(
        back_b_kernel,
        grid=(half // wide,),
        in_specs=[whole(grad_gate.shape), whole(grad_up.shape), mat, mat],
        out_specs=pl.BlockSpec((total, wide), lambda j: (0, j)),
        out_shape=jax.ShapeDtypeStruct((total, half), BF),
        compiler_params=params(44),
        cost_estimate=cost(4 * total * half * units, 4 * half * units + 4 * total * units + 2 * total * half),
        name="returned_b",
    )(grad_gate, grad_up, gate_mat, up_mat)


def sum_kernel(n_exp, slot, weight, *refs):
    blocks, (out,) = refs[:n_exp], refs[n_exp:]
    half = out.shape[1] - LANES
    rows = blocks[0].shape[0]
    place = lax.broadcasted_iota(jnp.int32, (slot.shape[0], rows), 1).astype(F32)
    sums = jnp.zeros((slot.shape[0], half), F32)
    gates = jnp.zeros((slot.shape[0], LANES), F32)
    for k in range(n_exp):
        hot = slot[:, k:k + 1] == place
        sums += dot(jnp.where(hot, weight[:, k:k + 1], 0.0).astype(BF), blocks[k][:, :half])
        gates += dot(jnp.where(hot, 1.0, 0.0).astype(BF), blocks[k][:, half:])
    out[:, :half] = sums.astype(BF)
    out[:, half:] = gates.astype(BF)


def group_sums(slot, weight, blocks):
    n_exp = len(blocks)
    n_rows, width = slot.shape[0], blocks[0].shape[1]
    return pl.pallas_call(
        lambda *refs: sum_kernel(n_exp, *refs),
        grid=(1,),
        in_specs=[whole(slot.shape), whole(weight.shape)] + [whole(blocks[0].shape)] * n_exp,
        out_specs=whole((n_rows, width)),
        out_shape=jax.ShapeDtypeStruct((n_rows, width), BF),
        compiler_params=params(32),
        cost_estimate=cost(2 * n_rows * blocks[0].shape[0] * n_exp * width, 2 * n_exp * blocks[0].size),
        name="group_sums",
    )(slot, weight, *blocks)


def named_here(top, eye, meta, local):
    flat = dot_nt(eye[...], meta)
    named = weight = jnp.zeros((local.shape[0], flat.shape[1]), F32)
    for k in range(top):
        hit = flat[k:k + 1, :] == local[:, 0:1]
        named += jnp.where(hit, 1.0, 0.0)
        weight += jnp.where(hit, flat[top + k:top + k + 1, :], 0.0)
    return named, weight


def hub_kernel(top, cap, eye, local, before, block, hub, *outs):
    *blocks, out_slot, out_weight = outs
    features = blocks[0].shape[1]
    named, out_weight[...] = named_here(top, eye, hub[:, features:], local)
    slot = jnp.where(named > 0.0, block[0:1, :] * cap + dot(named.astype(BF), before[...]), -1.0)
    out_slot[...] = slot
    place = lax.broadcasted_iota(jnp.int32, (blocks[0].shape[0], slot.shape[1]), 0).astype(F32)
    for k, out in enumerate(blocks):
        hot = jnp.where(place == slot[k:k + 1, :], 1.0, 0.0).astype(BF)
        out[...] = dot(hot, hub[:, :features]).astype(BF)


def lower_counts(total, size):
    at = jnp.arange(total)
    same = at[:, None] // size == at[None, :] // size
    return (same & (at[:, None] < at[None, :])).astype(BF), jnp.broadcast_to((at // size).astype(F32), (8, total))


def hub_blocks(hub, local, per_group, top, cap):
    n_rows, width = hub.shape
    n_exp = local.shape[0]
    before, block = lower_counts(n_rows, per_group)
    shape = (n_rows // per_group * cap, width - LANES)
    row = (n_exp, n_rows)
    eye = jnp.eye(LANES, dtype=BF)
    *blocks, slot, weight = pl.pallas_call(
        lambda *refs: hub_kernel(top, cap, *refs),
        grid=(1,),
        in_specs=[whole(x.shape) for x in (eye, local, before, block, hub)],
        out_specs=[whole(shape)] * n_exp + [whole(row)] * 2,
        out_shape=[jax.ShapeDtypeStruct(shape, BF)] * n_exp + [jax.ShapeDtypeStruct(row, F32)] * 2,
        compiler_params=params(32),
        cost_estimate=cost(2 * shape[0] * n_exp * n_rows * width, 2 * n_exp * shape[0] * shape[1]),
        name="hub_blocks",
    )(eye, local, before, block, hub)
    return blocks, slot.T, weight.T


def slots_kernel(top, rows, eye, theirs, before, start, meta, out_hot, out_slot, out_weight):
    named, out_weight[...] = named_here(top, eye, meta[...], theirs)
    size = before.shape[0]
    counts = [dot(named[:, at:at + size].astype(BF), before[...]) for at in range(0, named.shape[1], size)]
    slot = jnp.where(named > 0.0, start[0:1, :] + jnp.concatenate(counts, axis=1), -1.0)
    out_slot[...] = slot
    place = lax.broadcasted_iota(jnp.int32, (rows, slot.shape[1]), 0).astype(F32)
    for g in range(0, slot.shape[0], 2):
        pair = [jnp.where(place == slot[i:i + 1, :], 1.0, 0.0) for i in (g, g + 1)]
        out_hot[g * rows:(g + 2) * rows, :] = jnp.concatenate(pair, axis=0).astype(BF)


def column_slots(meta, theirs, member, n_tok, top, cap):
    total = meta.shape[0]
    n_seq, n_exp = theirs.shape[0], total // n_tok
    before, _ = lower_counts(n_tok, n_tok)
    start = ((jnp.arange(total) // n_tok) ^ member) * cap
    start = jnp.broadcast_to(start.astype(F32), (8, total))
    eye = jnp.eye(LANES, dtype=BF)
    shapes = (n_seq * n_exp * cap, total), (n_seq, total), (n_seq, total)
    hot, slot, weight = pl.pallas_call(
        lambda *refs: slots_kernel(top, n_exp * cap, *refs),
        grid=(1,),
        in_specs=[whole(x.shape) for x in (eye, theirs, before, start, meta)],
        out_specs=[whole(shape) for shape in shapes],
        out_shape=[jax.ShapeDtypeStruct(shape, kind) for shape, kind in zip(shapes, (BF, F32, F32))],
        compiler_params=params(32),
        cost_estimate=cost(4 * total * LANES * LANES, 2 * shapes[0][0] * total),
        name="column_slots",
    )(eye, theirs, before, start, meta)
    return hot, slot.T, weight.T


def column_kernel(n_exp, member, place, spread, slot, weight, got, *refs):
    outs, (mixed,) = refs[:n_exp], refs[n_exp:]
    n_tok = outs[0].shape[0]
    for k in range(n_exp):
        rows = pl.ds(pl.multiple_of((member[0] ^ k) * n_tok, n_tok), n_tok)
        hot = dot(slot[rows, :], spread[...]) == place[0:1, :]
        mixed[n_tok * k:n_tok * (k + 1), :] = jnp.where(hot, dot(weight[rows, :], spread[...]), 0.0).astype(BF)
    half = got.shape[1]
    wide = 256 if half % 256 == 0 else half
    for start in range(0, half, wide):
        sums = dot(mixed[...], got[:, start:start + wide]).astype(BF)
        for k in range(n_exp):
            outs[k][:, start:start + wide] = sums[n_tok * k:n_tok * (k + 1), :]


def column_sums(member, slot, weight, got, n_exp):
    n_rows, n_seq = slot.shape
    total, half = got.shape
    at = jnp.arange(total)
    place = jnp.broadcast_to((at % (total // n_seq)).astype(F32), (8, total))
    spread = (jnp.arange(n_seq)[:, None] == at[None, :] // (total // n_seq)).astype(BF)
    block = (n_rows // n_exp, half)
    return pl.pallas_call(
        lambda *refs: column_kernel(n_exp, *refs),
        grid=(1,),
        in_specs=[pl.BlockSpec(memory_space=pltpu.SMEM), whole(place.shape), whole(spread.shape), whole(slot.shape),
                  whole(weight.shape), whole(got.shape)],
        out_specs=[whole(block)] * n_exp,
        out_shape=[jax.ShapeDtypeStruct(block, BF)] * n_exp,
        scratch_shapes=[pltpu.VMEM((n_rows, total), BF)],
        compiler_params=params(32),
        cost_estimate=cost(2 * n_rows * total * half, 2 * total * half + 2 * n_rows * half),
        name="column_sums",
    )(member.reshape(1), place, spread, slot.astype(BF), weight.astype(BF), got)


def per_device(hidden_in, grad_out, expert_ids, gate_weights, w_gate, w_up, w_down):
    n_tok, features = hidden_in.shape
    top = expert_ids.shape[1]
    n_seq, n_exp = lax.axis_size("seq"), lax.axis_size("exp")
    group, member = lax.axis_index("seq"), lax.axis_index("exp")
    experts = n_seq * n_exp
    cap = 3 * top * n_tok // (2 * experts)
    per_group = top // 2 * n_tok // n_seq
    half = features // 2
    gate_mat, up_mat, down_mat = w_gate[0], w_up[0], w_down[0]
    partner = member ^ jnp.arange(n_exp)
    to_b, to_a = window_tables(n_seq, n_exp, cap)

    meta = jnp.concatenate(
        (expert_ids.astype(BF), gate_weights.astype(BF), jnp.zeros((n_tok, LANES - 2 * top), BF)), axis=1)

    column_meta = lax.all_gather(meta, "exp", axis=0, tiled=True)
    column = lax.all_gather(grad_out, "exp", axis=0, tiled=True)
    theirs = jnp.broadcast_to((jnp.arange(n_seq) * n_exp + member).astype(F32)[:, None], (n_seq, LANES))
    put_b, slot_b, weight_b = column_slots(column_meta, theirs, member, n_tok, top, cap)

    group_ids = expert_ids // n_exp
    in_group = jnp.any(group_ids[:, :, None] == jnp.arange(n_seq)[None, None, :], axis=1)
    group_rank = earlier_counts(in_group).T
    pick = (group_rank[:, None, :] == jnp.arange(per_group, dtype=F32)[None, :, None])
    pick = pick.astype(BF).reshape(n_seq * per_group, n_tok)
    send = dot(pick, jnp.concatenate((hidden_in, meta), axis=1)).astype(BF)
    hub = lax.all_to_all(send.reshape(n_seq, per_group, features + LANES), "seq", 0, 0, tiled=True)
    hub = hub.reshape(n_seq * per_group, features + LANES)

    send_b = dot(put_b, column).astype(BF)
    hub, send_b = barrier(hub, send_b)
    rows_b = n_exp * cap
    recv_b = lax.all_to_all(send_b.reshape(n_seq, rows_b, features), "seq", 0, 0, tiled=True)
    recv_b = recv_b.reshape(n_seq * rows_b, features)

    local = jnp.broadcast_to((partner + group * n_exp).astype(F32)[:, None], (n_exp, LANES))
    blocks, slot_a, weight_a = hub_blocks(hub, local, per_group, top, cap)
    rows_in = exchange(blocks, n_exp)

    pre_gate, pre_up = pre_products(to_b, rows_in, gate_mat, up_mat)
    lane = jnp.broadcast_to((jnp.arange(LANES) == group * n_exp + member).astype(F32), (8, LANES))
    grad_gate, grad_up, gate_dot = hidden_grads(lane, recv_b, down_mat, pre_gate, pre_up)

    got_a = exchange(returned_a(to_a, grad_gate, grad_up, gate_mat, up_mat, gate_dot, n_exp), n_exp)
    back_b = returned_b(grad_gate, grad_up, gate_mat, up_mat)
    got_b = lax.all_to_all(back_b.reshape(n_seq, rows_b, half), "seq", 0, 0, tiled=True)
    parts = column_sums(member, slot_b, weight_b, got_b.reshape(n_seq * rows_b, half), n_exp)
    *parts, slot_a = barrier(*parts, slot_a)
    back = group_sums(slot_a, weight_a, got_a)
    back = lax.all_to_all(back.reshape(n_seq, per_group, half + LANES), "seq", 0, 0, tiled=True)
    final_b = sum(p.astype(F32) for p in exchange(parts, n_exp))
    final_a = dot_t(pick, back.reshape(n_seq * per_group, half + LANES))

    grad_in = jnp.concatenate((final_a[:, :half], final_b), axis=1).astype(BF)
    table = final_a[:, half:]
    chosen = expert_ids[:, :, None] == jnp.arange(experts)[None, None, :]
    grad_gates = jnp.sum(jnp.where(chosen, table[:, None, :experts], 0.0), axis=2).astype(BF)
    return grad_in, grad_gates


def solution(mesh):
    rows, mats = P(("seq", "exp"), None), P(("seq", "exp"), None, None)
    return jax.shard_map(
        per_device, mesh=mesh, in_specs=(rows,) * 4 + (mats,) * 3, out_specs=(rows, rows), check_vma=False
    )
```

```python
import jax
import jax.numpy as jnp
from jax import lax
from jax.experimental import pallas as pl
from jax.experimental.pallas import tpu as pltpu
from jax.sharding import PartitionSpec as P

BF = jnp.bfloat16
F32 = jnp.float32
LANES = 128
VMEM_MIB = 60


def dot(a, b):
    return jnp.dot(a, b, preferred_element_type=F32)


def dot_t(a, b):
    return lax.dot_general(a, b, (((0,), (0,)), ((), ())), preferred_element_type=F32)


def dot_nt(a, b):
    return lax.dot_general(a, b, (((1,), (1,)), ((), ())), preferred_element_type=F32)


def earlier_counts(names):
    n = names.shape[-2]
    lower = (jnp.arange(n)[:, None] > jnp.arange(n)[None, :]).astype(BF)
    counts = jnp.einsum("ij,...jm->...im", lower, names.astype(BF), preferred_element_type=F32)
    return jnp.where(names, counts, -1.0)


def barrier(*values):
    return lax.optimization_barrier(values)


def swap(x, k):
    return lax.ppermute(x, "exp", [(i, i ^ k) for i in range(lax.axis_size("exp"))])


def exchange(blocks):
    return [blocks[0]] + [swap(block, 2 * a) for a, block in enumerate(blocks) if a]


def whole(shape, at=(0, 0)):
    return pl.BlockSpec(shape, lambda *_: at, pipeline_mode=pl.Buffered(1))


def params(mib):
    return pltpu.CompilerParams(vmem_limit_bytes=mib * 2**20)


def cost(flops, nbytes):
    return pl.CostEstimate(flops=flops, bytes_accessed=nbytes, transcendentals=0)


def window_tables(n_seq, n_exp, cap):
    pair = 2 * n_exp * cap
    d = jnp.arange(pair)
    source = d % (n_exp * cap) // cap * 32 + d // (n_exp * cap) * cap + d % cap
    i = jnp.arange(n_seq // 2)
    at = source[None, :] + (2 * cap - 16) * i[:, None]
    wide = jnp.arange(32 * n_exp)
    to_b = (at[:, :, None] == wide[None, None, :]).astype(BF)
    to_a = (at[:, None, :] == wide[None, :, None]).astype(BF)
    return to_b, to_a


def pre_kernel(chips, pairs, table, *refs):
    blocks, (gate, up, out_gate, out_up, rows) = refs[:chips], refs[chips:]
    size = table.shape[1]

    @pl.when(pl.program_id(0) == 0)
    def _():
        for i in range(pairs):
            at = [(b, 16 * i + side) for b in blocks for side in (0, b.shape[0] // 2)]
            window = jnp.concatenate([b[start:start + 32, :] for b, start in at], axis=0)
            rows[size * i:size * (i + 1), :] = dot(table[i], window).astype(BF)

    out_gate[...] = dot(rows[...], gate[...])
    out_up[...] = dot(rows[...], up[...])


def pre_products(table, blocks, gate_mat, up_mat):
    chips, pairs = len(blocks), table.shape[0]
    rows, features = blocks[0].shape
    total, units = rows * chips, gate_mat.shape[1]
    wide = 256 if units % 256 == 0 else units
    column = pl.BlockSpec((features, wide), lambda j: (0, j))
    result = pl.BlockSpec((total, wide), lambda j: (0, j))
    return pl.pallas_call(
        lambda *refs: pre_kernel(chips, pairs, *refs),
        grid=(units // wide,),
        in_specs=[whole(table.shape, (0, 0, 0))] + [whole((rows, features))] * chips + [column, column],
        out_specs=[result, result],
        out_shape=[jax.ShapeDtypeStruct((total, units), F32)] * 2,
        scratch_shapes=[pltpu.VMEM((total, features), BF)],
        compiler_params=params(VMEM_MIB),
        cost_estimate=cost(40 * total * features * units, 2 * total * features + 4 * features * units + 8 * total * units),
        name="pre_products",
    )(table, *blocks, gate_mat, up_mat)


def grad_kernel(lane, grad, down, pre_gate, pre_up, out_gate, out_up, out_dot):
    grad_hidden = dot_nt(grad[...], down[...])
    gate, up = pre_gate[...], pre_up[...]
    sigmoid = jax.nn.sigmoid(gate)
    active = gate * sigmoid
    hidden = (active * up).astype(BF).astype(F32)
    gate_dot = jnp.sum(hidden * grad_hidden, axis=1, keepdims=True)
    out_dot[...] = (gate_dot * lane[0:1, :]).astype(BF)
    out_gate[...] = (grad_hidden * up * sigmoid * (1.0 + gate * (1.0 - sigmoid))).astype(BF)
    out_up[...] = (grad_hidden * active).astype(BF)


def hidden_grads(lane, rows_grad, down_mat, pre_gate, pre_up):
    total, features = rows_grad.shape
    units = down_mat.shape[0]
    tall = total // 4
    row = lambda width: pl.BlockSpec((tall, width), lambda i: (i, 0))
    return pl.pallas_call(
        grad_kernel,
        grid=(4,),
        in_specs=[whole(lane.shape), row(features), whole(down_mat.shape), row(units), row(units)],
        out_specs=[row(units), row(units), row(LANES)],
        out_shape=[jax.ShapeDtypeStruct((total, units), BF)] * 2 + [jax.ShapeDtypeStruct((total, LANES), BF)],
        compiler_params=params(VMEM_MIB),
        cost_estimate=cost(2 * total * features * units, 2 * total * features + 2 * features * units + 12 * total * units),
        name="hidden_grads",
    )(lane, rows_grad, down_mat, pre_gate, pre_up)


def back_a_kernel(n_exp, pairs, table, grad_gate, grad_up, gate, up, gate_dot, *outs):
    wide = gate.shape[0]
    rows, half = outs[0].shape[0] // 2, outs[0].shape[1] - LANES
    size = table.shape[2]

    def reorder(values, start, width):
        before = None
        for i in range(pairs):
            moved = dot(table[i], values[size * i:size * (i + 1), :])
            for k in range(n_exp):
                part = moved[32 * k:32 * k + 16, :]
                if before is not None:
                    part = part + before[32 * k + 16:32 * k + 32, :]
                outs[k // 2][k % 2 * rows + 16 * i:k % 2 * rows + 16 * i + 16, pl.ds(start, width)] = part.astype(BF)
            before = moved
        for k in range(n_exp):
            part = before[32 * k + 16:32 * k + 32, :]
            outs[k // 2][k % 2 * rows + 16 * pairs:k % 2 * rows + 16 * pairs + 16, pl.ds(start, width)] = part.astype(BF)

    j = pl.program_id(0)
    values = dot_nt(grad_gate[...], gate[...]) + dot_nt(grad_up[...], up[...])
    reorder(values.astype(BF), pl.multiple_of(j * wide, wide), wide)

    @pl.when(j == 0)
    def _():
        reorder(gate_dot[...], half, LANES)


def returned_a(table, grad_gate, grad_up, gate_mat, up_mat, gate_dot, n_exp):
    total, units = grad_gate.shape
    half = gate_mat.shape[0] // 2
    pairs = table.shape[0]
    wide = 256 if half % 256 == 0 else half
    mat = pl.BlockSpec((wide, units), lambda j: (j, 0))
    block = (2 * total // n_exp, half + LANES)
    return pl.pallas_call(
        lambda *refs: back_a_kernel(n_exp, pairs, *refs),
        grid=(half // wide,),
        in_specs=[whole(table.shape, (0, 0, 0)), whole(grad_gate.shape), whole(grad_up.shape), mat, mat, whole(gate_dot.shape)],
        out_specs=[whole(block)] * (n_exp // 2),
        out_shape=[jax.ShapeDtypeStruct(block, BF)] * (n_exp // 2),
        compiler_params=params(VMEM_MIB),
        cost_estimate=cost(4 * total * half * units, 4 * half * units + 4 * total * units + 2 * total * half),
        name="returned_a",
    )(table, grad_gate, grad_up, gate_mat, up_mat, gate_dot)


def back_b_kernel(grad_gate, grad_up, gate, up, out):
    out[...] = (dot_nt(grad_gate[...], gate[...]) + dot_nt(grad_up[...], up[...])).astype(BF)


def returned_b(grad_gate, grad_up, gate_mat, up_mat):
    total, units = grad_gate.shape
    half = gate_mat.shape[0] // 2
    wide = 256 if half % 256 == 0 else half
    mat = pl.BlockSpec((wide, units), lambda j: (half // wide + j, 0))
    return pl.pallas_call(
        back_b_kernel,
        grid=(half // wide,),
        in_specs=[whole(grad_gate.shape), whole(grad_up.shape), mat, mat],
        out_specs=pl.BlockSpec((total, wide), lambda j: (0, j)),
        out_shape=jax.ShapeDtypeStruct((total, half), BF),
        compiler_params=params(VMEM_MIB),
        cost_estimate=cost(4 * total * half * units, 4 * half * units + 4 * total * units + 2 * total * half),
        name="returned_b",
    )(grad_gate, grad_up, gate_mat, up_mat)


def sum_kernel(chips, slot, weight, *refs):
    blocks, outs = refs[:chips], refs[chips:]
    half = outs[0].shape[1] - LANES
    rows = blocks[0].shape[0] // 2
    place = lax.broadcasted_iota(jnp.int32, (slot.shape[1], rows), 1).astype(F32)
    for side, out in enumerate(outs):
        sums = jnp.zeros((slot.shape[1], half), F32)
        gates = jnp.zeros((slot.shape[1], LANES), F32)
        for a in range(chips):
            hot = slot[side, :, 2 * a:2 * a + 1] == place
            block = blocks[a][rows * side:rows * (side + 1), :]
            sums += dot(jnp.where(hot, weight[side, :, 2 * a:2 * a + 1], 0.0).astype(BF), block[:, :half])
            gates += dot(jnp.where(hot, 1.0, 0.0).astype(BF), block[:, half:])
        out[:, :half] = sums.astype(out.dtype)
        out[:, half:] = gates.astype(out.dtype)


def group_sums(slot, weight, blocks):
    chips = len(blocks)
    shape = (slot.shape[1], blocks[0].shape[1])
    return pl.pallas_call(
        lambda *refs: sum_kernel(chips, *refs),
        grid=(1,),
        in_specs=[whole(slot.shape, (0, 0, 0)), whole(weight.shape, (0, 0, 0))] + [whole(blocks[0].shape)] * chips,
        out_specs=[whole(shape)] * 2,
        out_shape=[jax.ShapeDtypeStruct(shape, F32), jax.ShapeDtypeStruct(shape, BF)],
        compiler_params=params(VMEM_MIB),
        cost_estimate=cost(2 * shape[0] * blocks[0].size * chips, 2 * chips * blocks[0].size),
        name="group_sums",
    )(slot, weight, *blocks)


def named_here(top, eye, meta, local):
    flat = dot_nt(eye[...], meta)
    named = weight = jnp.zeros((local.shape[0], flat.shape[1]), F32)
    for k in range(top):
        hit = flat[k:k + 1, :] == local[:, 0:1]
        named += jnp.where(hit, 1.0, 0.0)
        weight += jnp.where(hit, flat[top + k:top + k + 1, :], 0.0)
    return named, weight


def hub_kernel(top, cap, eye, local, before, block, hub, other, *outs):
    *blocks, out_slot, out_weight = outs
    rows, features = blocks[0].shape[0] // 2, blocks[0].shape[1]
    for side, ref in enumerate((hub, other)):
        named, weight = named_here(top, eye, ref[:, features:], local)
        slot = jnp.where(named > 0.0, block[0:1, :] * cap + dot(named.astype(BF), before[...]), -1.0)
        out_slot[side], out_weight[side] = slot, weight
        place = lax.broadcasted_iota(jnp.int32, (rows, slot.shape[1]), 0).astype(F32)
        for a, out in enumerate(blocks):
            hot = jnp.where(place == slot[2 * a:2 * a + 1, :], 1.0, 0.0).astype(BF)
            out[rows * side:rows * (side + 1), :] = dot(hot, ref[:, :features]).astype(BF)


def lower_counts(total, size):
    at = jnp.arange(total)
    same = at[:, None] // size == at[None, :] // size
    return (same & (at[:, None] < at[None, :])).astype(BF), jnp.broadcast_to((at // size).astype(F32), (8, total))


def hub_blocks(hub, other, local, per_group, top, cap):
    n_rows, width = hub.shape
    n_exp = local.shape[0]
    before, block = lower_counts(n_rows, per_group)
    shape = (2 * (n_rows // per_group) * cap, width - LANES)
    pair = (2, n_exp, n_rows)
    eye = jnp.eye(LANES, dtype=BF)
    *blocks, slot, weight = pl.pallas_call(
        lambda *refs: hub_kernel(top, cap, *refs),
        grid=(1,),
        in_specs=[whole(x.shape) for x in (eye, local, before, block, hub, other)],
        out_specs=[whole(shape)] * (n_exp // 2) + [whole(pair, (0, 0, 0))] * 2,
        out_shape=[jax.ShapeDtypeStruct(shape, BF)] * (n_exp // 2) + [jax.ShapeDtypeStruct(pair, F32)] * 2,
        compiler_params=params(VMEM_MIB),
        cost_estimate=cost(shape[0] * n_exp * n_rows * width, n_exp * shape[0] * shape[1]),
        name="hub_blocks",
    )(eye, local, before, block, hub, other)
    return blocks, slot.transpose(0, 2, 1), weight.transpose(0, 2, 1)


def slots_kernel(top, n_exp, cap, member, eye, theirs, before, start, spread, place, meta, out_hot, out_slot, out_weight):
    n_tok = before.shape[0]
    parts = [meta[pl.ds(pl.multiple_of((member[0] ^ k) * n_tok, n_tok), n_tok), :] for k in range(n_exp)]
    named, out_weight[...] = named_here(top, eye, jnp.concatenate(parts, axis=0), theirs)
    counts = [dot(named[:, at:at + n_tok].astype(BF), before[...]) for at in range(0, named.shape[1], n_tok)]
    rank = jnp.concatenate(counts, axis=1)
    out_slot[...] = jnp.where(named > 0.0, start[0:1, :] + rank, -1.0)
    rank = jnp.where(named > 0.0, rank, -1.0).astype(BF)
    size = spread.shape[0]
    for k in range(n_exp):
        hot = dot(spread[...], rank[:, n_tok * k:n_tok * (k + 1)]) == place[:, 0:1]
        out_hot[size * k:size * (k + 1), :] = jnp.where(hot, 1.0, 0.0).astype(BF)


def column_slots(meta, theirs, member, n_tok, top, cap):
    total = meta.shape[0]
    n_seq, n_exp = theirs.shape[0], total // n_tok
    before, block = lower_counts(n_tok, n_tok)
    start = jnp.broadcast_to((jnp.arange(total) // n_tok * cap).astype(F32), (8, total))
    at = jnp.arange(n_seq * cap)
    spread = (at[:, None] // cap == jnp.arange(n_seq)[None, :]).astype(BF)
    place = jnp.broadcast_to((at % cap).astype(F32)[:, None], (n_seq * cap, LANES))
    eye = jnp.eye(LANES, dtype=BF)
    shapes = (n_seq * n_exp * cap, n_tok), (n_seq, total), (n_seq, total)
    inputs = (eye, theirs, before, start, spread, place, meta)
    hot, slot, weight = pl.pallas_call(
        lambda *refs: slots_kernel(top, n_exp, cap, *refs),
        grid=(1,),
        in_specs=[pl.BlockSpec(memory_space=pltpu.SMEM)] + [whole(x.shape) for x in inputs],
        out_specs=[whole(shape) for shape in shapes],
        out_shape=[jax.ShapeDtypeStruct(shape, kind) for shape, kind in zip(shapes, (BF, F32, F32))],
        compiler_params=params(VMEM_MIB),
        cost_estimate=cost(4 * total * LANES * LANES, 2 * shapes[0][0] * n_tok),
        name="column_slots",
    )(member.reshape(1), *inputs)
    return hot, slot.T, weight.T


def rows_kernel(n_exp, member, table, hot, column, out):
    pairs, size = table.shape[:2]
    n_tok = hot.shape[1]
    blocks = []
    for k in range(n_exp):
        rows = pl.ds(pl.multiple_of((member[0] ^ k) * n_tok, n_tok), n_tok)
        blocks.append(dot(hot[size * k:size * (k + 1), :], column[rows, :]).astype(BF))
    for i in range(pairs):
        window = jnp.concatenate([b[16 * i:16 * i + 32, :] for b in blocks], axis=0)
        out[size * i:size * (i + 1), :] = dot(table[i], window).astype(BF)


def column_rows(member, table, hot, column, n_exp):
    total, features = hot.shape[0], column.shape[1]
    wide = 512 if features % 512 == 0 else features
    return pl.pallas_call(
        lambda *refs: rows_kernel(n_exp, *refs),
        grid=(features // wide,),
        in_specs=[pl.BlockSpec(memory_space=pltpu.SMEM), whole(table.shape, (0, 0, 0)), whole(hot.shape),
                  pl.BlockSpec((column.shape[0], wide), lambda j: (0, j))],
        out_specs=pl.BlockSpec((total, wide), lambda j: (0, j)),
        out_shape=jax.ShapeDtypeStruct((total, features), BF),
        compiler_params=params(VMEM_MIB),
        cost_estimate=cost(2 * total * (hot.shape[1] + table.shape[2]) * features, 2 * column.size + 2 * total * features),
        name="column_rows",
    )(member.reshape(1), table, hot, column)


def column_kernel(n_exp, place, spread, slot, weight, got, out_mine, out_other, mixed):
    n_tok = out_mine.shape[0] // (n_exp // 2)
    mixed[...] = jnp.where(dot(slot[...], spread[...]) == place[0:1, :], dot(weight[...], spread[...]), 0.0).astype(BF)
    half = got.shape[1]
    wide = 256 if half % 256 == 0 else half
    for start in range(0, half, wide):
        sums = dot(mixed[...], got[:, start:start + wide])
        for k in range(0, n_exp, 2):
            at = slice(n_tok * k // 2, n_tok * (k // 2 + 1))
            out_mine[at, start:start + wide] = sums[n_tok * k:n_tok * (k + 1), :]
            out_other[at, start:start + wide] = sums[n_tok * (k + 1):n_tok * (k + 2), :].astype(BF)


def column_sums(slot, weight, got, n_exp):
    n_rows, n_seq = slot.shape
    total, half = got.shape
    at = jnp.arange(total)
    place = jnp.broadcast_to((at % (total // n_seq)).astype(F32), (8, total))
    spread = (jnp.arange(n_seq)[:, None] == at[None, :] // (total // n_seq)).astype(BF)
    shape = (n_rows // 2, half)
    return pl.pallas_call(
        lambda *refs: column_kernel(n_exp, *refs),
        grid=(1,),
        in_specs=[whole(place.shape), whole(spread.shape), whole(slot.shape), whole(weight.shape), whole(got.shape)],
        out_specs=[whole(shape)] * 2,
        out_shape=[jax.ShapeDtypeStruct(shape, F32), jax.ShapeDtypeStruct(shape, BF)],
        scratch_shapes=[pltpu.VMEM((n_rows, total), BF)],
        compiler_params=params(VMEM_MIB),
        cost_estimate=cost(40 * n_rows * total * half, 2 * total * half + 3 * n_rows * half),
        name="column_sums",
    )(place, spread, slot.astype(BF), weight.astype(BF), got)


def per_device(hidden_in, grad_out, expert_ids, gate_weights, w_gate, w_up, w_down):
    n_tok, features = hidden_in.shape
    top = expert_ids.shape[1]
    n_seq, n_exp = lax.axis_size("seq"), lax.axis_size("exp")
    group, member = lax.axis_index("seq"), lax.axis_index("exp")
    experts = n_seq * n_exp
    cap = 3 * top * n_tok // (2 * experts)
    per_group = top // 2 * n_tok // n_seq
    half = features // 2
    gate_mat, up_mat, down_mat = w_gate[0], w_up[0], w_down[0]
    partner = member ^ jnp.arange(n_exp)
    to_b, to_a = window_tables(n_seq, n_exp, cap)

    meta = jnp.concatenate(
        (expert_ids.astype(BF), gate_weights.astype(BF), jnp.zeros((n_tok, LANES - 2 * top), BF)), axis=1)

    column_meta = lax.all_gather(meta, "exp", axis=0, tiled=True)
    column = lax.all_gather(grad_out, "exp", axis=0, tiled=True)
    theirs = jnp.broadcast_to((jnp.arange(n_seq) * n_exp + member).astype(F32)[:, None], (n_seq, LANES))
    put_b, slot_b, weight_b = column_slots(column_meta, theirs, member, n_tok, top, cap)

    group_ids = expert_ids // n_exp
    in_group = jnp.any(group_ids[:, :, None] == jnp.arange(n_seq)[None, None, :], axis=1)
    group_rank = earlier_counts(in_group).T
    pick = (group_rank[:, None, :] == jnp.arange(per_group, dtype=F32)[None, :, None])
    pick = pick.astype(BF).reshape(n_seq * per_group, n_tok)
    send = dot(pick, jnp.concatenate((hidden_in, meta), axis=1)).astype(BF)
    hub = lax.all_to_all(send.reshape(n_seq, per_group, features + LANES), "seq", 0, 0, tiled=True)
    hub = hub.reshape(n_seq * per_group, features + LANES)

    send_b = column_rows(member, to_b, put_b, column, n_exp)
    rows_b = n_exp * cap
    recv_b = lax.all_to_all(send_b.reshape(n_seq, rows_b, features), "seq", 0, 0, tiled=True)
    recv_b = recv_b.reshape(n_seq * rows_b, features)

    local = jnp.broadcast_to((partner + group * n_exp).astype(F32)[:, None], (n_exp, LANES))
    blocks, slot_a, weight_a = hub_blocks(hub, swap(hub, 1), local, per_group, top, cap)
    rows_in = exchange(blocks)

    pre_gate, pre_up = pre_products(to_b, rows_in, gate_mat, up_mat)
    lane = jnp.broadcast_to((jnp.arange(LANES) == group * n_exp + member).astype(F32), (8, LANES))
    grad_gate, grad_up, gate_dot = hidden_grads(lane, recv_b, down_mat, pre_gate, pre_up)

    back_a = returned_a(to_a, grad_gate, grad_up, gate_mat, up_mat, gate_dot, n_exp)
    got_a = exchange(back_a)
    back_b = returned_b(grad_gate, grad_up, gate_mat, up_mat)
    got_b = lax.all_to_all(back_b.reshape(n_seq, rows_b, half), "seq", 0, 0, tiled=True)
    got_b, *_ = barrier(got_b, *back_a)
    mine, other = column_sums(slot_b, weight_b, got_b.reshape(n_seq * rows_b, half), n_exp)
    other, slot_a = barrier(other, slot_a)
    chip = (mine + swap(other, 1).astype(F32)).astype(BF).reshape(n_exp // 2, n_tok, half)
    final_b = sum(p.astype(F32) for p in exchange(list(chip)))
    mine, other = group_sums(slot_a, weight_a, got_a)
    back = (mine + swap(other, 1).astype(F32)).astype(BF)
    back = lax.all_to_all(back.reshape(n_seq, per_group, half + LANES), "seq", 0, 0, tiled=True)
    final_a = dot_t(pick, back.reshape(n_seq * per_group, half + LANES))

    grad_in = jnp.concatenate((final_a[:, :half], final_b), axis=1).astype(BF)
    table = final_a[:, half:]
    chosen = expert_ids[:, :, None] == jnp.arange(experts)[None, None, :]
    grad_gates = jnp.sum(jnp.where(chosen, table[:, None, :experts], 0.0), axis=2).astype(BF)
    return grad_in, grad_gates


def solution(mesh):
    rows, mats = P(("seq", "exp"), None), P(("seq", "exp"), None, None)
    return jax.shard_map(
        per_device, mesh=mesh, in_specs=(rows,) * 4 + (mats,) * 3, out_specs=(rows, rows), check_vma=False
    )
```

```python
import jax
import jax.numpy as jnp
from jax import lax
from jax.experimental import pallas as pl
from jax.experimental.pallas import tpu as pltpu
from jax.sharding import PartitionSpec as P

BF = jnp.bfloat16
F32 = jnp.float32
LANES = 128
VMEM_MIB = 60


def dot(a, b):
    return jnp.dot(a, b, preferred_element_type=F32)


def dot_t(a, b):
    return lax.dot_general(a, b, (((0,), (0,)), ((), ())), preferred_element_type=F32)


def dot_nt(a, b):
    return lax.dot_general(a, b, (((1,), (1,)), ((), ())), preferred_element_type=F32)


def earlier_counts(names):
    n = names.shape[-2]
    lower = (jnp.arange(n)[:, None] > jnp.arange(n)[None, :]).astype(BF)
    counts = jnp.einsum("ij,...jm->...im", lower, names.astype(BF), preferred_element_type=F32)
    return jnp.where(names, counts, -1.0)


def barrier(*values):
    return lax.optimization_barrier(values)


def swap(x, k):
    return lax.ppermute(x, "exp", [(i, i ^ k) for i in range(lax.axis_size("exp"))])


def exchange(blocks):
    return [blocks[0]] + [swap(block, 2 * a) for a, block in enumerate(blocks) if a]


def whole(shape, at=(0, 0)):
    return pl.BlockSpec(shape, lambda *_: at, pipeline_mode=pl.Buffered(1))


def params(mib):
    return pltpu.CompilerParams(vmem_limit_bytes=mib * 2**20)


def cost(flops, nbytes):
    return pl.CostEstimate(flops=flops, bytes_accessed=nbytes, transcendentals=0)


def window_tables(n_seq, n_exp, cap):
    pair = 2 * n_exp * cap
    d = jnp.arange(pair)
    source = d % (n_exp * cap) // cap * 32 + d // (n_exp * cap) * cap + d % cap
    i = jnp.arange(n_seq // 2)
    at = source[None, :] + (2 * cap - 16) * i[:, None]
    wide = jnp.arange(32 * n_exp)
    to_b = (at[:, :, None] == wide[None, None, :]).astype(BF)
    to_a = (at[:, None, :] == wide[None, :, None]).astype(BF)
    return to_b, to_a


def pre_kernel(chips, pairs, table, *refs):
    blocks, (gate, up, out_gate, out_up, rows) = refs[:chips], refs[chips:]
    size = table.shape[1]

    @pl.when(pl.program_id(0) == 0)
    def _():
        for i in range(pairs):
            at = [(b, 16 * i + side) for b in blocks for side in (0, b.shape[0] // 2)]
            window = jnp.concatenate([b[start:start + 32, :] for b, start in at], axis=0)
            rows[size * i:size * (i + 1), :] = dot(table[i], window).astype(BF)

    out_gate[...] = dot(rows[...], gate[...])
    out_up[...] = dot(rows[...], up[...])


def pre_products(table, blocks, gate_mat, up_mat):
    chips, pairs = len(blocks), table.shape[0]
    rows, features = blocks[0].shape
    total, units = rows * chips, gate_mat.shape[1]
    wide = 256 if units % 256 == 0 else units
    column = pl.BlockSpec((features, wide), lambda j: (0, j))
    result = pl.BlockSpec((total, wide), lambda j: (0, j))
    return pl.pallas_call(
        lambda *refs: pre_kernel(chips, pairs, *refs),
        grid=(units // wide,),
        in_specs=[whole(table.shape, (0, 0, 0))] + [whole((rows, features))] * chips + [column, column],
        out_specs=[result, result],
        out_shape=[jax.ShapeDtypeStruct((total, units), F32)] * 2,
        scratch_shapes=[pltpu.VMEM((total, features), BF)],
        compiler_params=params(VMEM_MIB),
        cost_estimate=cost(40 * total * features * units, 2 * total * features + 4 * features * units + 8 * total * units),
        name="pre_products",
    )(table, *blocks, gate_mat, up_mat)


def grad_kernel(lane, grad, down, pre_gate, pre_up, out_gate, out_up, out_dot):
    grad_hidden = dot_nt(grad[...], down[...])
    gate, up = pre_gate[...], pre_up[...]
    sigmoid = jax.nn.sigmoid(gate)
    active = gate * sigmoid
    hidden = (active * up).astype(BF).astype(F32)
    gate_dot = jnp.sum(hidden * grad_hidden, axis=1, keepdims=True)
    out_dot[...] = (gate_dot * lane[0:1, :]).astype(BF)
    out_gate[...] = (grad_hidden * up * sigmoid * (1.0 + gate * (1.0 - sigmoid))).astype(BF)
    out_up[...] = (grad_hidden * active).astype(BF)


def hidden_grads(lane, rows_grad, down_mat, pre_gate, pre_up):
    total, features = rows_grad.shape
    units = down_mat.shape[0]
    tall = total // 4
    row = lambda width: pl.BlockSpec((tall, width), lambda i: (i, 0))
    return pl.pallas_call(
        grad_kernel,
        grid=(4,),
        in_specs=[whole(lane.shape), row(features), whole(down_mat.shape), row(units), row(units)],
        out_specs=[row(units), row(units), row(LANES)],
        out_shape=[jax.ShapeDtypeStruct((total, units), BF)] * 2 + [jax.ShapeDtypeStruct((total, LANES), BF)],
        compiler_params=params(VMEM_MIB),
        cost_estimate=cost(2 * total * features * units, 2 * total * features + 2 * features * units + 12 * total * units),
        name="hidden_grads",
    )(lane, rows_grad, down_mat, pre_gate, pre_up)


def back_a_kernel(n_exp, pairs, table, grad_gate, grad_up, gate, up, gate_dot, *outs):
    wide = gate.shape[0]
    rows, half = outs[0].shape[0] // 2, outs[0].shape[1] - LANES
    size = table.shape[2]

    def reorder(values, start, width):
        before = None
        for i in range(pairs):
            moved = dot(table[i], values[size * i:size * (i + 1), :])
            for k in range(n_exp):
                part = moved[32 * k:32 * k + 16, :]
                if before is not None:
                    part = part + before[32 * k + 16:32 * k + 32, :]
                outs[k // 2][k % 2 * rows + 16 * i:k % 2 * rows + 16 * i + 16, pl.ds(start, width)] = part.astype(BF)
            before = moved
        for k in range(n_exp):
            part = before[32 * k + 16:32 * k + 32, :]
            outs[k // 2][k % 2 * rows + 16 * pairs:k % 2 * rows + 16 * pairs + 16, pl.ds(start, width)] = part.astype(BF)

    j = pl.program_id(0)
    values = dot_nt(grad_gate[...], gate[...]) + dot_nt(grad_up[...], up[...])
    reorder(values.astype(BF), pl.multiple_of(j * wide, wide), wide)

    @pl.when(j == 0)
    def _():
        reorder(gate_dot[...], half, LANES)


def returned_a(table, grad_gate, grad_up, gate_mat, up_mat, gate_dot, n_exp):
    total, units = grad_gate.shape
    half = gate_mat.shape[0] // 2
    pairs = table.shape[0]
    wide = 256 if half % 256 == 0 else half
    mat = pl.BlockSpec((wide, units), lambda j: (j, 0))
    block = (2 * total // n_exp, half + LANES)
    return pl.pallas_call(
        lambda *refs: back_a_kernel(n_exp, pairs, *refs),
        grid=(half // wide,),
        in_specs=[whole(table.shape, (0, 0, 0)), whole(grad_gate.shape), whole(grad_up.shape), mat, mat, whole(gate_dot.shape)],
        out_specs=[whole(block)] * (n_exp // 2),
        out_shape=[jax.ShapeDtypeStruct(block, BF)] * (n_exp // 2),
        compiler_params=params(VMEM_MIB),
        cost_estimate=cost(4 * total * half * units, 4 * half * units + 4 * total * units + 2 * total * half),
        name="returned_a",
    )(table, grad_gate, grad_up, gate_mat, up_mat, gate_dot)


def back_b_kernel(grad_gate, grad_up, gate, up, out):
    out[...] = (dot_nt(grad_gate[...], gate[...]) + dot_nt(grad_up[...], up[...])).astype(BF)


def returned_b(grad_gate, grad_up, gate_mat, up_mat):
    total, units = grad_gate.shape
    half = gate_mat.shape[0] // 2
    wide = 256 if half % 256 == 0 else half
    mat = pl.BlockSpec((wide, units), lambda j: (half // wide + j, 0))
    return pl.pallas_call(
        back_b_kernel,
        grid=(half // wide,),
        in_specs=[whole(grad_gate.shape), whole(grad_up.shape), mat, mat],
        out_specs=pl.BlockSpec((total, wide), lambda j: (0, j)),
        out_shape=jax.ShapeDtypeStruct((total, half), BF),
        compiler_params=params(VMEM_MIB),
        cost_estimate=cost(4 * total * half * units, 4 * half * units + 4 * total * units + 2 * total * half),
        name="returned_b",
    )(grad_gate, grad_up, gate_mat, up_mat)


def sum_kernel(chips, slot, weight, mine, first, last, *refs):
    blocks, outs, column = refs[:chips], refs[chips:chips + 2], refs[chips + 2:]
    n_tok = column[0].shape[0]
    for a, out in enumerate(column):
        half, at = (first, a) if 2 * a < chips else (last, a - chips // 2)
        other = half[n_tok * at:n_tok * (at + 1), :].astype(F32)
        out[...] = (mine[n_tok * a:n_tok * (a + 1), :] + other).astype(BF)
    half = outs[0].shape[1] - LANES
    rows = blocks[0].shape[0] // 2
    place = lax.broadcasted_iota(jnp.int32, (slot.shape[1], rows), 1).astype(F32)
    for side, out in enumerate(outs):
        sums = jnp.zeros((slot.shape[1], half), F32)
        gates = jnp.zeros((slot.shape[1], LANES), F32)
        for a in range(chips):
            hot = slot[side, :, 2 * a:2 * a + 1] == place
            block = blocks[a][rows * side:rows * (side + 1), :]
            sums += dot(jnp.where(hot, weight[side, :, 2 * a:2 * a + 1], 0.0).astype(BF), block[:, :half])
            gates += dot(jnp.where(hot, 1.0, 0.0).astype(BF), block[:, half:])
        out[:, :half] = sums.astype(out.dtype)
        out[:, half:] = gates.astype(out.dtype)


def group_sums(slot, weight, mine, first, last, blocks):
    chips = len(blocks)
    shape = (slot.shape[1], blocks[0].shape[1])
    column = (mine.shape[0] // chips, mine.shape[1])
    return pl.pallas_call(
        lambda *refs: sum_kernel(chips, *refs),
        grid=(1,),
        in_specs=[whole(slot.shape, (0, 0, 0)), whole(weight.shape, (0, 0, 0))]
        + [whole(x.shape) for x in (mine, first, last)] + [whole(blocks[0].shape)] * chips,
        out_specs=[whole(shape)] * 2 + [whole(column)] * chips,
        out_shape=[jax.ShapeDtypeStruct(shape, F32), jax.ShapeDtypeStruct(shape, BF)]
        + [jax.ShapeDtypeStruct(column, BF)] * chips,
        compiler_params=params(VMEM_MIB),
        cost_estimate=cost(2 * shape[0] * blocks[0].size * chips, 2 * chips * blocks[0].size),
        name="group_sums",
    )(slot, weight, mine, first, last, *blocks)


def named_here(top, eye, meta, local):
    flat = dot_nt(eye[...], meta)
    named = weight = jnp.zeros((local.shape[0], flat.shape[1]), F32)
    for k in range(top):
        hit = flat[k:k + 1, :] == local[:, 0:1]
        named += jnp.where(hit, 1.0, 0.0)
        weight += jnp.where(hit, flat[top + k:top + k + 1, :], 0.0)
    return named, weight


def hub_kernel(top, cap, eye, local, before, block, meta, other_meta, hub, other, *outs):
    *blocks, out_slot, out_weight, puts = outs
    rows = blocks[0].shape[0] // 2
    n_rows = hub.shape[0]

    @pl.when(pl.program_id(0) == 0)
    def _():
        for side, ref in enumerate((meta, other_meta)):
            named, weight = named_here(top, eye, ref[...], local)
            slot = jnp.where(named > 0.0, block[0:1, :] * cap + dot(named.astype(BF), before[...]), -1.0)
            out_slot[side], out_weight[side] = slot, weight
            place = lax.broadcasted_iota(jnp.int32, (rows, n_rows), 0).astype(F32)
            for a in range(len(blocks)):
                hot = jnp.where(place == slot[2 * a:2 * a + 1, :], 1.0, 0.0).astype(BF)
                puts[side, rows * a:rows * (a + 1), :] = hot

    for side, ref in enumerate((hub, other)):
        placed = dot(puts[side], ref[...]).astype(BF)
        for a, out in enumerate(blocks):
            out[rows * side:rows * (side + 1), :] = placed[rows * a:rows * (a + 1), :]


def lower_counts(total, size):
    at = jnp.arange(total)
    same = at[:, None] // size == at[None, :] // size
    return (same & (at[:, None] < at[None, :])).astype(BF), jnp.broadcast_to((at // size).astype(F32), (8, total))


def hub_blocks(hub, other, local, per_group, top, cap):
    n_rows, width = hub.shape
    n_exp = local.shape[0]
    before, block = lower_counts(n_rows, per_group)
    shape = (2 * (n_rows // per_group) * cap, width - LANES)
    pair = (2, n_exp, n_rows)
    eye = jnp.eye(LANES, dtype=BF)
    features, chips = width - LANES, n_exp // 2
    wide = 512 if features % 512 == 0 else features
    lanes = whole((n_rows, LANES), (0, width // LANES - 1))
    part = pl.BlockSpec((n_rows, wide), lambda j: (0, j))
    *blocks, slot, weight = pl.pallas_call(
        lambda *refs: hub_kernel(top, cap, *refs),
        grid=(features // wide,),
        in_specs=[whole(x.shape) for x in (eye, local, before, block)] + [lanes, lanes, part, part],
        out_specs=[pl.BlockSpec((shape[0], wide), lambda j: (0, j))] * chips + [whole(pair, (0, 0, 0))] * 2,
        out_shape=[jax.ShapeDtypeStruct(shape, BF)] * chips + [jax.ShapeDtypeStruct(pair, F32)] * 2,
        scratch_shapes=[pltpu.VMEM((2, shape[0] // 2 * chips, n_rows), BF)],
        compiler_params=params(VMEM_MIB),
        cost_estimate=cost(shape[0] * n_exp * n_rows * width, n_exp * shape[0] * shape[1]),
        name="hub_blocks",
    )(eye, local, before, block, hub, other, hub, other)
    return blocks, slot.transpose(0, 2, 1), weight.transpose(0, 2, 1)


def column_block(k, member, n_tok, mine, other):
    rows = pl.ds(pl.multiple_of((member[0] ^ k) // 2 * n_tok, n_tok), n_tok)
    return other[k // 2][...] if k % 2 else mine[rows, :]


def slots_kernel(top, n_exp, cap, member, eye, theirs, before, start, spread, place, meta, *refs):
    *other, out_hot, out_slot, out_weight = refs
    n_tok = before.shape[0]
    parts = [column_block(k, member, n_tok, meta, other) for k in range(n_exp)]
    named, out_weight[...] = named_here(top, eye, jnp.concatenate(parts, axis=0), theirs)
    counts = [dot(named[:, at:at + n_tok].astype(BF), before[...]) for at in range(0, named.shape[1], n_tok)]
    rank = jnp.concatenate(counts, axis=1)
    out_slot[...] = jnp.where(named > 0.0, start[0:1, :] + rank, -1.0)
    rank = jnp.where(named > 0.0, rank, -1.0).astype(BF)
    size = spread.shape[0]
    for k in range(n_exp):
        hot = dot(spread[...], rank[:, n_tok * k:n_tok * (k + 1)]) == place[:, 0:1]
        out_hot[size * k:size * (k + 1), :] = jnp.where(hot, 1.0, 0.0).astype(BF)


def column_slots(mine, other, theirs, member, n_tok, top, cap):
    total, last = 2 * mine.shape[0], mine.shape[1] // LANES - 1
    n_seq, n_exp = theirs.shape[0], total // n_tok
    lanes = whole((total // 2, LANES), (0, last))
    before, block = lower_counts(n_tok, n_tok)
    start = jnp.broadcast_to((jnp.arange(total) // n_tok * cap).astype(F32), (8, total))
    at = jnp.arange(n_seq * cap)
    spread = (at[:, None] // cap == jnp.arange(n_seq)[None, :]).astype(BF)
    place = jnp.broadcast_to((at % cap).astype(F32)[:, None], (n_seq * cap, LANES))
    eye = jnp.eye(LANES, dtype=BF)
    shapes = (n_seq * n_exp * cap, n_tok), (n_seq, total), (n_seq, total)
    inputs = (eye, theirs, before, start, spread, place)
    hot, slot, weight = pl.pallas_call(
        lambda *refs: slots_kernel(top, n_exp, cap, *refs),
        grid=(1,),
        in_specs=[pl.BlockSpec(memory_space=pltpu.SMEM)] + [whole(x.shape) for x in inputs] + [lanes] + [whole((n_tok, LANES), (0, last))] * len(other),
        out_specs=[whole(shape) for shape in shapes],
        out_shape=[jax.ShapeDtypeStruct(shape, kind) for shape, kind in zip(shapes, (BF, F32, F32))],
        compiler_params=params(VMEM_MIB),
        cost_estimate=cost(4 * total * LANES * LANES, 2 * shapes[0][0] * n_tok),
        name="column_slots",
    )(member.reshape(1), *inputs, mine, *other)
    return hot, slot.T, weight.T


def rows_kernel(n_exp, member, table, hot, mine, *refs):
    *other, out = refs
    pairs, size = table.shape[:2]
    n_tok = hot.shape[1]
    blocks = []
    for k in range(n_exp):
        blocks.append(dot(hot[size * k:size * (k + 1), :], column_block(k, member, n_tok, mine, other)).astype(BF))
    for i in range(pairs):
        window = jnp.concatenate([b[16 * i:16 * i + 32, :] for b in blocks], axis=0)
        out[size * i:size * (i + 1), :] = dot(table[i], window).astype(BF)


def column_rows(member, table, hot, mine, other, n_exp):
    total, features = hot.shape[0], mine.shape[1] - LANES
    wide = 512 if features % 512 == 0 else features
    part = lambda rows: pl.BlockSpec((rows, wide), lambda j: (0, j))
    return pl.pallas_call(
        lambda *refs: rows_kernel(n_exp, *refs),
        grid=(features // wide,),
        in_specs=[pl.BlockSpec(memory_space=pltpu.SMEM), whole(table.shape, (0, 0, 0)), whole(hot.shape),
                  part(mine.shape[0])] + [part(hot.shape[1])] * len(other),
        out_specs=part(total),
        out_shape=jax.ShapeDtypeStruct((total, features), BF),
        compiler_params=params(VMEM_MIB),
        cost_estimate=cost(2 * total * hot.shape[1] * LANES, 2 * total * LANES),
        name="column_rows",
    )(member.reshape(1), table, hot, mine, *other)


def column_kernel(n_exp, place, spread, slot, weight, got, out_mine, out_first, out_last, mixed):
    n_tok = out_mine.shape[0] // (n_exp // 2)

    @pl.when(pl.program_id(0) == 0)
    def _():
        hot = dot(slot[...], spread[...]) == place[0:1, :]
        mixed[...] = jnp.where(hot, dot(weight[...], spread[...]), 0.0).astype(BF)

    sums = dot(mixed[...], got[...])
    for k in range(0, n_exp, 2):
        at = slice(n_tok * k // 2, n_tok * (k // 2 + 1))
        out_mine[at, :] = sums[n_tok * k:n_tok * (k + 1), :]
        out, at = (out_first, k) if 2 * k < n_exp else (out_last, k - n_exp // 2)
        out[n_tok * at // 2:n_tok * (at // 2 + 1), :] = sums[n_tok * (k + 1):n_tok * (k + 2), :].astype(BF)


def column_sums(slot, weight, got, n_exp):
    n_rows, n_seq = slot.shape
    total, half = got.shape
    at = jnp.arange(total)
    place = jnp.broadcast_to((at % (total // n_seq)).astype(F32), (8, total))
    spread = (jnp.arange(n_seq)[:, None] == at[None, :] // (total // n_seq)).astype(BF)
    shape = (n_rows // 2, half)
    wide = 256 if half % 256 == 0 else half
    part = lambda rows: pl.BlockSpec((rows, wide), lambda j: (0, j))
    return pl.pallas_call(
        lambda *refs: column_kernel(n_exp, *refs),
        grid=(half // wide,),
        in_specs=[whole(place.shape), whole(spread.shape), whole(slot.shape), whole(weight.shape), part(total)],
        out_specs=[part(shape[0])] + [part(shape[0] // 2)] * 2,
        out_shape=[jax.ShapeDtypeStruct(shape, F32)] + [jax.ShapeDtypeStruct((shape[0] // 2, half), BF)] * 2,
        scratch_shapes=[pltpu.VMEM((n_rows, total), BF)],
        compiler_params=params(VMEM_MIB),
        cost_estimate=cost(400 * n_rows * total * half, 2 * total * half + 3 * n_rows * half),
        name="column_sums",
    )(place, spread, slot.astype(BF), weight.astype(BF), got)


def per_device(hidden_in, grad_out, expert_ids, gate_weights, w_gate, w_up, w_down):
    n_tok, features = hidden_in.shape
    top = expert_ids.shape[1]
    n_seq, n_exp = lax.axis_size("seq"), lax.axis_size("exp")
    group, member = lax.axis_index("seq"), lax.axis_index("exp")
    experts = n_seq * n_exp
    cap = 3 * top * n_tok // (2 * experts)
    per_group = top // 2 * n_tok // n_seq
    half = features // 2
    gate_mat, up_mat, down_mat = w_gate[0], w_up[0], w_down[0]
    partner = member ^ jnp.arange(n_exp)
    to_b, to_a = window_tables(n_seq, n_exp, cap)

    meta = jnp.concatenate(
        (expert_ids.astype(BF), gate_weights.astype(BF), jnp.zeros((n_tok, LANES - 2 * top), BF)), axis=1)

    places = [list(range(c, n_exp, 2)) for c in range(2)]
    column = lax.all_gather(jnp.concatenate((grad_out, meta), axis=1), "exp", axis_index_groups=places, axis=0, tiled=True)
    other_column = [
        swap(lax.dynamic_slice_in_dim(column, (member // 2 ^ a) * n_tok, n_tok, 0), 1) for a in range(n_exp // 2)]
    theirs = jnp.broadcast_to((jnp.arange(n_seq) * n_exp + member).astype(F32)[:, None], (n_seq, LANES))
    put_b, slot_b, weight_b = column_slots(column, other_column, theirs, member, n_tok, top, cap)
    send_b = column_rows(member, to_b, put_b, column, other_column, n_exp)

    group_ids = expert_ids // n_exp
    in_group = jnp.any(group_ids[:, :, None] == jnp.arange(n_seq)[None, None, :], axis=1)
    group_rank = earlier_counts(in_group).T
    pick = (group_rank[:, None, :] == jnp.arange(per_group, dtype=F32)[None, :, None])
    pick = pick.astype(BF).reshape(n_seq * per_group, n_tok)
    send = dot(pick, jnp.concatenate((hidden_in, meta), axis=1)).astype(BF)
    hub = lax.all_to_all(send.reshape(n_seq, per_group, features + LANES), "seq", 0, 0, tiled=True)
    hub = hub.reshape(n_seq * per_group, features + LANES)
    hub, send_b = barrier(hub, send_b)

    rows_b = n_exp * cap
    recv_b = lax.all_to_all(send_b.reshape(n_seq, rows_b, features), "seq", 0, 0, tiled=True)
    recv_b = recv_b.reshape(n_seq * rows_b, features)

    local = jnp.broadcast_to((partner + group * n_exp).astype(F32)[:, None], (n_exp, LANES))
    blocks, slot_a, weight_a = hub_blocks(hub, swap(hub, 1), local, per_group, top, cap)
    rows_in = exchange(blocks)

    pre_gate, pre_up = pre_products(to_b, rows_in, gate_mat, up_mat)
    lane = jnp.broadcast_to((jnp.arange(LANES) == group * n_exp + member).astype(F32), (8, LANES))
    grad_gate, grad_up, gate_dot = hidden_grads(lane, recv_b, down_mat, pre_gate, pre_up)

    back_a = returned_a(to_a, grad_gate, grad_up, gate_mat, up_mat, gate_dot, n_exp)
    got_a = exchange(back_a)
    back_b = returned_b(grad_gate, grad_up, gate_mat, up_mat)
    got_b = lax.all_to_all(back_b.reshape(n_seq, rows_b, half), "seq", 0, 0, tiled=True)
    got_b, *_ = barrier(got_b, *back_a)
    mine, *other = column_sums(slot_b, weight_b, got_b.reshape(n_seq * rows_b, half), n_exp)
    mine, other, *chip = group_sums(slot_a, weight_a, mine, *(swap(x, 1) for x in other), got_a)
    final_b = sum(p.astype(F32) for p in exchange(chip))
    back = (mine + swap(other, 1).astype(F32)).astype(BF)
    back = lax.all_to_all(back.reshape(n_seq, per_group, half + LANES), "seq", 0, 0, tiled=True)
    final_a = dot_t(pick, back.reshape(n_seq * per_group, half + LANES))

    grad_in = jnp.concatenate((final_a[:, :half], final_b), axis=1).astype(BF)
    table = final_a[:, half:]
    chosen = expert_ids[:, :, None] == jnp.arange(experts)[None, None, :]
    grad_gates = jnp.sum(jnp.where(chosen, table[:, None, :experts], 0.0), axis=2).astype(BF)
    return grad_in, grad_gates


def solution(mesh):
    rows, mats = P(("seq", "exp"), None), P(("seq", "exp"), None, None)
    return jax.shard_map(
        per_device, mesh=mesh, in_specs=(rows,) * 4 + (mats,) * 3, out_specs=(rows, rows), check_vma=False
    )
```

```python
import jax
import jax.numpy as jnp
from jax import lax
from jax.experimental import pallas as pl
from jax.experimental.pallas import tpu as pltpu
from jax.sharding import PartitionSpec as P

BF = jnp.bfloat16
F32 = jnp.float32
LANES = 128
VMEM_MIB = 60


def dot(a, b):
    return jnp.dot(a, b, preferred_element_type=F32)


def dot_t(a, b):
    return lax.dot_general(a, b, (((0,), (0,)), ((), ())), preferred_element_type=F32)


def dot_nt(a, b):
    return lax.dot_general(a, b, (((1,), (1,)), ((), ())), preferred_element_type=F32)


def earlier_counts(names):
    n = names.shape[-2]
    lower = (jnp.arange(n)[:, None] > jnp.arange(n)[None, :]).astype(BF)
    counts = jnp.einsum("ij,...jm->...im", lower, names.astype(BF), preferred_element_type=F32)
    return jnp.where(names, counts, -1.0)


def barrier(*values):
    return lax.optimization_barrier(values)


def swap(x, k):
    return lax.ppermute(x, "exp", [(i, i ^ k) for i in range(lax.axis_size("exp"))])


def exchange(blocks, step=1):
    return [blocks[0]] + [swap(block, step * k) for k, block in enumerate(blocks) if k]


def whole(shape, at=(0, 0)):
    return pl.BlockSpec(shape, lambda *_: at, pipeline_mode=pl.Buffered(1))


def params(mib):
    return pltpu.CompilerParams(vmem_limit_bytes=mib * 2**20)


def cost(flops, nbytes):
    return pl.CostEstimate(flops=flops, bytes_accessed=nbytes, transcendentals=0)


def window_tables(n_seq, n_exp, cap):
    pair = 2 * n_exp * cap
    d = jnp.arange(pair)
    source = d % (n_exp * cap) // cap * 32 + d // (n_exp * cap) * cap + d % cap
    i = jnp.arange(n_seq // 2)
    at = source[None, :] + (2 * cap - 16) * i[:, None]
    wide = jnp.arange(32 * n_exp)
    to_b = (at[:, :, None] == wide[None, None, :]).astype(BF)
    to_a = (at[:, None, :] == wide[None, :, None]).astype(BF)
    return to_b, to_a


def pre_kernel(n_exp, pairs, table, *refs):
    blocks, (gate, up, out_gate, out_up, rows) = refs[:n_exp], refs[n_exp:]
    size = table.shape[1]

    @pl.when(pl.program_id(0) == 0)
    def _():
        for i in range(pairs):
            window = jnp.concatenate([b[16 * i:16 * i + 32, :] for b in blocks], axis=0)
            rows[size * i:size * (i + 1), :] = dot(table[i], window).astype(BF)

    out_gate[...] = dot(rows[...], gate[...])
    out_up[...] = dot(rows[...], up[...])


def pre_products(table, blocks, gate_mat, up_mat):
    chips, pairs = len(blocks), table.shape[0]
    rows, features = blocks[0].shape
    total, units = rows * chips, gate_mat.shape[1]
    wide = 256 if units % 256 == 0 else units
    column = pl.BlockSpec((features, wide), lambda j: (0, j))
    result = pl.BlockSpec((total, wide), lambda j: (0, j))
    return pl.pallas_call(
        lambda *refs: pre_kernel(chips, pairs, *refs),
        grid=(units // wide,),
        in_specs=[whole(table.shape, (0, 0, 0))] + [whole((rows, features))] * chips + [column, column],
        out_specs=[result, result],
        out_shape=[jax.ShapeDtypeStruct((total, units), F32)] * 2,
        scratch_shapes=[pltpu.VMEM((total, features), BF)],
        compiler_params=params(VMEM_MIB),
        cost_estimate=cost(4 * total * features * units, 2 * total * features + 4 * features * units + 8 * total * units),
        name="pre_products",
    )(table, *blocks, gate_mat, up_mat)


def grad_kernel(steps, lane, grad, down, pre_gate, pre_up, gate_mat, up_mat, out_gate, out_up, out_dot, out, all_gate, all_up):
    i = pl.program_id(0)
    tall = grad.shape[0]

    @pl.when(i < steps)
    def _():
        grad_hidden = dot_nt(grad[...], down[...])
        gate, up = pre_gate[...], pre_up[...]
        sigmoid = jax.nn.sigmoid(gate)
        active = gate * sigmoid
        hidden = (active * up).astype(BF).astype(F32)
        gate_dot = jnp.sum(hidden * grad_hidden, axis=1, keepdims=True)
        out_dot[...] = (gate_dot * lane[0:1, :]).astype(BF)
        rows = pl.ds(pl.multiple_of(i * tall, tall), tall)
        grad_gate = (grad_hidden * up * sigmoid * (1.0 + gate * (1.0 - sigmoid))).astype(BF)
        grad_up = (grad_hidden * active).astype(BF)
        out_gate[...] = grad_gate
        out_up[...] = grad_up
        all_gate[rows, :] = grad_gate
        all_up[rows, :] = grad_up

    @pl.when(i >= steps)
    def _():
        out[...] = (dot_nt(all_gate[...], gate_mat[...]) + dot_nt(all_up[...], up_mat[...])).astype(BF)


def hidden_grads(lane, rows_grad, down_mat, pre_gate, pre_up, gate_mat, up_mat):
    total, features = rows_grad.shape
    units, half, steps = down_mat.shape[0], features // 2, 4
    tall = total // steps
    wide = 256 if half % 256 == 0 else half
    row = lambda width: pl.BlockSpec((tall, width), lambda i: (jnp.minimum(i, steps - 1), 0))
    mat = pl.BlockSpec((wide, units), lambda i: (half // wide + jnp.maximum(i - steps, 0), 0))
    return pl.pallas_call(
        lambda *refs: grad_kernel(steps, *refs),
        grid=(steps + half // wide,),
        in_specs=[whole(lane.shape), row(features), whole(down_mat.shape), row(units), row(units), mat, mat],
        out_specs=[row(units), row(units), row(LANES),
                   pl.BlockSpec((total, wide), lambda i: (0, jnp.maximum(i - steps, 0)))],
        out_shape=[jax.ShapeDtypeStruct((total, units), BF)] * 2
        + [jax.ShapeDtypeStruct((total, LANES), BF), jax.ShapeDtypeStruct((total, half), BF)],
        scratch_shapes=[pltpu.VMEM((total, units), BF)] * 2,
        compiler_params=params(VMEM_MIB),
        cost_estimate=cost(4 * total * features * units, 4 * total * features + 4 * features * units + 12 * total * units),
        name="hidden_grads",
    )(lane, rows_grad, down_mat, pre_gate, pre_up, gate_mat, up_mat)


def back_a_kernel(n_exp, pairs, table, grad_gate, grad_up, gate, up, gate_dot, *outs):
    wide = gate.shape[0]
    half = outs[0].shape[1] - LANES
    size = table.shape[2]

    def reorder(values, start, width):
        before = None
        for i in range(pairs):
            moved = dot(table[i], values[size * i:size * (i + 1), :])
            for k in range(n_exp):
                part = moved[32 * k:32 * k + 16, :]
                if before is not None:
                    part = part + before[32 * k + 16:32 * k + 32, :]
                outs[k][16 * i:16 * i + 16, pl.ds(start, width)] = part.astype(BF)
            before = moved
        for k in range(n_exp):
            part = before[32 * k + 16:32 * k + 32, :]
            outs[k][16 * pairs:16 * pairs + 16, pl.ds(start, width)] = part.astype(BF)

    j = pl.program_id(0)
    values = dot_nt(grad_gate[...], gate[...]) + dot_nt(grad_up[...], up[...])
    reorder(values.astype(BF), pl.multiple_of(j * wide, wide), wide)

    @pl.when(j == 0)
    def _():
        reorder(gate_dot[...], half, LANES)


def returned_a(table, grad_gate, grad_up, gate_mat, up_mat, gate_dot, n_exp):
    total, units = grad_gate.shape
    half = gate_mat.shape[0] // 2
    pairs = table.shape[0]
    wide = 256 if half % 256 == 0 else half
    mat = pl.BlockSpec((wide, units), lambda j: (j, 0))
    block = (total // n_exp, half + LANES)
    return pl.pallas_call(
        lambda *refs: back_a_kernel(n_exp, pairs, *refs),
        grid=(half // wide,),
        in_specs=[whole(table.shape, (0, 0, 0)), whole(grad_gate.shape), whole(grad_up.shape), mat, mat, whole(gate_dot.shape)],
        out_specs=[whole(block)] * n_exp,
        out_shape=[jax.ShapeDtypeStruct(block, BF)] * n_exp,
        compiler_params=params(VMEM_MIB),
        cost_estimate=cost(4 * total * half * units, 4 * half * units + 4 * total * units + 2 * total * half),
        name="returned_a",
    )(table, grad_gate, grad_up, gate_mat, up_mat, gate_dot)


def sum_kernel(n_exp, slot, weight, mine, first, last, *refs):
    blocks, out, column = refs[:n_exp], refs[n_exp], refs[n_exp + 1:]
    n_tok, chips = column[0].shape[0], len(column)
    for a, total in enumerate(column):
        half, at = (first, a) if 2 * a < chips else (last, a - chips // 2)
        other = half[n_tok * at:n_tok * (at + 1), :].astype(F32)
        total[...] = (mine[n_tok * a:n_tok * (a + 1), :] + other).astype(BF)
    half = out.shape[1] - LANES
    place = lax.broadcasted_iota(jnp.int32, (slot.shape[0], blocks[0].shape[0]), 1).astype(F32)
    sums = jnp.zeros((slot.shape[0], half), F32)
    gates = jnp.zeros((slot.shape[0], LANES), F32)
    for k in range(n_exp):
        hot = slot[:, k:k + 1] == place
        sums += dot(jnp.where(hot, weight[:, k:k + 1], 0.0).astype(BF), blocks[k][:, :half])
        gates += dot(jnp.where(hot, 1.0, 0.0).astype(BF), blocks[k][:, half:])
    out[:, :half] = sums.astype(BF)
    out[:, half:] = gates.astype(BF)


def group_sums(slot, weight, mine, first, last, blocks):
    n_exp = len(blocks)
    shape = (slot.shape[0], blocks[0].shape[1])
    column = (2 * mine.shape[0] // n_exp, mine.shape[1])
    return pl.pallas_call(
        lambda *refs: sum_kernel(n_exp, *refs),
        grid=(1,),
        in_specs=[whole(x.shape) for x in (slot, weight, mine, first, last)] + [whole(blocks[0].shape)] * n_exp,
        out_specs=[whole(shape)] + [whole(column)] * (n_exp // 2),
        out_shape=[jax.ShapeDtypeStruct(shape, BF)] + [jax.ShapeDtypeStruct(column, BF)] * (n_exp // 2),
        compiler_params=params(VMEM_MIB),
        cost_estimate=cost(2 * shape[0] * blocks[0].size * n_exp, 2 * n_exp * blocks[0].size),
        name="group_sums",
    )(slot, weight, mine, first, last, *blocks)


def named_here(top, eye, meta, local):
    flat = dot_nt(eye[...], meta)
    named = weight = jnp.zeros((local.shape[0], flat.shape[1]), F32)
    for k in range(top):
        hit = flat[k:k + 1, :] == local[:, 0:1]
        named += jnp.where(hit, 1.0, 0.0)
        weight += jnp.where(hit, flat[top + k:top + k + 1, :], 0.0)
    return named, weight


def hub_kernel(top, cap, eye, local, before, block, meta, hub, *outs):
    *blocks, out_slot, out_weight, puts = outs
    rows, n_rows = blocks[0].shape[0], hub.shape[0]

    @pl.when(pl.program_id(0) == 0)
    def _():
        named, out_weight[...] = named_here(top, eye, meta[...], local)
        slot = jnp.where(named > 0.0, block[0:1, :] * cap + dot(named.astype(BF), before[...]), -1.0)
        out_slot[...] = slot
        place = lax.broadcasted_iota(jnp.int32, (rows, n_rows), 0).astype(F32)
        for k in range(len(blocks)):
            puts[rows * k:rows * (k + 1), :] = jnp.where(place == slot[k:k + 1, :], 1.0, 0.0).astype(BF)

    placed = dot(puts[...], hub[...]).astype(BF)
    for k, out in enumerate(blocks):
        out[...] = placed[rows * k:rows * (k + 1), :]


def lower_counts(total, size):
    at = jnp.arange(total)
    same = at[:, None] // size == at[None, :] // size
    return (same & (at[:, None] < at[None, :])).astype(BF), jnp.broadcast_to((at // size).astype(F32), (8, total))


def hub_blocks(hub, local, per_group, top, cap):
    n_rows, width = hub.shape
    n_exp = local.shape[0]
    before, block = lower_counts(n_rows, per_group)
    features = width - LANES
    wide = 512 if features % 512 == 0 else features
    shape = (n_rows // per_group * cap, features)
    row = (n_exp, n_rows)
    eye = jnp.eye(LANES, dtype=BF)
    part = lambda rows: pl.BlockSpec((rows, wide), lambda j: (0, j))
    *blocks, slot, weight = pl.pallas_call(
        lambda *refs: hub_kernel(top, cap, *refs),
        grid=(features // wide,),
        in_specs=[whole(x.shape) for x in (eye, local, before, block)]
        + [whole((n_rows, LANES), (0, features // LANES)), part(n_rows)],
        out_specs=[part(shape[0])] * n_exp + [whole(row)] * 2,
        out_shape=[jax.ShapeDtypeStruct(shape, BF)] * n_exp + [jax.ShapeDtypeStruct(row, F32)] * 2,
        scratch_shapes=[pltpu.VMEM((shape[0] * n_exp, n_rows), BF)],
        compiler_params=params(VMEM_MIB),
        cost_estimate=cost(2 * shape[0] * n_exp * n_rows * width, 2 * n_exp * shape[0] * shape[1]),
        name="hub_blocks",
    )(eye, local, before, block, hub, hub)
    return blocks, slot.T, weight.T


def column_block(k, member, n_tok, column):
    return column[pl.ds(pl.multiple_of((member[0] ^ k) * n_tok, n_tok), n_tok), :]


def slots_kernel(top, n_exp, cap, member, eye, theirs, before, start, spread, place, meta, out_hot, out_slot, out_weight):
    n_tok = before.shape[0]
    parts = [column_block(k, member, n_tok, meta) for k in range(n_exp)]
    named, out_weight[...] = named_here(top, eye, jnp.concatenate(parts, axis=0), theirs)
    counts = [dot(named[:, at:at + n_tok].astype(BF), before[...]) for at in range(0, named.shape[1], n_tok)]
    rank = jnp.concatenate(counts, axis=1)
    out_slot[...] = jnp.where(named > 0.0, start[0:1, :] + rank, -1.0)
    rank = jnp.where(named > 0.0, rank, -1.0).astype(BF)
    size = spread.shape[0]
    for k in range(n_exp):
        hot = dot(spread[...], rank[:, n_tok * k:n_tok * (k + 1)]) == place[:, 0:1]
        out_hot[size * k:size * (k + 1), :] = jnp.where(hot, 1.0, 0.0).astype(BF)


def column_slots(meta, theirs, member, n_tok, top, cap):
    total = meta.shape[0]
    n_seq, n_exp = theirs.shape[0], total // n_tok
    before, block = lower_counts(n_tok, n_tok)
    start = jnp.broadcast_to((jnp.arange(total) // n_tok * cap).astype(F32), (8, total))
    at = jnp.arange(n_seq * cap)
    spread = (at[:, None] // cap == jnp.arange(n_seq)[None, :]).astype(BF)
    place = jnp.broadcast_to((at % cap).astype(F32)[:, None], (n_seq * cap, LANES))
    eye = jnp.eye(LANES, dtype=BF)
    shapes = (n_seq * n_exp * cap, n_tok), (n_seq, total), (n_seq, total)
    inputs = (eye, theirs, before, start, spread, place, meta)
    hot, slot, weight = pl.pallas_call(
        lambda *refs: slots_kernel(top, n_exp, cap, *refs),
        grid=(1,),
        in_specs=[pl.BlockSpec(memory_space=pltpu.SMEM)] + [whole(x.shape) for x in inputs],
        out_specs=[whole(shape) for shape in shapes],
        out_shape=[jax.ShapeDtypeStruct(shape, kind) for shape, kind in zip(shapes, (BF, F32, F32))],
        compiler_params=params(VMEM_MIB),
        cost_estimate=cost(4 * total * LANES * LANES, 2 * shapes[0][0] * n_tok),
        name="column_slots",
    )(member.reshape(1), *inputs)
    return hot, slot.T, weight.T


def rows_kernel(n_exp, member, table, hot, column, out):
    pairs, size = table.shape[:2]
    n_tok = hot.shape[1]
    blocks = []
    for k in range(n_exp):
        blocks.append(dot(hot[size * k:size * (k + 1), :], column_block(k, member, n_tok, column)).astype(BF))
    for i in range(pairs):
        window = jnp.concatenate([b[16 * i:16 * i + 32, :] for b in blocks], axis=0)
        out[size * i:size * (i + 1), :] = dot(table[i], window).astype(BF)


def column_rows(member, table, hot, column, n_exp):
    total, features = hot.shape[0], column.shape[1]
    wide = 512 if features % 512 == 0 else features
    part = lambda rows: pl.BlockSpec((rows, wide), lambda j: (0, j))
    return pl.pallas_call(
        lambda *refs: rows_kernel(n_exp, *refs),
        grid=(features // wide,),
        in_specs=[pl.BlockSpec(memory_space=pltpu.SMEM), whole(table.shape, (0, 0, 0)), whole(hot.shape),
                  part(column.shape[0])],
        out_specs=part(total),
        out_shape=jax.ShapeDtypeStruct((total, features), BF),
        compiler_params=params(VMEM_MIB),
        cost_estimate=cost(2 * total * hot.shape[1] * LANES, 2 * total * LANES),
        name="column_rows",
    )(member.reshape(1), table, hot, column)


def column_kernel(n_exp, place, spread, slot, weight, got, out_mine, out_first, out_last, mixed):
    n_tok = out_mine.shape[0] // (n_exp // 2)

    @pl.when(pl.program_id(0) == 0)
    def _():
        hot = dot(slot[...], spread[...]) == place[0:1, :]
        mixed[...] = jnp.where(hot, dot(weight[...], spread[...]), 0.0).astype(BF)

    sums = dot(mixed[...], got[...])
    for k in range(0, n_exp, 2):
        at = slice(n_tok * k // 2, n_tok * (k // 2 + 1))
        out_mine[at, :] = sums[n_tok * k:n_tok * (k + 1), :]
        out, at = (out_first, k) if 2 * k < n_exp else (out_last, k - n_exp // 2)
        out[n_tok * at // 2:n_tok * (at // 2 + 1), :] = sums[n_tok * (k + 1):n_tok * (k + 2), :].astype(BF)


def column_sums(slot, weight, got, n_exp):
    n_rows, n_seq = slot.shape
    total, half = got.shape
    at = jnp.arange(total)
    place = jnp.broadcast_to((at % (total // n_seq)).astype(F32), (8, total))
    spread = (jnp.arange(n_seq)[:, None] == at[None, :] // (total // n_seq)).astype(BF)
    shape = (n_rows // 2, half)
    wide = 256 if half % 256 == 0 else half
    part = lambda rows: pl.BlockSpec((rows, wide), lambda j: (0, j))
    return pl.pallas_call(
        lambda *refs: column_kernel(n_exp, *refs),
        grid=(half // wide,),
        in_specs=[whole(place.shape), whole(spread.shape), whole(slot.shape), whole(weight.shape), part(total)],
        out_specs=[part(shape[0])] + [part(shape[0] // 2)] * 2,
        out_shape=[jax.ShapeDtypeStruct(shape, F32)] + [jax.ShapeDtypeStruct((shape[0] // 2, half), BF)] * 2,
        scratch_shapes=[pltpu.VMEM((n_rows, total), BF)],
        compiler_params=params(VMEM_MIB),
        cost_estimate=cost(400 * n_rows * total * half, 2 * total * half + 3 * n_rows * half),
        name="column_sums",
    )(place, spread, slot.astype(BF), weight.astype(BF), got)


def per_device(hidden_in, grad_out, expert_ids, gate_weights, w_gate, w_up, w_down):
    n_tok, features = hidden_in.shape
    top = expert_ids.shape[1]
    n_seq, n_exp = lax.axis_size("seq"), lax.axis_size("exp")
    group, member = lax.axis_index("seq"), lax.axis_index("exp")
    experts = n_seq * n_exp
    cap = 3 * top * n_tok // (2 * experts)
    per_group = top // 2 * n_tok // n_seq
    half = features // 2
    gate_mat, up_mat, down_mat = w_gate[0], w_up[0], w_down[0]
    partner = member ^ jnp.arange(n_exp)
    to_b, to_a = window_tables(n_seq, n_exp, cap)

    meta = jnp.concatenate(
        (expert_ids.astype(BF), gate_weights.astype(BF), jnp.zeros((n_tok, LANES - 2 * top), BF)), axis=1)

    column_meta = lax.all_gather(meta, "exp", axis=0, tiled=True)
    column = lax.all_gather(grad_out, "exp", axis=0, tiled=True)
    theirs = jnp.broadcast_to((jnp.arange(n_seq) * n_exp + member).astype(F32)[:, None], (n_seq, LANES))
    put_b, slot_b, weight_b = column_slots(column_meta, theirs, member, n_tok, top, cap)
    send_b = column_rows(member, to_b, put_b, column, n_exp)

    group_ids = expert_ids // n_exp
    in_group = jnp.any(group_ids[:, :, None] == jnp.arange(n_seq)[None, None, :], axis=1)
    group_rank = earlier_counts(in_group).T
    pick = (group_rank[:, None, :] == jnp.arange(per_group, dtype=F32)[None, :, None])
    pick = pick.astype(BF).reshape(n_seq * per_group, n_tok)
    send = dot(pick, jnp.concatenate((hidden_in, meta), axis=1)).astype(BF)
    hub = lax.all_to_all(send.reshape(n_seq, per_group, features + LANES), "seq", 0, 0, tiled=True)
    hub = hub.reshape(n_seq * per_group, features + LANES)
    hub, send_b = barrier(hub, send_b)

    rows_b = n_exp * cap
    recv_b = lax.all_to_all(send_b.reshape(n_seq, rows_b, features), "seq", 0, 0, tiled=True)
    recv_b = recv_b.reshape(n_seq * rows_b, features)

    local = jnp.broadcast_to((partner + group * n_exp).astype(F32)[:, None], (n_exp, LANES))
    blocks, slot_a, weight_a = hub_blocks(hub, local, per_group, top, cap)
    rows_in = exchange(blocks)

    pre_gate, pre_up = pre_products(to_b, rows_in, gate_mat, up_mat)
    lane = jnp.broadcast_to((jnp.arange(LANES) == group * n_exp + member).astype(F32), (8, LANES))
    grad_gate, grad_up, gate_dot, back_b = hidden_grads(lane, recv_b, down_mat, pre_gate, pre_up, gate_mat, up_mat)

    back_a = returned_a(to_a, grad_gate, grad_up, gate_mat, up_mat, gate_dot, n_exp)
    got_a = exchange(back_a)
    got_b = lax.all_to_all(back_b.reshape(n_seq, rows_b, half), "seq", 0, 0, tiled=True)
    got_b, *_ = barrier(got_b, *back_a)
    mine, *other = column_sums(slot_b, weight_b, got_b.reshape(n_seq * rows_b, half), n_exp)
    back, *chip = group_sums(slot_a, weight_a, mine, *(swap(x, 1) for x in other), got_a)
    final_b = sum(p.astype(F32) for p in exchange(chip, 2))
    back = lax.all_to_all(back.reshape(n_seq, per_group, half + LANES), "seq", 0, 0, tiled=True)
    final_a = dot_t(pick, back.reshape(n_seq * per_group, half + LANES))

    grad_in = jnp.concatenate((final_a[:, :half], final_b), axis=1).astype(BF)
    table = final_a[:, half:]
    chosen = expert_ids[:, :, None] == jnp.arange(experts)[None, None, :]
    grad_gates = jnp.sum(jnp.where(chosen, table[:, None, :experts], 0.0), axis=2).astype(BF)
    return grad_in, grad_gates


def solution(mesh):
    rows, mats = P(("seq", "exp"), None), P(("seq", "exp"), None, None)
    return jax.shard_map(
        per_device, mesh=mesh, in_specs=(rows,) * 4 + (mats,) * 3, out_specs=(rows, rows), check_vma=False
    )
```

```python
import jax
import jax.numpy as jnp
from jax import lax
from jax.experimental import pallas as pl
from jax.experimental.pallas import tpu as pltpu
from jax.sharding import PartitionSpec as P

BF = jnp.bfloat16
F32 = jnp.float32
LANES = 128
VMEM_MIB = 60


def dot(a, b):
    return jnp.dot(a, b, preferred_element_type=F32)


def dot_t(a, b):
    return lax.dot_general(a, b, (((0,), (0,)), ((), ())), preferred_element_type=F32)


def dot_nt(a, b):
    return lax.dot_general(a, b, (((1,), (1,)), ((), ())), preferred_element_type=F32)


def earlier_counts(names):
    n = names.shape[-2]
    lower = (jnp.arange(n)[:, None] > jnp.arange(n)[None, :]).astype(BF)
    counts = jnp.einsum("ij,...jm->...im", lower, names.astype(BF), preferred_element_type=F32)
    return jnp.where(names, counts, -1.0)


def barrier(*values):
    return lax.optimization_barrier(values)


def swap(x, k):
    return lax.ppermute(x, "exp", [(i, i ^ k) for i in range(lax.axis_size("exp"))])


def exchange(blocks, step=1):
    return [blocks[0]] + [swap(block, step * k) for k, block in enumerate(blocks) if k]


def whole(shape, at=(0, 0)):
    return pl.BlockSpec(shape, lambda *_: at, pipeline_mode=pl.Buffered(1))


def params(mib):
    return pltpu.CompilerParams(vmem_limit_bytes=mib * 2**20)


def cost(flops, nbytes):
    return pl.CostEstimate(flops=flops, bytes_accessed=nbytes, transcendentals=0)


def window_tables(n_seq, n_exp, cap):
    pair = 2 * n_exp * cap
    d = jnp.arange(pair)
    source = d % (n_exp * cap) // cap * 32 + d // (n_exp * cap) * cap + d % cap
    i = jnp.arange(n_seq // 2)
    at = source[None, :] + (2 * cap - 16) * i[:, None]
    wide = jnp.arange(32 * n_exp)
    to_b = (at[:, :, None] == wide[None, None, :]).astype(BF)
    to_a = (at[:, None, :] == wide[None, :, None]).astype(BF)
    return to_b, to_a


def pre_kernel(n_exp, pairs, table, *refs):
    blocks, (gate, up, out_gate, out_up, rows) = refs[:n_exp], refs[n_exp:]
    size = table.shape[1]

    @pl.when(pl.program_id(0) == 0)
    def _():
        for i in range(pairs):
            window = jnp.concatenate([b[16 * i:16 * i + 32, :] for b in blocks], axis=0)
            rows[size * i:size * (i + 1), :] = dot(table[i], window).astype(BF)

    out_gate[...] = dot(rows[...], gate[...])
    out_up[...] = dot(rows[...], up[...])


def pre_products(table, blocks, gate_mat, up_mat):
    chips, pairs = len(blocks), table.shape[0]
    rows, features = blocks[0].shape
    total, units = rows * chips, gate_mat.shape[1]
    wide = 256 if units % 256 == 0 else units
    column = pl.BlockSpec((features, wide), lambda j: (0, j))
    result = pl.BlockSpec((total, wide), lambda j: (0, j))
    return pl.pallas_call(
        lambda *refs: pre_kernel(chips, pairs, *refs),
        grid=(units // wide,),
        in_specs=[whole(table.shape, (0, 0, 0))] + [whole((rows, features))] * chips + [column, column],
        out_specs=[result, result],
        out_shape=[jax.ShapeDtypeStruct((total, units), F32)] * 2,
        scratch_shapes=[pltpu.VMEM((total, features), BF)],
        compiler_params=params(VMEM_MIB),
        cost_estimate=cost(4 * total * features * units, 2 * total * features + 4 * features * units + 8 * total * units),
        name="pre_products",
    )(table, *blocks, gate_mat, up_mat)


def grad_kernel(steps, lane, grad, down, pre_gate, pre_up, gate_mat, up_mat, out_gate, out_up, out_dot, out, all_gate, all_up):
    i = pl.program_id(0)
    tall = grad.shape[0]

    @pl.when(i < steps)
    def _():
        grad_hidden = dot_nt(grad[...], down[...])
        gate, up = pre_gate[...], pre_up[...]
        sigmoid = jax.nn.sigmoid(gate)
        active = gate * sigmoid
        hidden = (active * up).astype(BF).astype(F32)
        gate_dot = jnp.sum(hidden * grad_hidden, axis=1, keepdims=True)
        out_dot[...] = (gate_dot * lane[0:1, :]).astype(BF)
        rows = pl.ds(pl.multiple_of(i * tall, tall), tall)
        grad_gate = (grad_hidden * up * sigmoid * (1.0 + gate * (1.0 - sigmoid))).astype(BF)
        grad_up = (grad_hidden * active).astype(BF)
        out_gate[...] = grad_gate
        out_up[...] = grad_up
        all_gate[rows, :] = grad_gate
        all_up[rows, :] = grad_up

    @pl.when(i >= steps)
    def _():
        out[...] = (dot_nt(all_gate[...], gate_mat[...]) + dot_nt(all_up[...], up_mat[...])).astype(BF)


def hidden_grads(lane, rows_grad, down_mat, pre_gate, pre_up, gate_mat, up_mat):
    total, features = rows_grad.shape
    units, half, steps = down_mat.shape[0], features // 2, 4
    tall = total // steps
    wide = 256 if half % 256 == 0 else half
    row = lambda width: pl.BlockSpec((tall, width), lambda i: (jnp.minimum(i, steps - 1), 0))
    mat = pl.BlockSpec((wide, units), lambda i: (half // wide + jnp.maximum(i - steps, 0), 0))
    return pl.pallas_call(
        lambda *refs: grad_kernel(steps, *refs),
        grid=(steps + half // wide,),
        in_specs=[whole(lane.shape), row(features), whole(down_mat.shape), row(units), row(units), mat, mat],
        out_specs=[row(units), row(units), row(LANES),
                   pl.BlockSpec((total, wide), lambda i: (0, jnp.maximum(i - steps, 0)))],
        out_shape=[jax.ShapeDtypeStruct((total, units), BF)] * 2
        + [jax.ShapeDtypeStruct((total, LANES), BF), jax.ShapeDtypeStruct((total, half), BF)],
        scratch_shapes=[pltpu.VMEM((total, units), BF)] * 2,
        compiler_params=params(VMEM_MIB),
        cost_estimate=cost(4 * total * features * units, 4 * total * features + 4 * features * units + 12 * total * units),
        name="hidden_grads",
    )(lane, rows_grad, down_mat, pre_gate, pre_up, gate_mat, up_mat)


def back_a_kernel(n_exp, pairs, table, grad_gate, grad_up, gate, up, gate_dot, *outs):
    wide = gate.shape[0]
    half = outs[0].shape[1] - LANES
    size = table.shape[2]

    def reorder(values, start, width):
        before = None
        for i in range(pairs):
            moved = dot(table[i], values[size * i:size * (i + 1), :])
            for k in range(n_exp):
                part = moved[32 * k:32 * k + 16, :]
                if before is not None:
                    part = part + before[32 * k + 16:32 * k + 32, :]
                outs[k][16 * i:16 * i + 16, pl.ds(start, width)] = part.astype(BF)
            before = moved
        for k in range(n_exp):
            part = before[32 * k + 16:32 * k + 32, :]
            outs[k][16 * pairs:16 * pairs + 16, pl.ds(start, width)] = part.astype(BF)

    j = pl.program_id(0)
    values = dot_nt(grad_gate[...], gate[...]) + dot_nt(grad_up[...], up[...])
    reorder(values.astype(BF), pl.multiple_of(j * wide, wide), wide)

    @pl.when(j == 0)
    def _():
        reorder(gate_dot[...], half, LANES)


def returned_a(table, grad_gate, grad_up, gate_mat, up_mat, gate_dot, n_exp):
    total, units = grad_gate.shape
    half = gate_mat.shape[0] // 2
    pairs = table.shape[0]
    wide = 256 if half % 256 == 0 else half
    mat = pl.BlockSpec((wide, units), lambda j: (j, 0))
    block = (total // n_exp, half + LANES)
    return pl.pallas_call(
        lambda *refs: back_a_kernel(n_exp, pairs, *refs),
        grid=(half // wide,),
        in_specs=[whole(table.shape, (0, 0, 0)), whole(grad_gate.shape), whole(grad_up.shape), mat, mat, whole(gate_dot.shape)],
        out_specs=[whole(block)] * n_exp,
        out_shape=[jax.ShapeDtypeStruct(block, BF)] * n_exp,
        compiler_params=params(VMEM_MIB),
        cost_estimate=cost(4 * total * half * units, 4 * half * units + 4 * total * units + 2 * total * half),
        name="returned_a",
    )(table, grad_gate, grad_up, gate_mat, up_mat, gate_dot)


def sum_kernel(n_exp, slot, weight, mine, first, last, *refs):
    blocks, out, column = refs[:n_exp], refs[n_exp], refs[n_exp + 1:]
    n_tok, chips = column[0].shape[0], len(column)
    for a, total in enumerate(column):
        half, at = (first, a) if 2 * a < chips else (last, a - chips // 2)
        other = half[n_tok * at:n_tok * (at + 1), :].astype(F32)
        total[...] = (mine[n_tok * a:n_tok * (a + 1), :] + other).astype(BF)
    half = out.shape[1] - LANES
    place = lax.broadcasted_iota(jnp.int32, (slot.shape[0], blocks[0].shape[0]), 1).astype(F32)
    sums = jnp.zeros((slot.shape[0], half), F32)
    gates = jnp.zeros((slot.shape[0], LANES), F32)
    for k in range(n_exp):
        hot = slot[:, k:k + 1] == place
        sums += dot(jnp.where(hot, weight[:, k:k + 1], 0.0).astype(BF), blocks[k][:, :half])
        gates += dot(jnp.where(hot, 1.0, 0.0).astype(BF), blocks[k][:, half:])
    out[:, :half] = sums.astype(BF)
    out[:, half:] = gates.astype(BF)


def group_sums(slot, weight, mine, first, last, blocks):
    n_exp = len(blocks)
    shape = (slot.shape[0], blocks[0].shape[1])
    column = (2 * mine.shape[0] // n_exp, mine.shape[1])
    return pl.pallas_call(
        lambda *refs: sum_kernel(n_exp, *refs),
        grid=(1,),
        in_specs=[whole(x.shape) for x in (slot, weight, mine, first, last)] + [whole(blocks[0].shape)] * n_exp,
        out_specs=[whole(shape)] + [whole(column)] * (n_exp // 2),
        out_shape=[jax.ShapeDtypeStruct(shape, BF)] + [jax.ShapeDtypeStruct(column, BF)] * (n_exp // 2),
        compiler_params=params(VMEM_MIB),
        cost_estimate=cost(2 * shape[0] * blocks[0].size * n_exp, 2 * n_exp * blocks[0].size),
        name="group_sums",
    )(slot, weight, mine, first, last, *blocks)


def named_here(top, eye, meta, local):
    flat = dot_nt(eye[...], meta)
    named = weight = jnp.zeros((local.shape[0], flat.shape[1]), F32)
    for k in range(top):
        hit = flat[k:k + 1, :] == local[:, 0:1]
        named += jnp.where(hit, 1.0, 0.0)
        weight += jnp.where(hit, flat[top + k:top + k + 1, :], 0.0)
    return named, weight


def hub_kernel(top, cap, eye, local, before, block, meta, hub, *outs):
    *blocks, out_slot, out_weight, puts = outs
    rows, n_rows = blocks[0].shape[0], hub.shape[0]

    @pl.when(pl.program_id(0) == 0)
    def _():
        named, out_weight[...] = named_here(top, eye, meta[...], local)
        slot = jnp.where(named > 0.0, block[0:1, :] * cap + dot(named.astype(BF), before[...]), -1.0)
        out_slot[...] = slot
        place = lax.broadcasted_iota(jnp.int32, (rows, n_rows), 0).astype(F32)
        for k in range(len(blocks)):
            puts[rows * k:rows * (k + 1), :] = jnp.where(place == slot[k:k + 1, :], 1.0, 0.0).astype(BF)

    placed = dot(puts[...], hub[...]).astype(BF)
    for k, out in enumerate(blocks):
        out[...] = placed[rows * k:rows * (k + 1), :]


def lower_counts(total, size):
    at = jnp.arange(total)
    same = at[:, None] // size == at[None, :] // size
    return (same & (at[:, None] < at[None, :])).astype(BF), jnp.broadcast_to((at // size).astype(F32), (8, total))


def hub_blocks(hub, tables, per_group, top, cap):
    n_rows, width = hub.shape
    n_exp = tables[1].shape[0]
    features = width - LANES
    wide = 512 if features % 512 == 0 else features
    shape = (n_rows // per_group * cap, features)
    row = (n_exp, n_rows)
    part = lambda rows: pl.BlockSpec((rows, wide), lambda j: (0, j))
    *blocks, slot, weight = pl.pallas_call(
        lambda *refs: hub_kernel(top, cap, *refs),
        grid=(features // wide,),
        in_specs=[whole(x.shape) for x in tables]
        + [whole((n_rows, LANES), (0, features // LANES)), part(n_rows)],
        out_specs=[part(shape[0])] * n_exp + [whole(row)] * 2,
        out_shape=[jax.ShapeDtypeStruct(shape, BF)] * n_exp + [jax.ShapeDtypeStruct(row, F32)] * 2,
        scratch_shapes=[pltpu.VMEM((shape[0] * n_exp, n_rows), BF)],
        compiler_params=params(VMEM_MIB),
        cost_estimate=cost(2 * shape[0] * n_exp * n_rows * width, 2 * n_exp * shape[0] * shape[1]),
        name="hub_blocks",
    )(*tables, hub, hub)
    return blocks, slot.T, weight.T


def column_block(k, member, n_tok, column):
    return column[pl.ds(pl.multiple_of((member[0] ^ k) * n_tok, n_tok), n_tok), :]


def slots_kernel(top, n_exp, cap, member, eye, theirs, before, start, spread, place, meta, out_hot, out_slot, out_weight):
    n_tok = before.shape[0]
    parts = [column_block(k, member, n_tok, meta) for k in range(n_exp)]
    named, out_weight[...] = named_here(top, eye, jnp.concatenate(parts, axis=0), theirs)
    counts = [dot(named[:, at:at + n_tok].astype(BF), before[...]) for at in range(0, named.shape[1], n_tok)]
    rank = jnp.concatenate(counts, axis=1)
    out_slot[...] = jnp.where(named > 0.0, start[0:1, :] + rank, -1.0)
    rank = jnp.where(named > 0.0, rank, -1.0).astype(BF)
    size = spread.shape[0]
    for k in range(n_exp):
        hot = dot(spread[...], rank[:, n_tok * k:n_tok * (k + 1)]) == place[:, 0:1]
        out_hot[size * k:size * (k + 1), :] = jnp.where(hot, 1.0, 0.0).astype(BF)


def column_slots(meta, theirs, member, n_tok, top, cap):
    total = meta.shape[0]
    n_seq, n_exp = theirs.shape[0], total // n_tok
    before, block = lower_counts(n_tok, n_tok)
    start = jnp.broadcast_to((jnp.arange(total) // n_tok * cap).astype(F32), (8, total))
    at = jnp.arange(n_seq * cap)
    spread = (at[:, None] // cap == jnp.arange(n_seq)[None, :]).astype(BF)
    place = jnp.broadcast_to((at % cap).astype(F32)[:, None], (n_seq * cap, LANES))
    eye = jnp.eye(LANES, dtype=BF)
    shapes = (n_seq * n_exp * cap, n_tok), (n_seq, total), (n_seq, total)
    inputs = (eye, theirs, before, start, spread, place, meta)
    hot, slot, weight = pl.pallas_call(
        lambda *refs: slots_kernel(top, n_exp, cap, *refs),
        grid=(1,),
        in_specs=[pl.BlockSpec(memory_space=pltpu.SMEM)] + [whole(x.shape) for x in inputs],
        out_specs=[whole(shape) for shape in shapes],
        out_shape=[jax.ShapeDtypeStruct(shape, kind) for shape, kind in zip(shapes, (BF, F32, F32))],
        compiler_params=params(VMEM_MIB),
        cost_estimate=cost(4 * total * LANES * LANES, 2 * shapes[0][0] * n_tok),
        name="column_slots",
    )(member.reshape(1), *inputs)
    return hot, slot.T, weight.T


def rows_kernel(n_exp, member, table, hot, column, out):
    pairs, size = table.shape[:2]
    n_tok = hot.shape[1]
    blocks = []
    for k in range(n_exp):
        blocks.append(dot(hot[size * k:size * (k + 1), :], column_block(k, member, n_tok, column)).astype(BF))
    for i in range(pairs):
        window = jnp.concatenate([b[16 * i:16 * i + 32, :] for b in blocks], axis=0)
        out[size * i:size * (i + 1), :] = dot(table[i], window).astype(BF)


def column_rows(member, table, hot, column, n_exp):
    total, features = hot.shape[0], column.shape[1]
    wide = 512 if features % 512 == 0 else features
    part = lambda rows: pl.BlockSpec((rows, wide), lambda j: (0, j))
    return pl.pallas_call(
        lambda *refs: rows_kernel(n_exp, *refs),
        grid=(features // wide,),
        in_specs=[pl.BlockSpec(memory_space=pltpu.SMEM), whole(table.shape, (0, 0, 0)), whole(hot.shape),
                  part(column.shape[0])],
        out_specs=part(total),
        out_shape=jax.ShapeDtypeStruct((total, features), BF),
        compiler_params=params(VMEM_MIB),
        cost_estimate=cost(2 * total * hot.shape[1] * LANES, 2 * total * LANES),
        name="column_rows",
    )(member.reshape(1), table, hot, column)


def column_kernel(n_exp, place, spread, slot, weight, got, out_mine, out_first, out_last, mixed):
    n_tok = out_mine.shape[0] // (n_exp // 2)

    @pl.when(pl.program_id(0) == 0)
    def _():
        hot = dot(slot[...], spread[...]) == place[0:1, :]
        mixed[...] = jnp.where(hot, dot(weight[...], spread[...]), 0.0).astype(BF)

    sums = dot(mixed[...], got[...])
    for k in range(0, n_exp, 2):
        at = slice(n_tok * k // 2, n_tok * (k // 2 + 1))
        out_mine[at, :] = sums[n_tok * k:n_tok * (k + 1), :]
        out, at = (out_first, k) if 2 * k < n_exp else (out_last, k - n_exp // 2)
        out[n_tok * at // 2:n_tok * (at // 2 + 1), :] = sums[n_tok * (k + 1):n_tok * (k + 2), :].astype(BF)


def column_sums(slot, weight, got, n_exp):
    n_rows, n_seq = slot.shape
    total, half = got.shape
    at = jnp.arange(total)
    place = jnp.broadcast_to((at % (total // n_seq)).astype(F32), (8, total))
    spread = (jnp.arange(n_seq)[:, None] == at[None, :] // (total // n_seq)).astype(BF)
    shape = (n_rows // 2, half)
    wide = 256 if half % 256 == 0 else half
    part = lambda rows: pl.BlockSpec((rows, wide), lambda j: (0, j))
    return pl.pallas_call(
        lambda *refs: column_kernel(n_exp, *refs),
        grid=(half // wide,),
        in_specs=[whole(place.shape), whole(spread.shape), whole(slot.shape), whole(weight.shape), part(total)],
        out_specs=[part(shape[0])] + [part(shape[0] // 2)] * 2,
        out_shape=[jax.ShapeDtypeStruct(shape, F32)] + [jax.ShapeDtypeStruct((shape[0] // 2, half), BF)] * 2,
        scratch_shapes=[pltpu.VMEM((n_rows, total), BF)],
        compiler_params=params(VMEM_MIB),
        cost_estimate=cost(400 * n_rows * total * half, 2 * total * half + 3 * n_rows * half),
        name="column_sums",
    )(place, spread, slot, weight, got)


def per_device(hidden_in, grad_out, expert_ids, gate_weights, w_gate, w_up, w_down):
    n_tok, features = hidden_in.shape
    top = expert_ids.shape[1]
    n_seq, n_exp = lax.axis_size("seq"), lax.axis_size("exp")
    group, member = lax.axis_index("seq"), lax.axis_index("exp")
    experts = n_seq * n_exp
    cap = 3 * top * n_tok // (2 * experts)
    per_group = top // 2 * n_tok // n_seq
    half = features // 2
    gate_mat, up_mat, down_mat = w_gate[0], w_up[0], w_down[0]
    partner = member ^ jnp.arange(n_exp)
    to_b, to_a = window_tables(n_seq, n_exp, cap)

    meta = jnp.concatenate(
        (expert_ids.astype(BF), gate_weights.astype(BF), jnp.zeros((n_tok, LANES - 2 * top), BF)), axis=1)

    column_meta = lax.all_gather(meta, "exp", axis=0, tiled=True)
    column = lax.all_gather(grad_out, "exp", axis=0, tiled=True)
    theirs = jnp.broadcast_to((jnp.arange(n_seq) * n_exp + member).astype(F32)[:, None], (n_seq, LANES))
    put_b, slot_b, weight_b = column_slots(column_meta, theirs, member, n_tok, top, cap)
    slot_b, weight_b = slot_b.astype(BF), weight_b.astype(BF)
    local = jnp.broadcast_to((partner + group * n_exp).astype(F32)[:, None], (n_exp, LANES))
    tables = (jnp.eye(LANES, dtype=BF), local) + lower_counts(n_seq * per_group, per_group)
    put_b, to_b, to_a, slot_b, weight_b, *tables = barrier(put_b, to_b, to_a, slot_b, weight_b, *tables)
    send_b = column_rows(member, to_b, put_b, column, n_exp)

    group_ids = expert_ids // n_exp
    in_group = jnp.any(group_ids[:, :, None] == jnp.arange(n_seq)[None, None, :], axis=1)
    group_rank = earlier_counts(in_group).T
    pick = (group_rank[:, None, :] == jnp.arange(per_group, dtype=F32)[None, :, None])
    pick = pick.astype(BF).reshape(n_seq * per_group, n_tok)
    send = dot(pick, jnp.concatenate((hidden_in, meta), axis=1)).astype(BF)
    hub = lax.all_to_all(send.reshape(n_seq, per_group, features + LANES), "seq", 0, 0, tiled=True)
    hub = hub.reshape(n_seq * per_group, features + LANES)
    hub, send_b = barrier(hub, send_b)

    rows_b = n_exp * cap
    recv_b = lax.all_to_all(send_b.reshape(n_seq, rows_b, features), "seq", 0, 0, tiled=True)
    recv_b = recv_b.reshape(n_seq * rows_b, features)

    blocks, slot_a, weight_a = hub_blocks(hub, tables, per_group, top, cap)
    rows_in = exchange(blocks)

    pre_gate, pre_up = pre_products(to_b, rows_in, gate_mat, up_mat)
    lane = jnp.broadcast_to((jnp.arange(LANES) == group * n_exp + member).astype(F32), (8, LANES))
    grad_gate, grad_up, gate_dot, back_b = hidden_grads(lane, recv_b, down_mat, pre_gate, pre_up, gate_mat, up_mat)

    back_a = returned_a(to_a, grad_gate, grad_up, gate_mat, up_mat, gate_dot, n_exp)
    got_a = exchange(back_a)
    got_b = lax.all_to_all(back_b.reshape(n_seq, rows_b, half), "seq", 0, 0, tiled=True)
    got_b, *got_a = barrier(got_b, *got_a)
    mine, *other = column_sums(slot_b, weight_b, got_b.reshape(n_seq * rows_b, half), n_exp)
    back, *chip = group_sums(slot_a, weight_a, mine, *(swap(x, 1) for x in other), got_a)
    final_b = sum(p.astype(F32) for p in exchange(chip, 2))
    back = lax.all_to_all(back.reshape(n_seq, per_group, half + LANES), "seq", 0, 0, tiled=True)
    final_a = dot_t(pick, back.reshape(n_seq * per_group, half + LANES))

    grad_in = jnp.concatenate((final_a[:, :half], final_b), axis=1).astype(BF)
    table = final_a[:, half:]
    chosen = expert_ids[:, :, None] == jnp.arange(experts)[None, None, :]
    grad_gates = jnp.sum(jnp.where(chosen, table[:, None, :experts], 0.0), axis=2).astype(BF)
    return grad_in, grad_gates


def solution(mesh):
    rows, mats = P(("seq", "exp"), None), P(("seq", "exp"), None, None)
    return jax.shard_map(
        per_device, mesh=mesh, in_specs=(rows,) * 4 + (mats,) * 3, out_specs=(rows, rows), check_vma=False
    )
```

```python
import jax
import jax.numpy as jnp
from jax import lax
from jax.experimental import pallas as pl
from jax.experimental.pallas import tpu as pltpu
from jax.sharding import PartitionSpec as P

BF = jnp.bfloat16
F32 = jnp.float32
LANES = 128
VMEM_MIB = 60


def dot(a, b):
    return jnp.dot(a, b, preferred_element_type=F32)


def dot_t(a, b):
    return lax.dot_general(a, b, (((0,), (0,)), ((), ())), preferred_element_type=F32)


def dot_nt(a, b):
    return lax.dot_general(a, b, (((1,), (1,)), ((), ())), preferred_element_type=F32)


def earlier_counts(names):
    n = names.shape[-2]
    lower = (jnp.arange(n)[:, None] > jnp.arange(n)[None, :]).astype(BF)
    counts = jnp.einsum("ij,...jm->...im", lower, names.astype(BF), preferred_element_type=F32)
    return jnp.where(names, counts, -1.0)


def first_columns(features):
    return max(2 * features // 5 // 256 * 256, 256)


def barrier(*values):
    return lax.optimization_barrier(values)


def swap(x, k):
    return lax.ppermute(x, "exp", [(i, i ^ k) for i in range(lax.axis_size("exp"))])


def exchange(blocks, step=1):
    return [blocks[0]] + [swap(block, step * k) for k, block in enumerate(blocks) if k]


def whole(shape, at=(0, 0)):
    return pl.BlockSpec(shape, lambda *_: at, pipeline_mode=pl.Buffered(1))


def params(mib):
    return pltpu.CompilerParams(vmem_limit_bytes=mib * 2**20)


def cost(flops, nbytes):
    return pl.CostEstimate(flops=flops, bytes_accessed=nbytes, transcendentals=0)


def window_tables(n_seq, n_exp, cap):
    pair = 2 * n_exp * cap
    d = jnp.arange(pair)
    source = d % (n_exp * cap) // cap * 32 + d // (n_exp * cap) * cap + d % cap
    i = jnp.arange(n_seq // 2)
    at = source[None, :] + (2 * cap - 16) * i[:, None]
    wide = jnp.arange(32 * n_exp)
    to_b = (at[:, :, None] == wide[None, None, :]).astype(BF)
    to_a = (at[:, None, :] == wide[None, :, None]).astype(BF)
    return to_b, to_a


def pre_kernel(n_exp, pairs, table, *refs):
    blocks, (gate, up, out_gate, out_up, rows) = refs[:n_exp], refs[n_exp:]
    size = table.shape[1]

    @pl.when(pl.program_id(0) == 0)
    def _():
        for i in range(pairs):
            window = jnp.concatenate([b[16 * i:16 * i + 32, :] for b in blocks], axis=0)
            rows[size * i:size * (i + 1), :] = dot(table[i], window).astype(BF)

    out_gate[...] = dot(rows[...], gate[...])
    out_up[...] = dot(rows[...], up[...])


def pre_products(table, blocks, gate_mat, up_mat):
    chips, pairs = len(blocks), table.shape[0]
    rows, features = blocks[0].shape
    total, units = rows * chips, gate_mat.shape[1]
    wide = 256 if units % 256 == 0 else units
    column = pl.BlockSpec((features, wide), lambda j: (0, j))
    result = pl.BlockSpec((total, wide), lambda j: (0, j))
    return pl.pallas_call(
        lambda *refs: pre_kernel(chips, pairs, *refs),
        grid=(units // wide,),
        in_specs=[whole(table.shape, (0, 0, 0))] + [whole((rows, features))] * chips + [column, column],
        out_specs=[result, result],
        out_shape=[jax.ShapeDtypeStruct((total, units), F32)] * 2,
        scratch_shapes=[pltpu.VMEM((total, features), BF)],
        compiler_params=params(VMEM_MIB),
        cost_estimate=cost(4 * total * features * units, 2 * total * features + 4 * features * units + 8 * total * units),
        name="pre_products",
    )(table, *blocks, gate_mat, up_mat)


def grad_kernel(steps, lane, grad, down, pre_gate, pre_up, gate_mat, up_mat, out_gate, out_up, out_dot, out, all_gate, all_up):
    i = pl.program_id(0)
    tall = grad.shape[0]

    @pl.when(i < steps)
    def _():
        grad_hidden = dot_nt(grad[...], down[...])
        gate, up = pre_gate[...], pre_up[...]
        sigmoid = jax.nn.sigmoid(gate)
        active = gate * sigmoid
        hidden = (active * up).astype(BF).astype(F32)
        gate_dot = jnp.sum(hidden * grad_hidden, axis=1, keepdims=True)
        out_dot[...] = (gate_dot * lane[0:1, :]).astype(BF)
        rows = pl.ds(pl.multiple_of(i * tall, tall), tall)
        grad_gate = (grad_hidden * up * sigmoid * (1.0 + gate * (1.0 - sigmoid))).astype(BF)
        grad_up = (grad_hidden * active).astype(BF)
        out_gate[...] = grad_gate
        out_up[...] = grad_up
        all_gate[rows, :] = grad_gate
        all_up[rows, :] = grad_up

    @pl.when(i >= steps)
    def _():
        out[...] = (dot_nt(all_gate[...], gate_mat[...]) + dot_nt(all_up[...], up_mat[...])).astype(BF)


def hidden_grads(lane, rows_grad, down_mat, pre_gate, pre_up, gate_mat, up_mat):
    total, features = rows_grad.shape
    units, first, steps = down_mat.shape[0], first_columns(features), 4
    half = features - first
    tall = total // steps
    wide = 512 if half % 512 == 0 else half
    row = lambda width: pl.BlockSpec((tall, width), lambda i: (jnp.minimum(i, steps - 1), 0))
    mat = pl.BlockSpec((wide, units), lambda i: (first // wide + jnp.maximum(i - steps, 0), 0))
    return pl.pallas_call(
        lambda *refs: grad_kernel(steps, *refs),
        grid=(steps + half // wide,),
        in_specs=[whole(lane.shape), row(features), whole(down_mat.shape), row(units), row(units), mat, mat],
        out_specs=[row(units), row(units), row(LANES),
                   pl.BlockSpec((total, wide), lambda i: (0, jnp.maximum(i - steps, 0)))],
        out_shape=[jax.ShapeDtypeStruct((total, units), BF)] * 2
        + [jax.ShapeDtypeStruct((total, LANES), BF), jax.ShapeDtypeStruct((total, half), BF)],
        scratch_shapes=[pltpu.VMEM((total, units), BF)] * 2,
        compiler_params=params(VMEM_MIB),
        cost_estimate=cost(4 * total * features * units, 4 * total * features + 4 * features * units + 12 * total * units),
        name="hidden_grads",
    )(lane, rows_grad, down_mat, pre_gate, pre_up, gate_mat, up_mat)


def back_a_kernel(n_exp, pairs, table, grad_gate, grad_up, gate, up, gate_dot, *outs):
    wide = gate.shape[0]
    half = outs[0].shape[1] - LANES
    size = table.shape[2]

    def reorder(values, start, width):
        before = None
        for i in range(pairs):
            moved = dot(table[i], values[size * i:size * (i + 1), :])
            for k in range(n_exp):
                part = moved[32 * k:32 * k + 16, :]
                if before is not None:
                    part = part + before[32 * k + 16:32 * k + 32, :]
                outs[k][16 * i:16 * i + 16, pl.ds(start, width)] = part.astype(BF)
            before = moved
        for k in range(n_exp):
            part = before[32 * k + 16:32 * k + 32, :]
            outs[k][16 * pairs:16 * pairs + 16, pl.ds(start, width)] = part.astype(BF)

    j = pl.program_id(0)
    values = dot_nt(grad_gate[...], gate[...]) + dot_nt(grad_up[...], up[...])
    reorder(values.astype(BF), pl.multiple_of(j * wide, wide), wide)

    @pl.when(j == 0)
    def _():
        reorder(gate_dot[...], half, LANES)


def returned_a(table, grad_gate, grad_up, gate_mat, up_mat, gate_dot, n_exp):
    total, units = grad_gate.shape
    half = first_columns(gate_mat.shape[0])
    pairs = table.shape[0]
    wide = 512 if half % 512 == 0 else half
    mat = pl.BlockSpec((wide, units), lambda j: (j, 0))
    block = (total // n_exp, half + LANES)
    return pl.pallas_call(
        lambda *refs: back_a_kernel(n_exp, pairs, *refs),
        grid=(half // wide,),
        in_specs=[whole(table.shape, (0, 0, 0)), whole(grad_gate.shape), whole(grad_up.shape), mat, mat, whole(gate_dot.shape)],
        out_specs=[whole(block)] * n_exp,
        out_shape=[jax.ShapeDtypeStruct(block, BF)] * n_exp,
        compiler_params=params(VMEM_MIB),
        cost_estimate=cost(4 * total * half * units, 4 * half * units + 4 * total * units + 2 * total * half),
        name="returned_a",
    )(table, grad_gate, grad_up, gate_mat, up_mat, gate_dot)


def sum_kernel(n_exp, slot, weight, mine, first, last, *refs):
    blocks, out, column = refs[:n_exp], refs[n_exp], refs[n_exp + 1:]
    n_tok, chips = column[0].shape[0], len(column)
    for a, total in enumerate(column):
        half, at = (first, a) if 2 * a < chips else (last, a - chips // 2)
        other = half[n_tok * at:n_tok * (at + 1), :].astype(F32)
        total[...] = (mine[n_tok * a:n_tok * (a + 1), :] + other).astype(BF)
    half = out.shape[1] - LANES
    place = lax.broadcasted_iota(jnp.int32, (slot.shape[0], blocks[0].shape[0]), 1).astype(F32)
    sums = jnp.zeros((slot.shape[0], half), F32)
    gates = jnp.zeros((slot.shape[0], LANES), F32)
    for k in range(n_exp):
        hot = slot[:, k:k + 1] == place
        sums += dot(jnp.where(hot, weight[:, k:k + 1], 0.0).astype(BF), blocks[k][:, :half])
        gates += dot(jnp.where(hot, 1.0, 0.0).astype(BF), blocks[k][:, half:])
    out[:, :half] = sums.astype(BF)
    out[:, half:] = gates.astype(BF)


def group_sums(slot, weight, mine, first, last, blocks):
    n_exp = len(blocks)
    shape = (slot.shape[0], blocks[0].shape[1])
    column = (2 * mine.shape[0] // n_exp, mine.shape[1])
    return pl.pallas_call(
        lambda *refs: sum_kernel(n_exp, *refs),
        grid=(1,),
        in_specs=[whole(x.shape) for x in (slot, weight, mine, first, last)] + [whole(blocks[0].shape)] * n_exp,
        out_specs=[whole(shape)] + [whole(column)] * (n_exp // 2),
        out_shape=[jax.ShapeDtypeStruct(shape, BF)] + [jax.ShapeDtypeStruct(column, BF)] * (n_exp // 2),
        compiler_params=params(VMEM_MIB),
        cost_estimate=cost(2 * shape[0] * blocks[0].size * n_exp, 2 * n_exp * blocks[0].size),
        name="group_sums",
    )(slot, weight, mine, first, last, *blocks)


def named_here(top, eye, meta, local):
    flat = dot_nt(eye[...], meta)
    named = weight = jnp.zeros((local.shape[0], flat.shape[1]), F32)
    for k in range(top):
        hit = flat[k:k + 1, :] == local[:, 0:1]
        named += jnp.where(hit, 1.0, 0.0)
        weight += jnp.where(hit, flat[top + k:top + k + 1, :], 0.0)
    return named, weight


def hub_kernel(top, cap, eye, local, before, block, meta, hub, *outs):
    *blocks, out_slot, out_weight, puts = outs
    rows, n_rows = blocks[0].shape[0], hub.shape[0]

    @pl.when(pl.program_id(0) == 0)
    def _():
        named, out_weight[...] = named_here(top, eye, meta[...], local)
        slot = jnp.where(named > 0.0, block[0:1, :] * cap + dot(named.astype(BF), before[...]), -1.0)
        out_slot[...] = slot
        place = lax.broadcasted_iota(jnp.int32, (rows, n_rows), 0).astype(F32)
        for k in range(len(blocks)):
            puts[rows * k:rows * (k + 1), :] = jnp.where(place == slot[k:k + 1, :], 1.0, 0.0).astype(BF)

    placed = dot(puts[...], hub[...]).astype(BF)
    for k, out in enumerate(blocks):
        out[...] = placed[rows * k:rows * (k + 1), :]


def lower_counts(total, size):
    at = jnp.arange(total)
    same = at[:, None] // size == at[None, :] // size
    return (same & (at[:, None] < at[None, :])).astype(BF), jnp.broadcast_to((at // size).astype(F32), (8, total))


def hub_blocks(hub, tables, per_group, top, cap):
    n_rows, width = hub.shape
    n_exp = tables[1].shape[0]
    features = width - LANES
    wide = 1280 if features % 1280 == 0 else features
    shape = (n_rows // per_group * cap, features)
    row = (n_exp, n_rows)
    part = lambda rows: pl.BlockSpec((rows, wide), lambda j: (0, j))
    *blocks, slot, weight = pl.pallas_call(
        lambda *refs: hub_kernel(top, cap, *refs),
        grid=(features // wide,),
        in_specs=[whole(x.shape) for x in tables]
        + [whole((n_rows, LANES), (0, features // LANES)), part(n_rows)],
        out_specs=[part(shape[0])] * n_exp + [whole(row)] * 2,
        out_shape=[jax.ShapeDtypeStruct(shape, BF)] * n_exp + [jax.ShapeDtypeStruct(row, F32)] * 2,
        scratch_shapes=[pltpu.VMEM((shape[0] * n_exp, n_rows), BF)],
        compiler_params=params(VMEM_MIB),
        cost_estimate=cost(2 * shape[0] * n_exp * n_rows * width, 2 * n_exp * shape[0] * shape[1]),
        name="hub_blocks",
    )(*tables, hub, hub)
    return blocks, slot.T, weight.T


def column_block(k, member, n_tok, column):
    return column[pl.ds(pl.multiple_of((member[0] ^ k) * n_tok, n_tok), n_tok), :]


def slots_kernel(top, n_exp, cap, member, eye, theirs, before, start, spread, place, meta, out_hot, out_slot, out_weight):
    n_tok = before.shape[0]
    parts = [column_block(k, member, n_tok, meta) for k in range(n_exp)]
    named, out_weight[...] = named_here(top, eye, jnp.concatenate(parts, axis=0), theirs)
    counts = [dot(named[:, at:at + n_tok].astype(BF), before[...]) for at in range(0, named.shape[1], n_tok)]
    rank = jnp.concatenate(counts, axis=1)
    out_slot[...] = jnp.where(named > 0.0, start[0:1, :] + rank, -1.0)
    rank = jnp.where(named > 0.0, rank, -1.0).astype(BF)
    size = spread.shape[0]
    for k in range(n_exp):
        hot = dot(spread[...], rank[:, n_tok * k:n_tok * (k + 1)]) == place[:, 0:1]
        out_hot[size * k:size * (k + 1), :] = jnp.where(hot, 1.0, 0.0).astype(BF)


def column_slots(meta, theirs, member, n_tok, top, cap):
    total = meta.shape[0]
    n_seq, n_exp = theirs.shape[0], total // n_tok
    before, block = lower_counts(n_tok, n_tok)
    start = jnp.broadcast_to((jnp.arange(total) // n_tok * cap).astype(F32), (8, total))
    at = jnp.arange(n_seq * cap)
    spread = (at[:, None] // cap == jnp.arange(n_seq)[None, :]).astype(BF)
    place = jnp.broadcast_to((at % cap).astype(F32)[:, None], (n_seq * cap, LANES))
    eye = jnp.eye(LANES, dtype=BF)
    shapes = (n_seq * n_exp * cap, n_tok), (n_seq, total), (n_seq, total)
    inputs = (eye, theirs, before, start, spread, place, meta)
    hot, slot, weight = pl.pallas_call(
        lambda *refs: slots_kernel(top, n_exp, cap, *refs),
        grid=(1,),
        in_specs=[pl.BlockSpec(memory_space=pltpu.SMEM)] + [whole(x.shape) for x in inputs],
        out_specs=[whole(shape) for shape in shapes],
        out_shape=[jax.ShapeDtypeStruct(shape, kind) for shape, kind in zip(shapes, (BF, F32, F32))],
        compiler_params=params(VMEM_MIB),
        cost_estimate=cost(4 * total * LANES * LANES, 2 * shapes[0][0] * n_tok),
        name="column_slots",
    )(member.reshape(1), *inputs)
    return hot, slot.T, weight.T


def rows_kernel(n_exp, member, table, hot, column, out):
    pairs, size = table.shape[:2]
    n_tok = hot.shape[1]
    blocks = []
    for k in range(n_exp):
        blocks.append(dot(hot[size * k:size * (k + 1), :], column_block(k, member, n_tok, column)).astype(BF))
    for i in range(pairs):
        window = jnp.concatenate([b[16 * i:16 * i + 32, :] for b in blocks], axis=0)
        out[size * i:size * (i + 1), :] = dot(table[i], window).astype(BF)


def column_rows(member, table, hot, column, n_exp):
    total, features = hot.shape[0], column.shape[1]
    wide = 1280 if features % 1280 == 0 else features
    part = lambda rows: pl.BlockSpec((rows, wide), lambda j: (0, j))
    return pl.pallas_call(
        lambda *refs: rows_kernel(n_exp, *refs),
        grid=(features // wide,),
        in_specs=[pl.BlockSpec(memory_space=pltpu.SMEM), whole(table.shape, (0, 0, 0)), whole(hot.shape),
                  part(column.shape[0])],
        out_specs=part(total),
        out_shape=jax.ShapeDtypeStruct((total, features), BF),
        compiler_params=params(VMEM_MIB),
        cost_estimate=cost(2 * total * hot.shape[1] * LANES, 2 * total * LANES),
        name="column_rows",
    )(member.reshape(1), table, hot, column)


def column_kernel(n_exp, place, spread, slot, weight, got, out_mine, out_first, out_last, mixed):
    n_tok = out_mine.shape[0] // (n_exp // 2)

    @pl.when(pl.program_id(0) == 0)
    def _():
        hot = dot(slot[...], spread[...]) == place[0:1, :]
        mixed[...] = jnp.where(hot, dot(weight[...], spread[...]), 0.0).astype(BF)

    sums = dot(mixed[...], got[...])
    for k in range(0, n_exp, 2):
        at = slice(n_tok * k // 2, n_tok * (k // 2 + 1))
        out_mine[at, :] = sums[n_tok * k:n_tok * (k + 1), :]
        out, at = (out_first, k) if 2 * k < n_exp else (out_last, k - n_exp // 2)
        out[n_tok * at // 2:n_tok * (at // 2 + 1), :] = sums[n_tok * (k + 1):n_tok * (k + 2), :].astype(BF)


def column_sums(slot, weight, got, n_exp):
    n_rows, n_seq = slot.shape
    total, half = got.shape
    at = jnp.arange(total)
    place = jnp.broadcast_to((at % (total // n_seq)).astype(F32), (8, total))
    spread = (jnp.arange(n_seq)[:, None] == at[None, :] // (total // n_seq)).astype(BF)
    shape = (n_rows // 2, half)
    wide = 512 if half % 512 == 0 else half
    part = lambda rows: pl.BlockSpec((rows, wide), lambda j: (0, j))
    return pl.pallas_call(
        lambda *refs: column_kernel(n_exp, *refs),
        grid=(half // wide,),
        in_specs=[whole(place.shape), whole(spread.shape), whole(slot.shape), whole(weight.shape), part(total)],
        out_specs=[part(shape[0])] + [part(shape[0] // 2)] * 2,
        out_shape=[jax.ShapeDtypeStruct(shape, F32)] + [jax.ShapeDtypeStruct((shape[0] // 2, half), BF)] * 2,
        scratch_shapes=[pltpu.VMEM((n_rows, total), BF)],
        compiler_params=params(VMEM_MIB),
        cost_estimate=cost(400 * n_rows * total * half, 2 * total * half + 3 * n_rows * half),
        name="column_sums",
    )(place, spread, slot, weight, got)


def per_device(hidden_in, grad_out, expert_ids, gate_weights, w_gate, w_up, w_down):
    n_tok, features = hidden_in.shape
    top = expert_ids.shape[1]
    n_seq, n_exp = lax.axis_size("seq"), lax.axis_size("exp")
    group, member = lax.axis_index("seq"), lax.axis_index("exp")
    experts = n_seq * n_exp
    cap = 3 * top * n_tok // (2 * experts)
    per_group = top // 2 * n_tok // n_seq
    first = first_columns(features)
    rest = features - first
    gate_mat, up_mat, down_mat = w_gate[0], w_up[0], w_down[0]
    partner = member ^ jnp.arange(n_exp)
    to_b, to_a = window_tables(n_seq, n_exp, cap)

    meta = jnp.concatenate(
        (expert_ids.astype(BF), gate_weights.astype(BF), jnp.zeros((n_tok, LANES - 2 * top), BF)), axis=1)

    column_meta = lax.all_gather(meta, "exp", axis=0, tiled=True)
    column = lax.all_gather(grad_out, "exp", axis=0, tiled=True)
    theirs = jnp.broadcast_to((jnp.arange(n_seq) * n_exp + member).astype(F32)[:, None], (n_seq, LANES))
    put_b, slot_b, weight_b = column_slots(column_meta, theirs, member, n_tok, top, cap)
    slot_b, weight_b = slot_b.astype(BF), weight_b.astype(BF)
    local = jnp.broadcast_to((partner + group * n_exp).astype(F32)[:, None], (n_exp, LANES))
    tables = (jnp.eye(LANES, dtype=BF), local) + lower_counts(n_seq * per_group, per_group)
    put_b, to_b, to_a, slot_b, weight_b, *tables = barrier(put_b, to_b, to_a, slot_b, weight_b, *tables)
    send_b = column_rows(member, to_b, put_b, column, n_exp)

    group_ids = expert_ids // n_exp
    in_group = jnp.any(group_ids[:, :, None] == jnp.arange(n_seq)[None, None, :], axis=1)
    group_rank = earlier_counts(in_group).T
    pick = (group_rank[:, None, :] == jnp.arange(per_group, dtype=F32)[None, :, None])
    pick = pick.astype(BF).reshape(n_seq * per_group, n_tok)
    send = dot(pick, jnp.concatenate((hidden_in, meta), axis=1)).astype(BF)
    hub = lax.all_to_all(send.reshape(n_seq, per_group, features + LANES), "seq", 0, 0, tiled=True)
    hub = hub.reshape(n_seq * per_group, features + LANES)
    hub, send_b = barrier(hub, send_b)

    rows_b = n_exp * cap
    recv_b = lax.all_to_all(send_b.reshape(n_seq, rows_b, features), "seq", 0, 0, tiled=True)
    recv_b = recv_b.reshape(n_seq * rows_b, features)

    blocks, slot_a, weight_a = hub_blocks(hub, tables, per_group, top, cap)
    rows_in = exchange(blocks)

    pre_gate, pre_up = pre_products(to_b, rows_in, gate_mat, up_mat)
    lane = jnp.broadcast_to((jnp.arange(LANES) == group * n_exp + member).astype(F32), (8, LANES))
    grad_gate, grad_up, gate_dot, back_b = hidden_grads(lane, recv_b, down_mat, pre_gate, pre_up, gate_mat, up_mat)

    back_a = returned_a(to_a, grad_gate, grad_up, gate_mat, up_mat, gate_dot, n_exp)
    got_a = exchange(back_a)
    got_b = lax.all_to_all(back_b.reshape(n_seq, rows_b, rest), "seq", 0, 0, tiled=True)
    got_b, *got_a = barrier(got_b, *got_a)
    mine, *other = column_sums(slot_b, weight_b, got_b.reshape(n_seq * rows_b, rest), n_exp)
    back, *chip = group_sums(slot_a, weight_a, mine, *(swap(x, 1) for x in other), got_a)
    final_b = sum(p.astype(F32) for p in exchange(chip, 2))
    back = lax.all_to_all(back.reshape(n_seq, per_group, first + LANES), "seq", 0, 0, tiled=True)
    final_a = dot_t(pick, back.reshape(n_seq * per_group, first + LANES))

    grad_in = jnp.concatenate((final_a[:, :first], final_b), axis=1).astype(BF)
    table = final_a[:, first:]
    chosen = expert_ids[:, :, None] == jnp.arange(experts)[None, None, :]
    grad_gates = jnp.sum(jnp.where(chosen, table[:, None, :experts], 0.0), axis=2).astype(BF)
    return grad_in, grad_gates


def solution(mesh):
    rows, mats = P(("seq", "exp"), None), P(("seq", "exp"), None, None)
    return jax.shard_map(
        per_device, mesh=mesh, in_specs=(rows,) * 4 + (mats,) * 3, out_specs=(rows, rows), check_vma=False
    )
```

```python
import jax
import jax.numpy as jnp
from jax import lax
from jax.experimental import pallas as pl
from jax.experimental.pallas import tpu as pltpu
from jax.sharding import PartitionSpec as P

BF = jnp.bfloat16
F32 = jnp.float32
LANES = 128
VMEM_MIB = 60


def dot(a, b):
    return jnp.dot(a, b, preferred_element_type=F32)


def dot_t(a, b):
    return lax.dot_general(a, b, (((0,), (0,)), ((), ())), preferred_element_type=F32)


def dot_nt(a, b):
    return lax.dot_general(a, b, (((1,), (1,)), ((), ())), preferred_element_type=F32)


def earlier_counts(names):
    n = names.shape[-2]
    lower = (jnp.arange(n)[:, None] > jnp.arange(n)[None, :]).astype(BF)
    counts = jnp.einsum("ij,...jm->...im", lower, names.astype(BF), preferred_element_type=F32)
    return jnp.where(names, counts, -1.0)


def first_columns(features):
    return max(2 * features // 5 // 256 * 256, 256)


def barrier(*values):
    return lax.optimization_barrier(values)


def swap(x, k):
    return lax.ppermute(x, "exp", [(i, i ^ k) for i in range(lax.axis_size("exp"))])


def exchange(blocks, step=1):
    return [blocks[0]] + [swap(block, step * k) for k, block in enumerate(blocks) if k]


def whole(shape, at=(0, 0)):
    return pl.BlockSpec(shape, lambda *_: at, pipeline_mode=pl.Buffered(1))


def params(mib):
    return pltpu.CompilerParams(vmem_limit_bytes=mib * 2**20)


def cost(flops, nbytes):
    return pl.CostEstimate(flops=flops, bytes_accessed=nbytes, transcendentals=0)


def window_tables(n_seq, n_exp, cap):
    pair = 2 * n_exp * cap
    d = jnp.arange(pair)
    source = d % (n_exp * cap) // cap * 32 + d // (n_exp * cap) * cap + d % cap
    i = jnp.arange(n_seq // 2)
    at = source[None, :] + (2 * cap - 16) * i[:, None]
    wide = jnp.arange(32 * n_exp)
    to_b = (at[:, :, None] == wide[None, None, :]).astype(BF)
    to_a = (at[:, None, :] == wide[None, :, None]).astype(BF)
    return to_b, to_a


def pre_kernel(n_exp, pairs, table, *refs):
    blocks, (gate, up, out_gate, out_up, rows) = refs[:n_exp], refs[n_exp:]
    size = table.shape[1]

    @pl.when(pl.program_id(0) == 0)
    def _():
        for i in range(pairs):
            window = jnp.concatenate([b[16 * i:16 * i + 32, :] for b in blocks], axis=0)
            rows[size * i:size * (i + 1), :] = dot(table[i], window).astype(BF)

    out_gate[...] = dot(rows[...], gate[...])
    out_up[...] = dot(rows[...], up[...])


def pre_products(table, blocks, gate_mat, up_mat):
    chips, pairs = len(blocks), table.shape[0]
    rows, features = blocks[0].shape
    total, units = rows * chips, gate_mat.shape[1]
    wide = 256 if units % 256 == 0 else units
    column = pl.BlockSpec((features, wide), lambda j: (0, j))
    result = pl.BlockSpec((total, wide), lambda j: (0, j))
    return pl.pallas_call(
        lambda *refs: pre_kernel(chips, pairs, *refs),
        grid=(units // wide,),
        in_specs=[whole(table.shape, (0, 0, 0))] + [whole((rows, features))] * chips + [column, column],
        out_specs=[result, result],
        out_shape=[jax.ShapeDtypeStruct((total, units), F32)] * 2,
        scratch_shapes=[pltpu.VMEM((total, features), BF)],
        compiler_params=params(VMEM_MIB),
        cost_estimate=cost(4 * total * features * units, 2 * total * features + 4 * features * units + 8 * total * units),
        name="pre_products",
    )(table, *blocks, gate_mat, up_mat)


def grad_kernel(steps, lane, grad, down, pre_gate, pre_up, gate_mat, up_mat, out_gate, out_up, out_dot, out, all_gate, all_up):
    i = pl.program_id(0)
    tall = grad.shape[0]

    @pl.when(i < steps)
    def _():
        grad_hidden = dot_nt(grad[...], down[...])
        gate, up = pre_gate[...], pre_up[...]
        sigmoid = jax.nn.sigmoid(gate)
        active = gate * sigmoid
        hidden = (active * up).astype(BF).astype(F32)
        gate_dot = jnp.sum(hidden * grad_hidden, axis=1, keepdims=True)
        out_dot[...] = (gate_dot * lane[0:1, :]).astype(BF)
        rows = pl.ds(pl.multiple_of(i * tall, tall), tall)
        grad_gate = (grad_hidden * up * sigmoid * (1.0 + gate * (1.0 - sigmoid))).astype(BF)
        grad_up = (grad_hidden * active).astype(BF)
        out_gate[...] = grad_gate
        out_up[...] = grad_up
        all_gate[rows, :] = grad_gate
        all_up[rows, :] = grad_up

    @pl.when(i >= steps)
    def _():
        out[...] = (dot_nt(all_gate[...], gate_mat[...]) + dot_nt(all_up[...], up_mat[...])).astype(BF)


def hidden_grads(lane, rows_grad, down_mat, pre_gate, pre_up, gate_mat, up_mat):
    total, features = rows_grad.shape
    units, first, steps = down_mat.shape[0], first_columns(features), 4
    half = features - first
    tall = total // steps
    wide = 512 if half % 512 == 0 else half
    row = lambda width: pl.BlockSpec((tall, width), lambda i: (jnp.minimum(i, steps - 1), 0))
    mat = pl.BlockSpec((wide, units), lambda i: (first // wide + jnp.maximum(i - steps, 0), 0))
    return pl.pallas_call(
        lambda *refs: grad_kernel(steps, *refs),
        grid=(steps + half // wide,),
        in_specs=[whole(lane.shape), row(features), whole(down_mat.shape), row(units), row(units), mat, mat],
        out_specs=[row(units), row(units), row(LANES),
                   pl.BlockSpec((total, wide), lambda i: (0, jnp.maximum(i - steps, 0)))],
        out_shape=[jax.ShapeDtypeStruct((total, units), BF)] * 2
        + [jax.ShapeDtypeStruct((total, LANES), BF), jax.ShapeDtypeStruct((total, half), BF)],
        scratch_shapes=[pltpu.VMEM((total, units), BF)] * 2,
        compiler_params=params(VMEM_MIB),
        cost_estimate=cost(4 * total * features * units, 4 * total * features + 4 * features * units + 12 * total * units),
        name="hidden_grads",
    )(lane, rows_grad, down_mat, pre_gate, pre_up, gate_mat, up_mat)


def back_a_kernel(n_exp, pairs, table, grad_gate, grad_up, gate, up, gate_dot, *outs):
    wide = gate.shape[0]
    half = outs[0].shape[1] - LANES
    size = table.shape[2]

    def reorder(values, start, width):
        before = None
        for i in range(pairs):
            moved = dot(table[i], values[size * i:size * (i + 1), :])
            for k in range(n_exp):
                part = moved[32 * k:32 * k + 16, :]
                if before is not None:
                    part = part + before[32 * k + 16:32 * k + 32, :]
                outs[k][16 * i:16 * i + 16, pl.ds(start, width)] = part.astype(BF)
            before = moved
        for k in range(n_exp):
            part = before[32 * k + 16:32 * k + 32, :]
            outs[k][16 * pairs:16 * pairs + 16, pl.ds(start, width)] = part.astype(BF)

    j = pl.program_id(0)
    values = dot_nt(grad_gate[...], gate[...]) + dot_nt(grad_up[...], up[...])
    reorder(values.astype(BF), pl.multiple_of(j * wide, wide), wide)

    @pl.when(j == 0)
    def _():
        reorder(gate_dot[...], half, LANES)


def returned_a(table, grad_gate, grad_up, gate_mat, up_mat, gate_dot, n_exp):
    total, units = grad_gate.shape
    half = first_columns(gate_mat.shape[0])
    pairs = table.shape[0]
    wide = 512 if half % 512 == 0 else half
    mat = pl.BlockSpec((wide, units), lambda j: (j, 0))
    block = (total // n_exp, half + LANES)
    return pl.pallas_call(
        lambda *refs: back_a_kernel(n_exp, pairs, *refs),
        grid=(half // wide,),
        in_specs=[whole(table.shape, (0, 0, 0)), whole(grad_gate.shape), whole(grad_up.shape), mat, mat, whole(gate_dot.shape)],
        out_specs=[whole(block)] * n_exp,
        out_shape=[jax.ShapeDtypeStruct(block, BF)] * n_exp,
        compiler_params=params(VMEM_MIB),
        cost_estimate=cost(4 * total * half * units, 4 * half * units + 4 * total * units + 2 * total * half),
        name="returned_a",
    )(table, grad_gate, grad_up, gate_mat, up_mat, gate_dot)


def sum_kernel(n_exp, slot, weight, *refs):
    blocks, out = refs[:n_exp], refs[n_exp]
    half = out.shape[1] - LANES
    place = lax.broadcasted_iota(jnp.int32, (slot.shape[0], blocks[0].shape[0]), 1).astype(F32)
    sums = jnp.zeros((slot.shape[0], half), F32)
    gates = jnp.zeros((slot.shape[0], LANES), F32)
    for k in range(n_exp):
        hot = slot[:, k:k + 1] == place
        sums += dot(jnp.where(hot, weight[:, k:k + 1], 0.0).astype(BF), blocks[k][:, :half])
        gates += dot(jnp.where(hot, 1.0, 0.0).astype(BF), blocks[k][:, half:])
    out[:, :half] = sums.astype(BF)
    out[:, half:] = gates.astype(BF)


def group_sums(slot, weight, blocks):
    n_exp = len(blocks)
    shape = (slot.shape[0], blocks[0].shape[1])
    return pl.pallas_call(
        lambda *refs: sum_kernel(n_exp, *refs),
        grid=(1,),
        in_specs=[whole(slot.shape), whole(weight.shape)] + [whole(blocks[0].shape)] * n_exp,
        out_specs=whole(shape),
        out_shape=jax.ShapeDtypeStruct(shape, BF),
        compiler_params=params(VMEM_MIB),
        cost_estimate=cost(2 * shape[0] * blocks[0].size * n_exp, 2 * n_exp * blocks[0].size),
        name="group_sums",
    )(slot, weight, *blocks)


def named_here(top, eye, meta, local):
    flat = dot_nt(eye[...], meta)
    named = weight = jnp.zeros((local.shape[0], flat.shape[1]), F32)
    for k in range(top):
        hit = flat[k:k + 1, :] == local[:, 0:1]
        named += jnp.where(hit, 1.0, 0.0)
        weight += jnp.where(hit, flat[top + k:top + k + 1, :], 0.0)
    return named, weight


def hub_kernel(top, cap, eye, local, before, block, meta, hub, *outs):
    *blocks, out_slot, out_weight, puts = outs
    rows, n_rows = blocks[0].shape[0], hub.shape[0]

    @pl.when(pl.program_id(0) == 0)
    def _():
        named, out_weight[...] = named_here(top, eye, meta[...], local)
        slot = jnp.where(named > 0.0, block[0:1, :] * cap + dot(named.astype(BF), before[...]), -1.0)
        out_slot[...] = slot
        place = lax.broadcasted_iota(jnp.int32, (rows, n_rows), 0).astype(F32)
        for k in range(len(blocks)):
            puts[rows * k:rows * (k + 1), :] = jnp.where(place == slot[k:k + 1, :], 1.0, 0.0).astype(BF)

    placed = dot(puts[...], hub[...]).astype(BF)
    for k, out in enumerate(blocks):
        out[...] = placed[rows * k:rows * (k + 1), :]


def lower_counts(total, size):
    at = jnp.arange(total)
    same = at[:, None] // size == at[None, :] // size
    return (same & (at[:, None] < at[None, :])).astype(BF), jnp.broadcast_to((at // size).astype(F32), (8, total))


def hub_blocks(hub, tables, per_group, top, cap):
    n_rows, width = hub.shape
    n_exp = tables[1].shape[0]
    features = width - LANES
    wide = 1280 if features % 1280 == 0 else features
    shape = (n_rows // per_group * cap, features)
    row = (n_exp, n_rows)
    part = lambda rows: pl.BlockSpec((rows, wide), lambda j: (0, j))
    *blocks, slot, weight = pl.pallas_call(
        lambda *refs: hub_kernel(top, cap, *refs),
        grid=(features // wide,),
        in_specs=[whole(x.shape) for x in tables]
        + [whole((n_rows, LANES), (0, features // LANES)), part(n_rows)],
        out_specs=[part(shape[0])] * n_exp + [whole(row)] * 2,
        out_shape=[jax.ShapeDtypeStruct(shape, BF)] * n_exp + [jax.ShapeDtypeStruct(row, F32)] * 2,
        scratch_shapes=[pltpu.VMEM((shape[0] * n_exp, n_rows), BF)],
        compiler_params=params(VMEM_MIB),
        cost_estimate=cost(2 * shape[0] * n_exp * n_rows * width, 2 * n_exp * shape[0] * shape[1]),
        name="hub_blocks",
    )(*tables, hub, hub)
    return blocks, slot.T, weight.T


def column_block(k, member, n_tok, column):
    return column[pl.ds(pl.multiple_of((member[0] ^ k) * n_tok, n_tok), n_tok), :]


def slots_kernel(top, n_exp, cap, member, eye, theirs, before, start, spread, place, meta, out_hot, out_slot, out_weight):
    n_tok = before.shape[0]
    parts = [column_block(k, member, n_tok, meta) for k in range(n_exp)]
    named, out_weight[...] = named_here(top, eye, jnp.concatenate(parts, axis=0), theirs)
    counts = [dot(named[:, at:at + n_tok].astype(BF), before[...]) for at in range(0, named.shape[1], n_tok)]
    rank = jnp.concatenate(counts, axis=1)
    out_slot[...] = jnp.where(named > 0.0, start[0:1, :] + rank, -1.0)
    rank = jnp.where(named > 0.0, rank, -1.0).astype(BF)
    size = spread.shape[0]
    for k in range(n_exp):
        hot = dot(spread[...], rank[:, n_tok * k:n_tok * (k + 1)]) == place[:, 0:1]
        out_hot[size * k:size * (k + 1), :] = jnp.where(hot, 1.0, 0.0).astype(BF)


def column_slots(meta, theirs, member, n_tok, top, cap):
    total = meta.shape[0]
    n_seq, n_exp = theirs.shape[0], total // n_tok
    before, block = lower_counts(n_tok, n_tok)
    start = jnp.broadcast_to((jnp.arange(total) // n_tok * cap).astype(F32), (8, total))
    at = jnp.arange(n_seq * cap)
    spread = (at[:, None] // cap == jnp.arange(n_seq)[None, :]).astype(BF)
    place = jnp.broadcast_to((at % cap).astype(F32)[:, None], (n_seq * cap, LANES))
    eye = jnp.eye(LANES, dtype=BF)
    shapes = (n_seq * n_exp * cap, n_tok), (n_seq, total), (n_seq, total)
    inputs = (eye, theirs, before, start, spread, place, meta)
    hot, slot, weight = pl.pallas_call(
        lambda *refs: slots_kernel(top, n_exp, cap, *refs),
        grid=(1,),
        in_specs=[pl.BlockSpec(memory_space=pltpu.SMEM)] + [whole(x.shape) for x in inputs],
        out_specs=[whole(shape) for shape in shapes],
        out_shape=[jax.ShapeDtypeStruct(shape, kind) for shape, kind in zip(shapes, (BF, F32, F32))],
        compiler_params=params(VMEM_MIB),
        cost_estimate=cost(4 * total * LANES * LANES, 2 * shapes[0][0] * n_tok),
        name="column_slots",
    )(member.reshape(1), *inputs)
    return hot, slot.T, weight.T


def rows_kernel(n_exp, member, table, hot, column, out):
    pairs, size = table.shape[:2]
    n_tok = hot.shape[1]
    blocks = []
    for k in range(n_exp):
        blocks.append(dot(hot[size * k:size * (k + 1), :], column_block(k, member, n_tok, column)).astype(BF))
    for i in range(pairs):
        window = jnp.concatenate([b[16 * i:16 * i + 32, :] for b in blocks], axis=0)
        out[size * i:size * (i + 1), :] = dot(table[i], window).astype(BF)


def column_rows(member, table, hot, column, n_exp):
    total, features = hot.shape[0], column.shape[1]
    wide = 1280 if features % 1280 == 0 else features
    part = lambda rows: pl.BlockSpec((rows, wide), lambda j: (0, j))
    return pl.pallas_call(
        lambda *refs: rows_kernel(n_exp, *refs),
        grid=(features // wide,),
        in_specs=[pl.BlockSpec(memory_space=pltpu.SMEM), whole(table.shape, (0, 0, 0)), whole(hot.shape),
                  part(column.shape[0])],
        out_specs=part(total),
        out_shape=jax.ShapeDtypeStruct((total, features), BF),
        compiler_params=params(VMEM_MIB),
        cost_estimate=cost(2 * total * hot.shape[1] * LANES, 2 * total * LANES),
        name="column_rows",
    )(member.reshape(1), table, hot, column)


def column_kernel(n_exp, place, spread, slot, weight, got, out_mine, out_first, out_last, mixed):
    n_tok = out_mine.shape[0] // (n_exp // 2)

    @pl.when(pl.program_id(0) == 0)
    def _():
        hot = dot(slot[...], spread[...]) == place[0:1, :]
        mixed[...] = jnp.where(hot, dot(weight[...], spread[...]), 0.0).astype(BF)

    sums = dot(mixed[...], got[...])
    for k in range(0, n_exp, 2):
        at = slice(n_tok * k // 2, n_tok * (k // 2 + 1))
        out_mine[at, :] = sums[n_tok * k:n_tok * (k + 1), :]
        out, at = (out_first, k) if 2 * k < n_exp else (out_last, k - n_exp // 2)
        out[n_tok * at // 2:n_tok * (at // 2 + 1), :] = sums[n_tok * (k + 1):n_tok * (k + 2), :].astype(BF)


def column_sums(slot, weight, got, n_exp):
    n_rows, n_seq = slot.shape
    total, half = got.shape
    at = jnp.arange(total)
    place = jnp.broadcast_to((at % (total // n_seq)).astype(F32), (8, total))
    spread = (jnp.arange(n_seq)[:, None] == at[None, :] // (total // n_seq)).astype(BF)
    shape = (n_rows // 2, half)
    wide = 512 if half % 512 == 0 else half
    part = lambda rows: pl.BlockSpec((rows, wide), lambda j: (0, j))
    return pl.pallas_call(
        lambda *refs: column_kernel(n_exp, *refs),
        grid=(half // wide,),
        in_specs=[whole(place.shape), whole(spread.shape), whole(slot.shape), whole(weight.shape), part(total)],
        out_specs=[part(shape[0])] + [part(shape[0] // 2)] * 2,
        out_shape=[jax.ShapeDtypeStruct(shape, F32)] + [jax.ShapeDtypeStruct((shape[0] // 2, half), BF)] * 2,
        scratch_shapes=[pltpu.VMEM((n_rows, total), BF)],
        compiler_params=params(VMEM_MIB),
        cost_estimate=cost(400 * n_rows * total * half, 2 * total * half + 3 * n_rows * half),
        name="column_sums",
    )(place, spread, slot, weight, got)


def per_device(hidden_in, grad_out, expert_ids, gate_weights, w_gate, w_up, w_down):
    n_tok, features = hidden_in.shape
    top = expert_ids.shape[1]
    n_seq, n_exp = lax.axis_size("seq"), lax.axis_size("exp")
    group, member = lax.axis_index("seq"), lax.axis_index("exp")
    experts = n_seq * n_exp
    cap = 3 * top * n_tok // (2 * experts)
    per_group = top // 2 * n_tok // n_seq
    first = first_columns(features)
    rest = features - first
    gate_mat, up_mat, down_mat = w_gate[0], w_up[0], w_down[0]
    partner = member ^ jnp.arange(n_exp)
    to_b, to_a = window_tables(n_seq, n_exp, cap)

    meta = jnp.concatenate(
        (expert_ids.astype(BF), gate_weights.astype(BF), jnp.zeros((n_tok, LANES - 2 * top), BF)), axis=1)

    column_meta = lax.all_gather(meta, "exp", axis=0, tiled=True)
    column = lax.all_gather(grad_out, "exp", axis=0, tiled=True)
    theirs = jnp.broadcast_to((jnp.arange(n_seq) * n_exp + member).astype(F32)[:, None], (n_seq, LANES))
    put_b, slot_b, weight_b = column_slots(column_meta, theirs, member, n_tok, top, cap)
    slot_b, weight_b = slot_b.astype(BF), weight_b.astype(BF)
    local = jnp.broadcast_to((partner + group * n_exp).astype(F32)[:, None], (n_exp, LANES))
    tables = (jnp.eye(LANES, dtype=BF), local) + lower_counts(n_seq * per_group, per_group)
    put_b, to_b, to_a, slot_b, weight_b, *tables = barrier(put_b, to_b, to_a, slot_b, weight_b, *tables)
    send_b = column_rows(member, to_b, put_b, column, n_exp)

    group_ids = expert_ids // n_exp
    in_group = jnp.any(group_ids[:, :, None] == jnp.arange(n_seq)[None, None, :], axis=1)
    group_rank = earlier_counts(in_group).T
    pick = (group_rank[:, None, :] == jnp.arange(per_group, dtype=F32)[None, :, None])
    pick = pick.astype(BF).reshape(n_seq * per_group, n_tok)
    send = dot(pick, jnp.concatenate((hidden_in, meta), axis=1)).astype(BF)
    hub = lax.all_to_all(send.reshape(n_seq, per_group, features + LANES), "seq", 0, 0, tiled=True)
    hub = hub.reshape(n_seq * per_group, features + LANES)
    hub, send_b = barrier(hub, send_b)

    rows_b = n_exp * cap
    recv_b = lax.all_to_all(send_b.reshape(n_seq, rows_b, features), "seq", 0, 0, tiled=True)
    recv_b = recv_b.reshape(n_seq * rows_b, features)

    blocks, slot_a, weight_a = hub_blocks(hub, tables, per_group, top, cap)
    rows_in = exchange(blocks)

    pre_gate, pre_up = pre_products(to_b, rows_in, gate_mat, up_mat)
    lane = jnp.broadcast_to((jnp.arange(LANES) == group * n_exp + member).astype(F32), (8, LANES))
    grad_gate, grad_up, gate_dot, back_b = hidden_grads(lane, recv_b, down_mat, pre_gate, pre_up, gate_mat, up_mat)

    back_a = returned_a(to_a, grad_gate, grad_up, gate_mat, up_mat, gate_dot, n_exp)
    got_a = exchange(back_a)
    got_b = lax.all_to_all(back_b.reshape(n_seq, rows_b, rest), "seq", 0, 0, tiled=True)
    back = group_sums(slot_a, weight_a, got_a)
    got_b, back = barrier(got_b, back)
    mine, *other = column_sums(slot_b, weight_b, got_b.reshape(n_seq * rows_b, rest), n_exp)
    back, *other = barrier(back, *other)
    other = jnp.split(jnp.concatenate([swap(x, 1) for x in other], axis=0), n_exp // 2)
    chip = [(x + y.astype(F32)).astype(BF) for x, y in zip(jnp.split(mine, n_exp // 2), other)]
    final_b = sum(p.astype(F32) for p in exchange(chip, 2))
    back = lax.all_to_all(back.reshape(n_seq, per_group, first + LANES), "seq", 0, 0, tiled=True)
    final_a = dot_t(pick, back.reshape(n_seq * per_group, first + LANES))

    grad_in = jnp.concatenate((final_a[:, :first], final_b), axis=1).astype(BF)
    table = final_a[:, first:]
    chosen = expert_ids[:, :, None] == jnp.arange(experts)[None, None, :]
    grad_gates = jnp.sum(jnp.where(chosen, table[:, None, :experts], 0.0), axis=2).astype(BF)
    return grad_in, grad_gates


def solution(mesh):
    rows, mats = P(("seq", "exp"), None), P(("seq", "exp"), None, None)
    return jax.shard_map(
        per_device, mesh=mesh, in_specs=(rows,) * 4 + (mats,) * 3, out_specs=(rows, rows), check_vma=False
    )
```

```python
import jax
import jax.numpy as jnp
from jax import lax
from jax.experimental import pallas as pl
from jax.experimental.pallas import tpu as pltpu
from jax.sharding import PartitionSpec as P

BF = jnp.bfloat16
F32 = jnp.float32
LANES = 128
VMEM_MIB = 60


def dot(a, b):
    return jnp.dot(a, b, preferred_element_type=F32)


def dot_t(a, b):
    return lax.dot_general(a, b, (((0,), (0,)), ((), ())), preferred_element_type=F32)


def dot_nt(a, b):
    return lax.dot_general(a, b, (((1,), (1,)), ((), ())), preferred_element_type=F32)


def earlier_counts(names):
    n = names.shape[-2]
    lower = (jnp.arange(n)[:, None] > jnp.arange(n)[None, :]).astype(BF)
    counts = jnp.einsum("ij,...jm->...im", lower, names.astype(BF), preferred_element_type=F32)
    return jnp.where(names, counts, -1.0)


def first_columns(features):
    return features // 2


def barrier(*values):
    return lax.optimization_barrier(values)


def swap(x, k):
    return lax.ppermute(x, "exp", [(i, i ^ k) for i in range(lax.axis_size("exp"))])


def exchange(blocks, step=1):
    return [blocks[0]] + [swap(block, step * k) for k, block in enumerate(blocks) if k]


def whole(shape, at=(0, 0)):
    return pl.BlockSpec(shape, lambda *_: at, pipeline_mode=pl.Buffered(1))


def params(mib):
    return pltpu.CompilerParams(vmem_limit_bytes=mib * 2**20)


def cost(flops, nbytes):
    return pl.CostEstimate(flops=flops, bytes_accessed=nbytes, transcendentals=0)


def window_tables(n_seq, n_exp, cap):
    pair = 2 * n_exp * cap
    d = jnp.arange(pair)
    source = d % (n_exp * cap) // cap * 32 + d // (n_exp * cap) * cap + d % cap
    i = jnp.arange(n_seq // 2)
    at = source[None, :] + (2 * cap - 16) * i[:, None]
    wide = jnp.arange(32 * n_exp)
    to_b = (at[:, :, None] == wide[None, None, :]).astype(BF)
    to_a = (at[:, None, :] == wide[None, :, None]).astype(BF)
    return to_b, to_a


def pre_kernel(n_exp, pairs, table, *refs):
    blocks, (gate, up, out_gate, out_up, rows) = refs[:n_exp], refs[n_exp:]
    size = table.shape[1]

    @pl.when(pl.program_id(0) == 0)
    def _():
        for i in range(pairs):
            window = jnp.concatenate([b[16 * i:16 * i + 32, :] for b in blocks], axis=0)
            rows[size * i:size * (i + 1), :] = dot(table[i], window).astype(BF)

    out_gate[...] = dot(rows[...], gate[...])
    out_up[...] = dot(rows[...], up[...])


def pre_products(table, blocks, gate_mat, up_mat):
    chips, pairs = len(blocks), table.shape[0]
    rows, features = blocks[0].shape
    total, units = rows * chips, gate_mat.shape[1]
    wide = 256 if units % 256 == 0 else units
    column = pl.BlockSpec((features, wide), lambda j: (0, j))
    result = pl.BlockSpec((total, wide), lambda j: (0, j))
    return pl.pallas_call(
        lambda *refs: pre_kernel(chips, pairs, *refs),
        grid=(units // wide,),
        in_specs=[whole(table.shape, (0, 0, 0))] + [whole((rows, features))] * chips + [column, column],
        out_specs=[result, result],
        out_shape=[jax.ShapeDtypeStruct((total, units), F32)] * 2,
        scratch_shapes=[pltpu.VMEM((total, features), BF)],
        compiler_params=params(VMEM_MIB),
        cost_estimate=cost(4 * total * features * units, 2 * total * features + 4 * features * units + 8 * total * units),
        name="pre_products",
    )(table, *blocks, gate_mat, up_mat)


def grad_kernel(steps, lane, grad, down, pre_gate, pre_up, gate_mat, up_mat, out_gate, out_up, out_dot, out, all_gate, all_up):
    i = pl.program_id(0)
    tall = grad.shape[0]

    @pl.when(i < steps)
    def _():
        grad_hidden = dot_nt(grad[...], down[...])
        gate, up = pre_gate[...], pre_up[...]
        sigmoid = jax.nn.sigmoid(gate)
        active = gate * sigmoid
        hidden = (active * up).astype(BF).astype(F32)
        gate_dot = jnp.sum(hidden * grad_hidden, axis=1, keepdims=True)
        out_dot[...] = (gate_dot * lane[0:1, :]).astype(BF)
        rows = pl.ds(pl.multiple_of(i * tall, tall), tall)
        grad_gate = (grad_hidden * up * sigmoid * (1.0 + gate * (1.0 - sigmoid))).astype(BF)
        grad_up = (grad_hidden * active).astype(BF)
        out_gate[...] = grad_gate
        out_up[...] = grad_up
        all_gate[rows, :] = grad_gate
        all_up[rows, :] = grad_up

    @pl.when(i >= steps)
    def _():
        out[...] = (dot_nt(all_gate[...], gate_mat[...]) + dot_nt(all_up[...], up_mat[...])).astype(BF)


def hidden_grads(lane, rows_grad, down_mat, pre_gate, pre_up, gate_mat, up_mat):
    total, features = rows_grad.shape
    units, first, steps = down_mat.shape[0], first_columns(features), 4
    half = features - first
    tall = total // steps
    wide = 640 if half % 640 == 0 else half
    row = lambda width: pl.BlockSpec((tall, width), lambda i: (jnp.minimum(i, steps - 1), 0))
    mat = pl.BlockSpec((wide, units), lambda i: (first // wide + jnp.maximum(i - steps, 0), 0))
    return pl.pallas_call(
        lambda *refs: grad_kernel(steps, *refs),
        grid=(steps + half // wide,),
        in_specs=[whole(lane.shape), row(features), whole(down_mat.shape), row(units), row(units), mat, mat],
        out_specs=[row(units), row(units), row(LANES),
                   pl.BlockSpec((total, wide), lambda i: (0, jnp.maximum(i - steps, 0)))],
        out_shape=[jax.ShapeDtypeStruct((total, units), BF)] * 2
        + [jax.ShapeDtypeStruct((total, LANES), BF), jax.ShapeDtypeStruct((total, half), BF)],
        scratch_shapes=[pltpu.VMEM((total, units), BF)] * 2,
        compiler_params=params(VMEM_MIB),
        cost_estimate=cost(4 * total * features * units, 4 * total * features + 4 * features * units + 12 * total * units),
        name="hidden_grads",
    )(lane, rows_grad, down_mat, pre_gate, pre_up, gate_mat, up_mat)


def back_a_kernel(n_exp, pairs, table, grad_gate, grad_up, gate, up, gate_dot, *outs):
    wide = gate.shape[0]
    half = outs[0].shape[1] - LANES
    size = table.shape[2]

    def reorder(values, start, width):
        before = None
        for i in range(pairs):
            moved = dot(table[i], values[size * i:size * (i + 1), :])
            for k in range(n_exp):
                part = moved[32 * k:32 * k + 16, :]
                if before is not None:
                    part = part + before[32 * k + 16:32 * k + 32, :]
                outs[k][16 * i:16 * i + 16, pl.ds(start, width)] = part.astype(BF)
            before = moved
        for k in range(n_exp):
            part = before[32 * k + 16:32 * k + 32, :]
            outs[k][16 * pairs:16 * pairs + 16, pl.ds(start, width)] = part.astype(BF)

    j = pl.program_id(0)
    values = dot_nt(grad_gate[...], gate[...]) + dot_nt(grad_up[...], up[...])
    reorder(values.astype(BF), pl.multiple_of(j * wide, wide), wide)

    @pl.when(j == 0)
    def _():
        reorder(gate_dot[...], half, LANES)


def returned_a(table, grad_gate, grad_up, gate_mat, up_mat, gate_dot, n_exp):
    total, units = grad_gate.shape
    half = first_columns(gate_mat.shape[0])
    pairs = table.shape[0]
    wide = 640 if half % 640 == 0 else half
    mat = pl.BlockSpec((wide, units), lambda j: (j, 0))
    block = (total // n_exp, half + LANES)
    return pl.pallas_call(
        lambda *refs: back_a_kernel(n_exp, pairs, *refs),
        grid=(half // wide,),
        in_specs=[whole(table.shape, (0, 0, 0)), whole(grad_gate.shape), whole(grad_up.shape), mat, mat, whole(gate_dot.shape)],
        out_specs=[whole(block)] * n_exp,
        out_shape=[jax.ShapeDtypeStruct(block, BF)] * n_exp,
        compiler_params=params(VMEM_MIB),
        cost_estimate=cost(4 * total * half * units, 4 * half * units + 4 * total * units + 2 * total * half),
        name="returned_a",
    )(table, grad_gate, grad_up, gate_mat, up_mat, gate_dot)


def sum_kernel(n_exp, slot, weight, *refs):
    blocks, out = refs[:n_exp], refs[n_exp]
    half = out.shape[1] - LANES
    place = lax.broadcasted_iota(jnp.int32, (slot.shape[0], blocks[0].shape[0]), 1).astype(F32)
    sums = jnp.zeros((slot.shape[0], half), F32)
    gates = jnp.zeros((slot.shape[0], LANES), F32)
    for k in range(n_exp):
        hot = slot[:, k:k + 1] == place
        sums += dot(jnp.where(hot, weight[:, k:k + 1], 0.0).astype(BF), blocks[k][:, :half])
        gates += dot(jnp.where(hot, 1.0, 0.0).astype(BF), blocks[k][:, half:])
    out[:, :half] = sums.astype(BF)
    out[:, half:] = gates.astype(BF)


def group_sums(slot, weight, blocks):
    n_exp = len(blocks)
    shape = (slot.shape[0], blocks[0].shape[1])
    return pl.pallas_call(
        lambda *refs: sum_kernel(n_exp, *refs),
        grid=(1,),
        in_specs=[whole(slot.shape), whole(weight.shape)] + [whole(blocks[0].shape)] * n_exp,
        out_specs=whole(shape),
        out_shape=jax.ShapeDtypeStruct(shape, BF),
        compiler_params=params(VMEM_MIB),
        cost_estimate=cost(2 * shape[0] * blocks[0].size * n_exp, 2 * n_exp * blocks[0].size),
        name="group_sums",
    )(slot, weight, *blocks)


def named_here(top, eye, meta, local):
    flat = dot_nt(eye[...], meta)
    named = weight = jnp.zeros((local.shape[0], flat.shape[1]), F32)
    for k in range(top):
        hit = flat[k:k + 1, :] == local[:, 0:1]
        named += jnp.where(hit, 1.0, 0.0)
        weight += jnp.where(hit, flat[top + k:top + k + 1, :], 0.0)
    return named, weight


def hub_kernel(top, cap, eye, local, before, block, meta, hub, *outs):
    *blocks, out_slot, out_weight, puts = outs
    rows, n_rows = blocks[0].shape[0], hub.shape[0]

    @pl.when(pl.program_id(0) == 0)
    def _():
        named, out_weight[...] = named_here(top, eye, meta[...], local)
        slot = jnp.where(named > 0.0, block[0:1, :] * cap + dot(named.astype(BF), before[...]), -1.0)
        out_slot[...] = slot
        place = lax.broadcasted_iota(jnp.int32, (rows, n_rows), 0).astype(F32)
        for k in range(len(blocks)):
            puts[rows * k:rows * (k + 1), :] = jnp.where(place == slot[k:k + 1, :], 1.0, 0.0).astype(BF)

    placed = dot(puts[...], hub[...]).astype(BF)
    for k, out in enumerate(blocks):
        out[...] = placed[rows * k:rows * (k + 1), :]


def lower_counts(total, size):
    at = jnp.arange(total)
    same = at[:, None] // size == at[None, :] // size
    return (same & (at[:, None] < at[None, :])).astype(BF), jnp.broadcast_to((at // size).astype(F32), (8, total))


def hub_blocks(hub, tables, per_group, top, cap):
    n_rows, width = hub.shape
    n_exp = tables[1].shape[0]
    features = width - LANES
    wide = 1280 if features % 1280 == 0 else features
    shape = (n_rows // per_group * cap, features)
    row = (n_exp, n_rows)
    part = lambda rows: pl.BlockSpec((rows, wide), lambda j: (0, j))
    *blocks, slot, weight = pl.pallas_call(
        lambda *refs: hub_kernel(top, cap, *refs),
        grid=(features // wide,),
        in_specs=[whole(x.shape) for x in tables]
        + [whole((n_rows, LANES), (0, features // LANES)), part(n_rows)],
        out_specs=[part(shape[0])] * n_exp + [whole(row)] * 2,
        out_shape=[jax.ShapeDtypeStruct(shape, BF)] * n_exp + [jax.ShapeDtypeStruct(row, F32)] * 2,
        scratch_shapes=[pltpu.VMEM((shape[0] * n_exp, n_rows), BF)],
        compiler_params=params(VMEM_MIB),
        cost_estimate=cost(2 * shape[0] * n_exp * n_rows * width, 2 * n_exp * shape[0] * shape[1]),
        name="hub_blocks",
    )(*tables, hub, hub)
    return blocks, slot.T, weight.T


def column_block(k, member, n_tok, column):
    return column[pl.ds(pl.multiple_of((member[0] ^ k) * n_tok, n_tok), n_tok), :]


def slots_kernel(top, n_exp, cap, member, eye, theirs, before, start, spread, place, meta, out_hot, out_slot, out_weight):
    n_tok = before.shape[0]
    parts = [column_block(k, member, n_tok, meta) for k in range(n_exp)]
    named, out_weight[...] = named_here(top, eye, jnp.concatenate(parts, axis=0), theirs)
    counts = [dot(named[:, at:at + n_tok].astype(BF), before[...]) for at in range(0, named.shape[1], n_tok)]
    rank = jnp.concatenate(counts, axis=1)
    out_slot[...] = jnp.where(named > 0.0, start[0:1, :] + rank, -1.0)
    rank = jnp.where(named > 0.0, rank, -1.0).astype(BF)
    size = spread.shape[0]
    for k in range(n_exp):
        hot = dot(spread[...], rank[:, n_tok * k:n_tok * (k + 1)]) == place[:, 0:1]
        out_hot[size * k:size * (k + 1), :] = jnp.where(hot, 1.0, 0.0).astype(BF)


def column_slots(meta, theirs, member, n_tok, top, cap):
    total = meta.shape[0]
    n_seq, n_exp = theirs.shape[0], total // n_tok
    before, block = lower_counts(n_tok, n_tok)
    start = jnp.broadcast_to((jnp.arange(total) // n_tok * cap).astype(F32), (8, total))
    at = jnp.arange(n_seq * cap)
    spread = (at[:, None] // cap == jnp.arange(n_seq)[None, :]).astype(BF)
    place = jnp.broadcast_to((at % cap).astype(F32)[:, None], (n_seq * cap, LANES))
    eye = jnp.eye(LANES, dtype=BF)
    shapes = (n_seq * n_exp * cap, n_tok), (n_seq, total), (n_seq, total)
    inputs = (eye, theirs, before, start, spread, place, meta)
    hot, slot, weight = pl.pallas_call(
        lambda *refs: slots_kernel(top, n_exp, cap, *refs),
        grid=(1,),
        in_specs=[pl.BlockSpec(memory_space=pltpu.SMEM)] + [whole(x.shape) for x in inputs],
        out_specs=[whole(shape) for shape in shapes],
        out_shape=[jax.ShapeDtypeStruct(shape, kind) for shape, kind in zip(shapes, (BF, F32, F32))],
        compiler_params=params(VMEM_MIB),
        cost_estimate=cost(4 * total * LANES * LANES, 2 * shapes[0][0] * n_tok),
        name="column_slots",
    )(member.reshape(1), *inputs)
    return hot, slot.T, weight.T


def rows_kernel(n_exp, member, table, hot, column, out):
    pairs, size = table.shape[:2]
    n_tok = hot.shape[1]
    blocks = []
    for k in range(n_exp):
        blocks.append(dot(hot[size * k:size * (k + 1), :], column_block(k, member, n_tok, column)).astype(BF))
    for i in range(pairs):
        window = jnp.concatenate([b[16 * i:16 * i + 32, :] for b in blocks], axis=0)
        out[size * i:size * (i + 1), :] = dot(table[i], window).astype(BF)


def column_rows(member, table, hot, column, n_exp):
    total, features = hot.shape[0], column.shape[1]
    wide = 1280 if features % 1280 == 0 else features
    part = lambda rows: pl.BlockSpec((rows, wide), lambda j: (0, j))
    return pl.pallas_call(
        lambda *refs: rows_kernel(n_exp, *refs),
        grid=(features // wide,),
        in_specs=[pl.BlockSpec(memory_space=pltpu.SMEM), whole(table.shape, (0, 0, 0)), whole(hot.shape),
                  part(column.shape[0])],
        out_specs=part(total),
        out_shape=jax.ShapeDtypeStruct((total, features), BF),
        compiler_params=params(VMEM_MIB),
        cost_estimate=cost(2 * total * hot.shape[1] * LANES, 2 * total * LANES),
        name="column_rows",
    )(member.reshape(1), table, hot, column)


def column_kernel(n_exp, place, spread, slot, weight, got, out_mine, out_first, out_last, mixed):
    n_tok = out_mine.shape[0] // (n_exp // 2)

    @pl.when(pl.program_id(0) == 0)
    def _():
        hot = dot(slot[...], spread[...]) == place[0:1, :]
        mixed[...] = jnp.where(hot, dot(weight[...], spread[...]), 0.0).astype(BF)

    sums = dot(mixed[...], got[...])
    for k in range(0, n_exp, 2):
        at = slice(n_tok * k // 2, n_tok * (k // 2 + 1))
        out_mine[at, :] = sums[n_tok * k:n_tok * (k + 1), :].astype(BF)
        out, at = (out_first, k) if 2 * k < n_exp else (out_last, k - n_exp // 2)
        out[n_tok * at // 2:n_tok * (at // 2 + 1), :] = sums[n_tok * (k + 1):n_tok * (k + 2), :].astype(BF)


def column_sums(slot, weight, got, n_exp):
    n_rows, n_seq = slot.shape
    total, half = got.shape
    at = jnp.arange(total)
    place = jnp.broadcast_to((at % (total // n_seq)).astype(F32), (8, total))
    spread = (jnp.arange(n_seq)[:, None] == at[None, :] // (total // n_seq)).astype(BF)
    shape = (n_rows // 2, half)
    wide = 640 if half % 640 == 0 else half
    part = lambda rows: pl.BlockSpec((rows, wide), lambda j: (0, j))
    return pl.pallas_call(
        lambda *refs: column_kernel(n_exp, *refs),
        grid=(half // wide,),
        in_specs=[whole(place.shape), whole(spread.shape), whole(slot.shape), whole(weight.shape), part(total)],
        out_specs=[part(shape[0])] + [part(shape[0] // 2)] * 2,
        out_shape=[jax.ShapeDtypeStruct(shape, BF)] + [jax.ShapeDtypeStruct((shape[0] // 2, half), BF)] * 2,
        scratch_shapes=[pltpu.VMEM((n_rows, total), BF)],
        compiler_params=params(VMEM_MIB),
        cost_estimate=cost(400 * n_rows * total * half, 2 * total * half + 3 * n_rows * half),
        name="column_sums",
    )(place, spread, slot, weight, got)


def per_device(hidden_in, grad_out, expert_ids, gate_weights, w_gate, w_up, w_down):
    n_tok, features = hidden_in.shape
    top = expert_ids.shape[1]
    n_seq, n_exp = lax.axis_size("seq"), lax.axis_size("exp")
    group, member = lax.axis_index("seq"), lax.axis_index("exp")
    experts = n_seq * n_exp
    cap = 3 * top * n_tok // (2 * experts)
    per_group = top // 2 * n_tok // n_seq
    first = first_columns(features)
    rest = features - first
    gate_mat, up_mat, down_mat = w_gate[0], w_up[0], w_down[0]
    partner = member ^ jnp.arange(n_exp)
    to_b, to_a = window_tables(n_seq, n_exp, cap)

    meta = jnp.concatenate(
        (expert_ids.astype(BF), gate_weights.astype(BF), jnp.zeros((n_tok, LANES - 2 * top), BF)), axis=1)

    column_meta = lax.all_gather(meta, "exp", axis=0, tiled=True)
    column = lax.all_gather(grad_out, "exp", axis=0, tiled=True)
    theirs = jnp.broadcast_to((jnp.arange(n_seq) * n_exp + member).astype(F32)[:, None], (n_seq, LANES))
    put_b, slot_b, weight_b = column_slots(column_meta, theirs, member, n_tok, top, cap)
    slot_b, weight_b = slot_b.astype(BF), weight_b.astype(BF)
    local = jnp.broadcast_to((partner + group * n_exp).astype(F32)[:, None], (n_exp, LANES))
    tables = (jnp.eye(LANES, dtype=BF), local) + lower_counts(n_seq * per_group, per_group)
    put_b, to_b, to_a, slot_b, weight_b, *tables = barrier(put_b, to_b, to_a, slot_b, weight_b, *tables)
    send_b = column_rows(member, to_b, put_b, column, n_exp)

    group_ids = expert_ids // n_exp
    in_group = jnp.any(group_ids[:, :, None] == jnp.arange(n_seq)[None, None, :], axis=1)
    group_rank = earlier_counts(in_group).T
    pick = (group_rank[:, None, :] == jnp.arange(per_group, dtype=F32)[None, :, None])
    pick = pick.astype(BF).reshape(n_seq * per_group, n_tok)
    send = dot(pick, jnp.concatenate((hidden_in, meta), axis=1)).astype(BF)
    hub = lax.all_to_all(send.reshape(n_seq, per_group, features + LANES), "seq", 0, 0, tiled=True)
    hub = hub.reshape(n_seq * per_group, features + LANES)
    hub, send_b = barrier(hub, send_b)

    rows_b = n_exp * cap
    recv_b = lax.all_to_all(send_b.reshape(n_seq, rows_b, features), "seq", 0, 0, tiled=True)
    recv_b = recv_b.reshape(n_seq * rows_b, features)

    blocks, slot_a, weight_a = hub_blocks(hub, tables, per_group, top, cap)
    rows_in = exchange(blocks)

    pre_gate, pre_up = pre_products(to_b, rows_in, gate_mat, up_mat)
    lane = jnp.broadcast_to((jnp.arange(LANES) == group * n_exp + member).astype(F32), (8, LANES))
    grad_gate, grad_up, gate_dot, back_b = hidden_grads(lane, recv_b, down_mat, pre_gate, pre_up, gate_mat, up_mat)

    back_a = returned_a(to_a, grad_gate, grad_up, gate_mat, up_mat, gate_dot, n_exp)
    got_a = exchange(back_a)
    got_b = lax.all_to_all(back_b.reshape(n_seq, rows_b, rest), "seq", 0, 0, tiled=True)
    back = group_sums(slot_a, weight_a, got_a)
    got_b, back = barrier(got_b, back)
    mine, *other = column_sums(slot_b, weight_b, got_b.reshape(n_seq * rows_b, rest), n_exp)
    back, *other = barrier(back, *other)
    other = jnp.split(jnp.concatenate([swap(x, 1) for x in other], axis=0), n_exp // 2)
    chip = [(x.astype(F32) + y.astype(F32)).astype(BF) for x, y in zip(jnp.split(mine, n_exp // 2), other)]
    final_b = sum(p.astype(F32) for p in exchange(chip, 2))
    back = lax.all_to_all(back.reshape(n_seq, per_group, first + LANES), "seq", 0, 0, tiled=True)
    final_a = dot_t(pick, back.reshape(n_seq * per_group, first + LANES))

    grad_in = jnp.concatenate((final_a[:, :first], final_b), axis=1).astype(BF)
    table = final_a[:, first:]
    chosen = expert_ids[:, :, None] == jnp.arange(experts)[None, None, :]
    grad_gates = jnp.sum(jnp.where(chosen, table[:, None, :experts], 0.0), axis=2).astype(BF)
    return grad_in, grad_gates


def solution(mesh):
    rows, mats = P(("seq", "exp"), None), P(("seq", "exp"), None, None)
    return jax.shard_map(
        per_device, mesh=mesh, in_specs=(rows,) * 4 + (mats,) * 3, out_specs=(rows, rows), check_vma=False
    )
```

```python
import jax
import jax.numpy as jnp
from jax import lax
from jax.experimental import pallas as pl
from jax.experimental.pallas import tpu as pltpu
from jax.sharding import PartitionSpec as P

BF = jnp.bfloat16
F32 = jnp.float32
LANES = 128
VMEM_MIB = 60


def dot(a, b):
    return jnp.dot(a, b, preferred_element_type=F32)


def dot_t(a, b):
    return lax.dot_general(a, b, (((0,), (0,)), ((), ())), preferred_element_type=F32)


def dot_nt(a, b):
    return lax.dot_general(a, b, (((1,), (1,)), ((), ())), preferred_element_type=F32)


def earlier_counts(names):
    n = names.shape[-2]
    lower = (jnp.arange(n)[:, None] > jnp.arange(n)[None, :]).astype(BF)
    counts = jnp.einsum("ij,...jm->...im", lower, names.astype(BF), preferred_element_type=F32)
    return jnp.where(names, counts, -1.0)


def first_columns(features):
    return max(2 * features // 5 // 256 * 256, 256)


def barrier(*values):
    return lax.optimization_barrier(values)


def swap(x, k):
    return lax.ppermute(x, "exp", [(i, i ^ k) for i in range(lax.axis_size("exp"))])


def exchange(blocks, step=1):
    return [blocks[0]] + [swap(block, step * k) for k, block in enumerate(blocks) if k]


def whole(shape, at=(0, 0)):
    return pl.BlockSpec(shape, lambda *_: at, pipeline_mode=pl.Buffered(1))


def params(mib):
    return pltpu.CompilerParams(vmem_limit_bytes=mib * 2**20)


def cost(flops, nbytes):
    return pl.CostEstimate(flops=flops, bytes_accessed=nbytes, transcendentals=0)


def window_tables(n_seq, n_exp, cap):
    pair = 2 * n_exp * cap
    d = jnp.arange(pair)
    source = d % (n_exp * cap) // cap * 32 + d // (n_exp * cap) * cap + d % cap
    i = jnp.arange(n_seq // 2)
    at = source[None, :] + (2 * cap - 16) * i[:, None]
    wide = jnp.arange(32 * n_exp)
    to_b = (at[:, :, None] == wide[None, None, :]).astype(BF)
    to_a = (at[:, None, :] == wide[None, :, None]).astype(BF)
    return to_b, to_a


def pre_kernel(n_exp, pairs, table, *refs):
    blocks, (gate, up, out_gate, out_up, rows) = refs[:n_exp], refs[n_exp:]
    size = table.shape[1]

    @pl.when(pl.program_id(0) == 0)
    def _():
        for i in range(pairs):
            window = jnp.concatenate([b[16 * i:16 * i + 32, :] for b in blocks], axis=0)
            rows[size * i:size * (i + 1), :] = dot(table[i], window).astype(BF)

    out_gate[...] = dot(rows[...], gate[...])
    out_up[...] = dot(rows[...], up[...])


def pre_products(table, blocks, gate_mat, up_mat):
    chips, pairs = len(blocks), table.shape[0]
    rows, features = blocks[0].shape
    total, units = rows * chips, gate_mat.shape[1]
    wide = 256 if units % 256 == 0 else units
    column = pl.BlockSpec((features, wide), lambda j: (0, j))
    result = pl.BlockSpec((total, wide), lambda j: (0, j))
    return pl.pallas_call(
        lambda *refs: pre_kernel(chips, pairs, *refs),
        grid=(units // wide,),
        in_specs=[whole(table.shape, (0, 0, 0))] + [whole((rows, features))] * chips + [column, column],
        out_specs=[result, result],
        out_shape=[jax.ShapeDtypeStruct((total, units), F32)] * 2,
        scratch_shapes=[pltpu.VMEM((total, features), BF)],
        compiler_params=params(VMEM_MIB),
        cost_estimate=cost(4 * total * features * units, 2 * total * features + 4 * features * units + 8 * total * units),
        name="pre_products",
    )(table, *blocks, gate_mat, up_mat)


def grad_kernel(steps, lane, grad, down, pre_gate, pre_up, gate_mat, up_mat, out_gate, out_up, out_dot, out, all_gate, all_up):
    i = pl.program_id(0)
    tall = grad.shape[0]

    @pl.when(i < steps)
    def _():
        grad_hidden = dot_nt(grad[...], down[...])
        gate, up = pre_gate[...], pre_up[...]
        sigmoid = jax.nn.sigmoid(gate)
        active = gate * sigmoid
        hidden = (active * up).astype(BF).astype(F32)
        gate_dot = jnp.sum(hidden * grad_hidden, axis=1, keepdims=True)
        out_dot[...] = (gate_dot * lane[0:1, :]).astype(BF)
        rows = pl.ds(pl.multiple_of(i * tall, tall), tall)
        grad_gate = (grad_hidden * up * sigmoid * (1.0 + gate * (1.0 - sigmoid))).astype(BF)
        grad_up = (grad_hidden * active).astype(BF)
        out_gate[...] = grad_gate
        out_up[...] = grad_up
        all_gate[rows, :] = grad_gate
        all_up[rows, :] = grad_up

    @pl.when(i >= steps)
    def _():
        out[...] = (dot_nt(all_gate[...], gate_mat[...]) + dot_nt(all_up[...], up_mat[...])).astype(BF)


def hidden_grads(lane, rows_grad, down_mat, pre_gate, pre_up, gate_mat, up_mat):
    total, features = rows_grad.shape
    units, first, steps = down_mat.shape[0], first_columns(features), 4
    half = features - first
    tall = total // steps
    wide = 512 if half % 512 == 0 else half
    row = lambda width: pl.BlockSpec((tall, width), lambda i: (jnp.minimum(i, steps - 1), 0))
    mat = pl.BlockSpec((wide, units), lambda i: (first // wide + jnp.maximum(i - steps, 0), 0))
    return pl.pallas_call(
        lambda *refs: grad_kernel(steps, *refs),
        grid=(steps + half // wide,),
        in_specs=[whole(lane.shape), row(features), whole(down_mat.shape), row(units), row(units), mat, mat],
        out_specs=[row(units), row(units), row(LANES),
                   pl.BlockSpec((total, wide), lambda i: (0, jnp.maximum(i - steps, 0)))],
        out_shape=[jax.ShapeDtypeStruct((total, units), BF)] * 2
        + [jax.ShapeDtypeStruct((total, LANES), BF), jax.ShapeDtypeStruct((total, half), BF)],
        scratch_shapes=[pltpu.VMEM((total, units), BF)] * 2,
        compiler_params=params(VMEM_MIB),
        cost_estimate=cost(4 * total * features * units, 4 * total * features + 4 * features * units + 12 * total * units),
        name="hidden_grads",
    )(lane, rows_grad, down_mat, pre_gate, pre_up, gate_mat, up_mat)


def back_a_kernel(n_exp, pairs, table, grad_gate, grad_up, gate, up, gate_dot, *outs):
    wide = gate.shape[0]
    half = outs[0].shape[1] - LANES
    size = table.shape[2]

    def reorder(values, start, width):
        before = None
        for i in range(pairs):
            moved = dot(table[i], values[size * i:size * (i + 1), :])
            for k in range(n_exp):
                part = moved[32 * k:32 * k + 16, :]
                if before is not None:
                    part = part + before[32 * k + 16:32 * k + 32, :]
                outs[k][16 * i:16 * i + 16, pl.ds(start, width)] = part.astype(BF)
            before = moved
        for k in range(n_exp):
            part = before[32 * k + 16:32 * k + 32, :]
            outs[k][16 * pairs:16 * pairs + 16, pl.ds(start, width)] = part.astype(BF)

    j = pl.program_id(0)
    values = dot_nt(grad_gate[...], gate[...]) + dot_nt(grad_up[...], up[...])
    reorder(values.astype(BF), pl.multiple_of(j * wide, wide), wide)

    @pl.when(j == 0)
    def _():
        reorder(gate_dot[...], half, LANES)


def returned_a(table, grad_gate, grad_up, gate_mat, up_mat, gate_dot, n_exp):
    total, units = grad_gate.shape
    half = first_columns(gate_mat.shape[0])
    pairs = table.shape[0]
    wide = 512 if half % 512 == 0 else half
    mat = pl.BlockSpec((wide, units), lambda j: (j, 0))
    block = (total // n_exp, half + LANES)
    return pl.pallas_call(
        lambda *refs: back_a_kernel(n_exp, pairs, *refs),
        grid=(half // wide,),
        in_specs=[whole(table.shape, (0, 0, 0)), whole(grad_gate.shape), whole(grad_up.shape), mat, mat, whole(gate_dot.shape)],
        out_specs=[whole(block)] * n_exp,
        out_shape=[jax.ShapeDtypeStruct(block, BF)] * n_exp,
        compiler_params=params(VMEM_MIB),
        cost_estimate=cost(4 * total * half * units, 4 * half * units + 4 * total * units + 2 * total * half),
        name="returned_a",
    )(table, grad_gate, grad_up, gate_mat, up_mat, gate_dot)


def sum_kernel(n_exp, slot, weight, *refs):
    blocks, out = refs[:n_exp], refs[n_exp]
    half = out.shape[1] - LANES
    place = lax.broadcasted_iota(jnp.int32, (slot.shape[0], blocks[0].shape[0]), 1).astype(F32)
    sums = jnp.zeros((slot.shape[0], half), F32)
    gates = jnp.zeros((slot.shape[0], LANES), F32)
    for k in range(n_exp):
        hot = slot[:, k:k + 1] == place
        sums += dot(jnp.where(hot, weight[:, k:k + 1], 0.0).astype(BF), blocks[k][:, :half])
        gates += dot(jnp.where(hot, 1.0, 0.0).astype(BF), blocks[k][:, half:])
    out[:, :half] = sums.astype(BF)
    out[:, half:] = gates.astype(BF)


def group_sums(slot, weight, blocks):
    n_exp = len(blocks)
    shape = (slot.shape[0], blocks[0].shape[1])
    return pl.pallas_call(
        lambda *refs: sum_kernel(n_exp, *refs),
        grid=(1,),
        in_specs=[whole(slot.shape), whole(weight.shape)] + [whole(blocks[0].shape)] * n_exp,
        out_specs=whole(shape),
        out_shape=jax.ShapeDtypeStruct(shape, BF),
        compiler_params=params(VMEM_MIB),
        cost_estimate=cost(2 * shape[0] * blocks[0].size * n_exp, 2 * n_exp * blocks[0].size),
        name="group_sums",
    )(slot, weight, *blocks)


def named_here(top, eye, meta, local):
    flat = dot_nt(eye[...], meta)
    named = weight = jnp.zeros((local.shape[0], flat.shape[1]), F32)
    for k in range(top):
        hit = flat[k:k + 1, :] == local[:, 0:1]
        named += jnp.where(hit, 1.0, 0.0)
        weight += jnp.where(hit, flat[top + k:top + k + 1, :], 0.0)
    return named, weight


def hub_kernel(top, cap, eye, local, before, block, meta, hub, *outs):
    *blocks, out_slot, out_weight, puts = outs
    rows, n_rows = blocks[0].shape[0], hub.shape[0]

    @pl.when(pl.program_id(0) == 0)
    def _():
        named, out_weight[...] = named_here(top, eye, meta[...], local)
        slot = jnp.where(named > 0.0, block[0:1, :] * cap + dot(named.astype(BF), before[...]), -1.0)
        out_slot[...] = slot
        place = lax.broadcasted_iota(jnp.int32, (rows, n_rows), 0).astype(F32)
        for k in range(len(blocks)):
            puts[rows * k:rows * (k + 1), :] = jnp.where(place == slot[k:k + 1, :], 1.0, 0.0).astype(BF)

    placed = dot(puts[...], hub[...]).astype(BF)
    for k, out in enumerate(blocks):
        out[...] = placed[rows * k:rows * (k + 1), :]


def lower_counts(total, size):
    at = jnp.arange(total)
    same = at[:, None] // size == at[None, :] // size
    return (same & (at[:, None] < at[None, :])).astype(BF), jnp.broadcast_to((at // size).astype(F32), (8, total))


def hub_blocks(hub, tables, per_group, top, cap):
    n_rows, width = hub.shape
    n_exp = tables[1].shape[0]
    features = width - LANES
    wide = 1280 if features % 1280 == 0 else features
    shape = (n_rows // per_group * cap, features)
    row = (n_exp, n_rows)
    part = lambda rows: pl.BlockSpec((rows, wide), lambda j: (0, j))
    *blocks, slot, weight = pl.pallas_call(
        lambda *refs: hub_kernel(top, cap, *refs),
        grid=(features // wide,),
        in_specs=[whole(x.shape) for x in tables]
        + [whole((n_rows, LANES), (0, features // LANES)), part(n_rows)],
        out_specs=[part(shape[0])] * n_exp + [whole(row)] * 2,
        out_shape=[jax.ShapeDtypeStruct(shape, BF)] * n_exp + [jax.ShapeDtypeStruct(row, F32)] * 2,
        scratch_shapes=[pltpu.VMEM((shape[0] * n_exp, n_rows), BF)],
        compiler_params=params(VMEM_MIB),
        cost_estimate=cost(2 * shape[0] * n_exp * n_rows * width, 2 * n_exp * shape[0] * shape[1]),
        name="hub_blocks",
    )(*tables, hub, hub)
    return blocks, slot.T, weight.T


def column_block(k, member, n_tok, column):
    return column[pl.ds(pl.multiple_of((member[0] ^ k) * n_tok, n_tok), n_tok), :]


def slots_kernel(top, n_exp, cap, member, eye, theirs, before, start, spread, place, meta, out_hot, out_slot, out_weight):
    n_tok = before.shape[0]
    parts = [column_block(k, member, n_tok, meta) for k in range(n_exp)]
    named, out_weight[...] = named_here(top, eye, jnp.concatenate(parts, axis=0), theirs)
    counts = [dot(named[:, at:at + n_tok].astype(BF), before[...]) for at in range(0, named.shape[1], n_tok)]
    rank = jnp.concatenate(counts, axis=1)
    out_slot[...] = jnp.where(named > 0.0, start[0:1, :] + rank, -1.0)
    rank = jnp.where(named > 0.0, rank, -1.0).astype(BF)
    size = spread.shape[0]
    for k in range(n_exp):
        hot = dot(spread[...], rank[:, n_tok * k:n_tok * (k + 1)]) == place[:, 0:1]
        out_hot[size * k:size * (k + 1), :] = jnp.where(hot, 1.0, 0.0).astype(BF)


def column_slots(meta, theirs, member, n_tok, top, cap):
    total = meta.shape[0]
    n_seq, n_exp = theirs.shape[0], total // n_tok
    before, block = lower_counts(n_tok, n_tok)
    start = jnp.broadcast_to((jnp.arange(total) // n_tok * cap).astype(F32), (8, total))
    at = jnp.arange(n_seq * cap)
    spread = (at[:, None] // cap == jnp.arange(n_seq)[None, :]).astype(BF)
    place = jnp.broadcast_to((at % cap).astype(F32)[:, None], (n_seq * cap, LANES))
    eye = jnp.eye(LANES, dtype=BF)
    shapes = (n_seq * n_exp * cap, n_tok), (n_seq, total), (n_seq, total)
    inputs = (eye, theirs, before, start, spread, place, meta)
    hot, slot, weight = pl.pallas_call(
        lambda *refs: slots_kernel(top, n_exp, cap, *refs),
        grid=(1,),
        in_specs=[pl.BlockSpec(memory_space=pltpu.SMEM)] + [whole(x.shape) for x in inputs],
        out_specs=[whole(shape) for shape in shapes],
        out_shape=[jax.ShapeDtypeStruct(shape, kind) for shape, kind in zip(shapes, (BF, F32, F32))],
        compiler_params=params(VMEM_MIB),
        cost_estimate=cost(4 * total * LANES * LANES, 2 * shapes[0][0] * n_tok),
        name="column_slots",
    )(member.reshape(1), *inputs)
    return hot, slot.T, weight.T


def rows_kernel(n_exp, member, table, hot, column, out):
    pairs, size = table.shape[:2]
    n_tok = hot.shape[1]
    blocks = []
    for k in range(n_exp):
        blocks.append(dot(hot[size * k:size * (k + 1), :], column_block(k, member, n_tok, column)).astype(BF))
    for i in range(pairs):
        window = jnp.concatenate([b[16 * i:16 * i + 32, :] for b in blocks], axis=0)
        out[size * i:size * (i + 1), :] = dot(table[i], window).astype(BF)


def column_rows(member, table, hot, column, n_exp):
    total, features = hot.shape[0], column.shape[1]
    wide = 1280 if features % 1280 == 0 else features
    part = lambda rows: pl.BlockSpec((rows, wide), lambda j: (0, j))
    return pl.pallas_call(
        lambda *refs: rows_kernel(n_exp, *refs),
        grid=(features // wide,),
        in_specs=[pl.BlockSpec(memory_space=pltpu.SMEM), whole(table.shape, (0, 0, 0)), whole(hot.shape),
                  part(column.shape[0])],
        out_specs=part(total),
        out_shape=jax.ShapeDtypeStruct((total, features), BF),
        compiler_params=params(VMEM_MIB),
        cost_estimate=cost(2 * total * hot.shape[1] * LANES, 2 * total * LANES),
        name="column_rows",
    )(member.reshape(1), table, hot, column)


def column_kernel(n_exp, place, spread, slot, weight, got, out_mine, out_first, out_last, mixed):
    n_tok = out_mine.shape[0] // (n_exp // 2)

    @pl.when(pl.program_id(0) == 0)
    def _():
        hot = dot(slot[...], spread[...]) == place[0:1, :]
        mixed[...] = jnp.where(hot, dot(weight[...], spread[...]), 0.0).astype(BF)

    sums = dot(mixed[...], got[...])
    for k in range(0, n_exp, 2):
        at = slice(n_tok * k // 2, n_tok * (k // 2 + 1))
        out_mine[at, :] = sums[n_tok * k:n_tok * (k + 1), :].astype(BF)
        out, at = (out_first, k) if 2 * k < n_exp else (out_last, k - n_exp // 2)
        out[n_tok * at // 2:n_tok * (at // 2 + 1), :] = sums[n_tok * (k + 1):n_tok * (k + 2), :].astype(BF)


def column_sums(slot, weight, got, n_exp):
    n_rows, n_seq = slot.shape
    total, half = got.shape
    at = jnp.arange(total)
    place = jnp.broadcast_to((at % (total // n_seq)).astype(F32), (8, total))
    spread = (jnp.arange(n_seq)[:, None] == at[None, :] // (total // n_seq)).astype(BF)
    shape = (n_rows // 2, half)
    wide = 512 if half % 512 == 0 else half
    part = lambda rows: pl.BlockSpec((rows, wide), lambda j: (0, j))
    return pl.pallas_call(
        lambda *refs: column_kernel(n_exp, *refs),
        grid=(half // wide,),
        in_specs=[whole(place.shape), whole(spread.shape), whole(slot.shape), whole(weight.shape), part(total)],
        out_specs=[part(shape[0])] + [part(shape[0] // 2)] * 2,
        out_shape=[jax.ShapeDtypeStruct(shape, BF)] + [jax.ShapeDtypeStruct((shape[0] // 2, half), BF)] * 2,
        scratch_shapes=[pltpu.VMEM((n_rows, total), BF)],
        compiler_params=params(VMEM_MIB),
        cost_estimate=cost(400 * n_rows * total * half, 2 * total * half + 3 * n_rows * half),
        name="column_sums",
    )(place, spread, slot, weight, got)


def per_device(hidden_in, grad_out, expert_ids, gate_weights, w_gate, w_up, w_down):
    n_tok, features = hidden_in.shape
    top = expert_ids.shape[1]
    n_seq, n_exp = lax.axis_size("seq"), lax.axis_size("exp")
    group, member = lax.axis_index("seq"), lax.axis_index("exp")
    experts = n_seq * n_exp
    cap = 3 * top * n_tok // (2 * experts)
    per_group = top // 2 * n_tok // n_seq
    first = first_columns(features)
    rest = features - first
    gate_mat, up_mat, down_mat = w_gate[0], w_up[0], w_down[0]
    partner = member ^ jnp.arange(n_exp)
    to_b, to_a = window_tables(n_seq, n_exp, cap)

    meta = jnp.concatenate(
        (expert_ids.astype(BF), gate_weights.astype(BF), jnp.zeros((n_tok, LANES - 2 * top), BF)), axis=1)

    column_meta = lax.all_gather(meta, "exp", axis=0, tiled=True)
    column = lax.all_gather(grad_out, "exp", axis=0, tiled=True)
    theirs = jnp.broadcast_to((jnp.arange(n_seq) * n_exp + member).astype(F32)[:, None], (n_seq, LANES))
    put_b, slot_b, weight_b = column_slots(column_meta, theirs, member, n_tok, top, cap)
    slot_b, weight_b = slot_b.astype(BF), weight_b.astype(BF)
    local = jnp.broadcast_to((partner + group * n_exp).astype(F32)[:, None], (n_exp, LANES))
    tables = (jnp.eye(LANES, dtype=BF), local) + lower_counts(n_seq * per_group, per_group)
    put_b, to_b, to_a, slot_b, weight_b, *tables = barrier(put_b, to_b, to_a, slot_b, weight_b, *tables)
    send_b = column_rows(member, to_b, put_b, column, n_exp)

    group_ids = expert_ids // n_exp
    in_group = jnp.any(group_ids[:, :, None] == jnp.arange(n_seq)[None, None, :], axis=1)
    group_rank = earlier_counts(in_group).T
    pick = (group_rank[:, None, :] == jnp.arange(per_group, dtype=F32)[None, :, None])
    pick = pick.astype(BF).reshape(n_seq * per_group, n_tok)
    send = dot(pick, jnp.concatenate((hidden_in, meta), axis=1)).astype(BF)
    hub = lax.all_to_all(send.reshape(n_seq, per_group, features + LANES), "seq", 0, 0, tiled=True)
    hub = hub.reshape(n_seq * per_group, features + LANES)
    hub, send_b = barrier(hub, send_b)

    rows_b = n_exp * cap
    recv_b = lax.all_to_all(send_b.reshape(n_seq, rows_b, features), "seq", 0, 0, tiled=True)
    recv_b = recv_b.reshape(n_seq * rows_b, features)

    blocks, slot_a, weight_a = hub_blocks(hub, tables, per_group, top, cap)
    rows_in = exchange(blocks)

    pre_gate, pre_up = pre_products(to_b, rows_in, gate_mat, up_mat)
    lane = jnp.broadcast_to((jnp.arange(LANES) == group * n_exp + member).astype(F32), (8, LANES))
    grad_gate, grad_up, gate_dot, back_b = hidden_grads(lane, recv_b, down_mat, pre_gate, pre_up, gate_mat, up_mat)

    back_a = returned_a(to_a, grad_gate, grad_up, gate_mat, up_mat, gate_dot, n_exp)
    got_a = exchange(back_a)
    got_b = lax.all_to_all(back_b.reshape(n_seq, rows_b, rest), "seq", 0, 0, tiled=True)
    back = group_sums(slot_a, weight_a, got_a)
    got_b, back = barrier(got_b, back)
    mine, *other = column_sums(slot_b, weight_b, got_b.reshape(n_seq * rows_b, rest), n_exp)
    back, *other = barrier(back, *other)
    other = jnp.split(jnp.concatenate([swap(x, 1) for x in other], axis=0), n_exp // 2)
    chip = [(x.astype(F32) + y.astype(F32)).astype(BF) for x, y in zip(jnp.split(mine, n_exp // 2), other)]
    final_b = sum(p.astype(F32) for p in exchange(chip, 2))
    back = lax.all_to_all(back.reshape(n_seq, per_group, first + LANES), "seq", 0, 0, tiled=True)
    final_a = dot_t(pick, back.reshape(n_seq * per_group, first + LANES))

    grad_in = jnp.concatenate((final_a[:, :first], final_b), axis=1).astype(BF)
    table = final_a[:, first:]
    chosen = expert_ids[:, :, None] == jnp.arange(experts)[None, None, :]
    grad_gates = jnp.sum(jnp.where(chosen, table[:, None, :experts], 0.0), axis=2).astype(BF)
    return grad_in, grad_gates


def solution(mesh):
    rows, mats = P(("seq", "exp"), None), P(("seq", "exp"), None, None)
    return jax.shard_map(
        per_device, mesh=mesh, in_specs=(rows,) * 4 + (mats,) * 3, out_specs=(rows, rows), check_vma=False
    )
```
